128 devices in a mesh: morton: 32 (over x_hi, z, y), oct: 4 (over x_lo, core).
Axes of the slice: x: 4 (x_hi: 2, x_lo: 2; x = x_hi * 2 + x_lo), y: 4, z: 4, core: 2. Of those that a mesh axis runs over, the one named last changes fastest.
Arguments:
- state: float32 [5, 512, 128, 128], P(None, 'morton', 'oct'), may hold values from -25 to 200
- fine_pairs: int32 [64, 16, 16, 32], P('morton', 'oct'), may hold values from 0 to 124, as said below
- fine_count: int32 [64, 16, 16], P('morton', 'oct'), may hold values from 1 to 32, as said below
- coarse_pairs: int32 [32, 8, 8, 32], P('morton', 'oct'), may hold values from 0 to 2047, as said below
Outputs:
- new_state: float32 [5, 512, 128, 128], P(None, 'morton', 'oct')
- gravity: float32 [3, 512, 128, 128], P(None, 'morton', 'oct')
The draws below stay inside these ranges and needn't reach their ends.
Inputs may be any that keep to these rules, and one draw needn't show every extreme that they name: `fine_pairs`: each entry codes an offset (ox, oy, oz), each of -2 to 2, as (ox + 2) * 25 + (oy + 2) * 5 + oz + 2, and the largest of |ox|, |oy|, |oz| is 2. Entries of a row of fine_pairs at or past fine_count are not used. `coarse_pairs`: each entry is a parent's index (px * 8 + py) * 8 + pz; its pz differs from that of the row's own parent by 2 or more.
All inputs are finite; a program needn't handle non-finite values.
Results may differ from the reference program's by a relative error of at most 0.0001.
Values sent between devices are 32-bit elements; how exact they have to be, the bound alone decides.
No kernel may reach another device: no remote copies, remote signals or barrier semaphores. Data moves between devices by JAX's collectives and lax.ppermute only.
A program may use at most 64 MiB of HBM per device.

```python
import math
import jax
import jax.numpy as jnp
from jax import lax

PAIRS = 32
FAR = 32
NX = 512
NY = 128
NZ = 128
SX = 64
SY = 16
SZ = 16
PX = 32
PY = 8
PZ = 8


def core_profile(first_centre, second_centre, first_width, second_width):
    along_x = ((jnp.arange(NX, dtype=jnp.float32) + 0.5) / NX).reshape(NX, 1, 1)
    along_y = ((jnp.arange(NY, dtype=jnp.float32) + 0.5) / NY).reshape(1, NY, 1)
    along_z = ((jnp.arange(NZ, dtype=jnp.float32) + 0.5) / NZ).reshape(1, 1, NZ)
    first_sq = (along_x - first_centre[0]) ** 2 + (along_y - first_centre[1]) ** 2 + (along_z - first_centre[2]) ** 2
    second_sq = (along_x - second_centre[0]) ** 2 + (along_y - second_centre[1]) ** 2 + (along_z - second_centre[2]) ** 2
    cores = jnp.exp(-first_sq / (first_width * first_width)) + jnp.exp(-second_sq / (second_width * second_width))
    return 0.4 + 2.4 * cores


def draw_state(key, part):
    key = jax.random.fold_in(key, 11)
    key_density, key_velocity, key_pressure = jax.random.split(key, 3)
    grid_shape = (NX, NY, NZ)
    position = (jnp.arange(NX, dtype=jnp.float32) / (NX - 1)).reshape(NX, 1, 1)
    profile = core_profile((0.3, 0.4, 0.45), (0.7, 0.6, 0.55), 0.12, 0.12)
    roughness = jnp.exp(jax.random.uniform(key_density, grid_shape, jnp.float32, math.log(0.75), math.log(1.2)))
    amplitude = 0.5 + position
    velocity = jnp.clip(jax.random.normal(key_velocity, (3,) + grid_shape, jnp.float32), -4.0, 4.0) * amplitude
    pressure = jnp.exp(jax.random.uniform(key_pressure, grid_shape, jnp.float32, math.log(0.5), math.log(2.0)))
    density = jnp.clip(profile * roughness, 0.3, 3.4)
    momenta = density * velocity
    energy = 0.5 * density * jnp.sum(velocity * velocity, axis=0) + 1.5 * pressure
    return jnp.concatenate([density[None], momenta, energy[None]]).astype(jnp.float32)


def draw_fine_pairs(key, part):
    key = jax.random.fold_in(key, 23)
    key_pick, key_sign, key_other = jax.random.split(key, 3)
    pair_shape = (SX, SY, SZ, PAIRS)
    picked_axis = jax.random.randint(key_pick, pair_shape, 0, 3)
    signed_two = jax.random.randint(key_sign, pair_shape, 0, 2) * 4 - 2
    others = jax.random.randint(key_other, (3,) + pair_shape, -2, 3)
    chooser = jnp.arange(3, dtype=jnp.int32).reshape(3, 1, 1, 1, 1)
    offsets = jnp.where(chooser == picked_axis[None], signed_two[None], others)
    codes = (offsets[0] + 2) * 25 + (offsets[1] + 2) * 5 + (offsets[2] + 2)
    codes = codes.at[0, 0, 0, 0].set(124).at[0, 0, 0, 1].set(0)
    return codes.astype(jnp.int32)


def draw_fine_count(key, part):
    key = jax.random.fold_in(key, 37)
    key_busy, key_light = jax.random.split(key, 2)
    count_shape = (SX, SY, SZ)
    column = jnp.arange(SX, dtype=jnp.int32).reshape(SX, 1, 1)
    central = jnp.abs(2 * column - SX + 1) < SX // 4
    busy = jax.random.randint(key_busy, count_shape, PAIRS // 2, PAIRS + 1)
    light = jax.random.randint(key_light, count_shape, 1, PAIRS // 4 + 1)
    counts = jnp.where(central, busy, light)
    counts = counts.at[0, 0, 0].set(PAIRS).at[0, 0, 1].set(1)
    return counts.astype(jnp.int32)


def draw_coarse_pairs(key, part):
    key = jax.random.fold_in(key, 53)
    key_first, key_second, key_third = jax.random.split(key, 3)
    pair_shape = (PX, PY, PZ, FAR)
    source_x = jax.random.randint(key_first, pair_shape, 0, PX)
    source_y = jax.random.randint(key_second, pair_shape, 0, PY)
    stride = jax.random.randint(key_third, pair_shape, 0, PZ - 3)
    own_z = jnp.arange(PZ, dtype=jnp.int32).reshape(1, 1, PZ, 1)
    source_z = (own_z + 2 + stride) % PZ
    indices = (source_x * PY + source_y) * PZ + source_z
    indices = indices.at[0, 0, 0, 0].set(PX * PY * PZ - 1).at[0, 0, 2, 0].set(0)
    return indices.astype(jnp.int32)


def setup_inputs(seed: int = 0) -> dict:
    keys = jax.random.split(jax.random.key(seed), 5)
    state = draw_state(jax.random.fold_in(keys[4], 71), 0)
    fine_pairs = draw_fine_pairs(jax.random.fold_in(keys[4], 71), 0)
    fine_count = draw_fine_count(jax.random.fold_in(keys[4], 71), 0)
    coarse_pairs = draw_coarse_pairs(jax.random.fold_in(keys[4], 71), 0)
    return dict(state=state, fine_pairs=fine_pairs, fine_count=fine_count, coarse_pairs=coarse_pairs)


ADIABATIC = 5.0 / 3.0
COURANT = 0.2
GRAVITY = 1.0

def window(values, offset, extent, dimension):
    return lax.slice_in_dim(values, offset, offset + extent, axis=dimension)

def pressure_of(fields):
    kinetic = 0.5 * (fields[1] * fields[1] + fields[2] * fields[2] + fields[3] * fields[3]) / fields[0]
    return (ADIABATIC - 1.0) * (fields[4] - kinetic)

def wave_speed(fields, direction):
    sound_speed = jnp.sqrt(ADIABATIC * pressure_of(fields) / fields[0])
    return jnp.abs(fields[1 + direction] / fields[0]) + sound_speed

def euler_flux(fields, direction):
    velocity = fields[1 + direction] / fields[0]
    pressure = pressure_of(fields)
    momenta = []
    for component in range(3):
        carried = fields[1 + component] * velocity
        if component == direction:
            carried = carried + pressure
        momenta.append(carried)
    return jnp.stack([fields[1 + direction]] + momenta + [(fields[4] + pressure) * velocity])

def flux_difference(padded, speeds, direction):
    dimension = direction + 1
    length = padded.shape[dimension] - 6
    left_far = window(padded, 0, length + 3, dimension)
    left_near = window(padded, 1, length + 3, dimension)
    right_near = window(padded, 2, length + 3, dimension)
    right_far = window(padded, 3, length + 3, dimension)
    face_value = 7.0 / 12.0 * (left_near + right_near) - 1.0 / 12.0 * (left_far + right_far)
    face_value = jnp.minimum(jnp.maximum(face_value, jnp.minimum(left_near, right_near)), jnp.maximum(left_near, right_near))
    centre = window(padded, 2, length + 2, dimension)
    upper_jump = window(face_value, 1, length + 2, dimension) - centre
    lower_jump = window(face_value, 0, length + 2, dimension) - centre
    upper_state = centre + jnp.minimum(jnp.maximum(upper_jump, -2.0 * jnp.abs(lower_jump)), 2.0 * jnp.abs(lower_jump))
    lower_state = centre + jnp.minimum(jnp.maximum(lower_jump, -2.0 * jnp.abs(upper_jump)), 2.0 * jnp.abs(upper_jump))
    from_left = window(upper_state, 0, length + 1, dimension)
    from_right = window(lower_state, 1, length + 1, dimension)
    face_speed = jnp.maximum(window(speeds, 2, length + 1, direction), window(speeds, 3, length + 1, direction))
    flux = 0.5 * (euler_flux(from_left, direction) + euler_flux(from_right, direction)) - 0.5 * face_speed * (from_right - from_left)
    return window(flux, 1, length, dimension) - window(flux, 0, length, dimension)

def cell_offsets(count_cells, factor):
    return (jnp.arange(count_cells, dtype=jnp.int32) % factor).astype(jnp.float32) - 0.5 * (factor - 1)

def subgrid_moments(density):
    count_x, count_y, count_z = density.shape
    weighted = jnp.stack([density, density * cell_offsets(count_x, 8)[:, None, None], density * cell_offsets(count_y, 8)[None, :, None], density * cell_offsets(count_z, 8)[None, None, :]])
    folded = weighted.reshape(4, count_x // 8, 8, count_y, count_z).sum(axis=2)
    folded = folded.reshape(4, count_x // 8, count_y // 8, 8, count_z).sum(axis=3)
    selector = (jnp.arange(count_z, dtype=jnp.int32)[:, None] // 8 == jnp.arange(count_z // 8, dtype=jnp.int32)[None, :]).astype(jnp.float32)
    return jnp.dot(folded, selector, precision=lax.Precision.HIGHEST)

def parent_moments(moments):
    groups_x = moments.shape[1] // 2
    groups_y = moments.shape[2] // 2
    groups_z = moments.shape[3] // 2
    grouped = moments.reshape(4, groups_x, 2, groups_y, 2, groups_z, 2)
    child_side = jnp.array([-4.0, 4.0], jnp.float32)
    source_mass = grouped[0]
    pieces = [source_mass, grouped[1] + source_mass * child_side.reshape(1, 2, 1, 1, 1, 1), grouped[2] + source_mass * child_side.reshape(1, 1, 1, 2, 1, 1), grouped[3] + source_mass * child_side.reshape(1, 1, 1, 1, 1, 2)]
    return jnp.stack([piece_sum.sum(axis=(1, 3, 5)) for piece_sum in pieces])

def far_field(sources, separation, weight):
    distance_sq = separation[0] * separation[0] + separation[1] * separation[1] + separation[2] * separation[2]
    inverse_cube = 1.0 / (distance_sq * jnp.sqrt(distance_sq))
    inverse_fifth = inverse_cube / distance_sq
    source_mass = sources[0] * weight
    acceleration = []
    tidal_terms = []
    for row_index in range(3):
        summed = source_mass * separation[row_index] * inverse_cube
        for col_index in range(3):
            jacobian = 3.0 * separation[row_index] * separation[col_index] * inverse_fifth
            if row_index == col_index:
                jacobian = jacobian - inverse_cube
            summed = summed - jacobian * (sources[1 + col_index] * weight)
            tidal_terms.append(lax.optimization_barrier(jnp.sum(source_mass * jacobian, axis=-1)))
        acceleration.append(lax.optimization_barrier(jnp.sum(summed, axis=-1)))
    return (GRAVITY * jnp.stack(acceleration), GRAVITY * jnp.stack(tidal_terms))

def spread(values, factor):
    return jnp.repeat(jnp.repeat(jnp.repeat(values, factor, axis=1), factor, axis=2), factor, axis=3)

def level_field(acceleration, tidal_terms, factor):
    full_accel = spread(acceleration, factor)
    full_tidal = spread(tidal_terms, factor)
    count_x, count_y, count_z = full_accel.shape[1:]
    offsets = [cell_offsets(count_x, factor)[:, None, None], cell_offsets(count_y, factor)[None, :, None], cell_offsets(count_z, factor)[None, None, :]]
    components = []
    for row_index in range(3):
        summed = full_accel[row_index]
        for col_index in range(3):
            summed = summed + full_tidal[3 * row_index + col_index] * offsets[col_index]
        components.append(summed)
    return jnp.stack(components)

def advance(fields, divergence, gravity, time_step):
    updated = fields - time_step * divergence
    momentum_gain = time_step * fields[0] * gravity
    energy_gain = time_step * (fields[1] * gravity[0] + fields[2] * gravity[1] + fields[3] * gravity[2])
    return jnp.concatenate([updated[0:1], updated[1:4] + momentum_gain, (updated[4] + energy_gain)[None]])

def reference(state, fine_pairs, fine_count, coarse_pairs):
    fastest = jnp.maximum(jnp.maximum(wave_speed(state, 0), wave_speed(state, 1)), wave_speed(state, 2))
    time_step = COURANT / jnp.max(fastest)
    moments = subgrid_moments(state[0])
    padded_moments = jnp.pad(moments, ((0, 0), (2, 2), (2, 2), (2, 2)))
    offset_x = fine_pairs // 25 - 2
    offset_y = fine_pairs // 5 % 5 - 2
    offset_z = fine_pairs % 5 - 2
    index_x = jnp.arange(SX, dtype=jnp.int32)[:, None, None, None] + 2 + offset_x
    index_y = jnp.arange(SY, dtype=jnp.int32)[None, :, None, None] + 2 + offset_y
    index_z = jnp.arange(SZ, dtype=jnp.int32)[None, None, :, None] + 2 + offset_z
    sources = padded_moments[:, index_x, index_y, index_z]
    in_use = (jnp.arange(PAIRS, dtype=jnp.int32)[None, None, None, :] < fine_count[:, :, :, None]).astype(jnp.float32)
    separation = 8.0 * jnp.stack([offset_x, offset_y, offset_z]).astype(jnp.float32)
    fine_accel, fine_tidal = far_field(sources, separation, in_use)
    parents = parent_moments(moments)
    far_sources = parents.reshape(4, PX * PY * PZ)[:, coarse_pairs]
    source_x = coarse_pairs // (PY * PZ)
    source_y = coarse_pairs // PZ % PY
    source_z = coarse_pairs % PZ
    far_separation = 16.0 * jnp.stack([source_x - jnp.arange(PX, dtype=jnp.int32)[:, None, None, None], source_y - jnp.arange(PY, dtype=jnp.int32)[None, :, None, None], source_z - jnp.arange(PZ, dtype=jnp.int32)[None, None, :, None]]).astype(jnp.float32)
    coarse_accel, coarse_tidal = far_field(far_sources, far_separation, 1.0)
    padded_x = jnp.pad(state, ((0, 0), (3, 3), (0, 0), (0, 0)), mode='edge')

    def update_slab(slab_index):
        rows_x = lax.dynamic_slice_in_dim(padded_x, slab_index * 16, 22, axis=1)
        interior = window(rows_x, 3, 16, 1)
        rows_y = jnp.pad(interior, ((0, 0), (0, 0), (3, 3), (0, 0)), mode='edge')
        rows_z = jnp.pad(interior, ((0, 0), (0, 0), (0, 0), (3, 3)), mode='edge')
        divergence = flux_difference(rows_x, wave_speed(rows_x, 0), 0)
        divergence = divergence + flux_difference(rows_y, wave_speed(rows_y, 1), 1)
        divergence = divergence + flux_difference(rows_z, wave_speed(rows_z, 2), 2)
        gravity = level_field(lax.dynamic_slice_in_dim(fine_accel, slab_index * 2, 2, axis=1), lax.dynamic_slice_in_dim(fine_tidal, slab_index * 2, 2, axis=1), 8)
        gravity = gravity + level_field(lax.dynamic_slice_in_dim(coarse_accel, slab_index, 1, axis=1), lax.dynamic_slice_in_dim(coarse_tidal, slab_index, 1, axis=1), 16)
        return (advance(interior, divergence, gravity, time_step), gravity)
    new_slabs, gravity_slabs = lax.map(update_slab, jnp.arange(NX // 16, dtype=jnp.int32))
    new_state = jnp.moveaxis(new_slabs, 0, 1).reshape(5, NX, NY, NZ)
    gravity = jnp.moveaxis(gravity_slabs, 0, 1).reshape(3, NX, NY, NZ)
    return (new_state, gravity)
```

```python
import functools

import jax
import jax.numpy as jnp
from jax import lax
from jax.experimental import pallas as pl
from jax.experimental.pallas import tpu as pltpu
from jax.sharding import PartitionSpec as P

ADIABATIC = 5.0 / 3.0
COURANT = 0.2
GRAVITY = 1.0
AXES = ("morton", "oct")
F32 = jnp.float32
HIGH = lax.Precision.HIGHEST

NX, NY, NZ = 16, 32, 128
ROWS = NX * NY
SENT = 5
SYM = ((0, 0), (0, 1), (0, 2), (1, 1), (1, 2), (2, 2))


def iota(shape, dim):
    return lax.broadcasted_iota(jnp.int32, shape, dim)


def sym(i, j):
    return SYM.index((min(i, j), max(i, j)))


def reciprocal(x):
    guess = pl.reciprocal(x, approx=True)
    return guess * (2.0 - x * guess)


def sound_of(q, inverse):
    kinetic = (q[1] * q[1] + q[2] * q[2] + q[3] * q[3]) * inverse
    pressure = (2.0 / 3.0) * q[4] - (1.0 / 3.0) * kinetic
    return jnp.sqrt(ADIABATIC * pressure * inverse)


def fold_rows(values, group):
    keep = iota(values.shape, 1) // group == iota(values.shape, 0)
    return jnp.sum(jnp.where(keep, values, 0.0), axis=0, keepdims=True)


def prepare_kernel(place, state, sent, x_one, x_two, y_one, y_two):
    morton_odd = place[0] % 2
    oct_odd = place[1] % 2
    x_starts = (jnp.where(morton_odd == 0, NX - 3, 0), jnp.where(morton_odd == 0, 0, NX - 3))
    y_starts = (jnp.where(oct_odd == 0, NY - 3, 0), jnp.where(oct_odd == 0, 0, NY - 3))
    for field in range(5):
        for out, start in ((x_one, x_starts[0]), (x_two, x_starts[1])):
            out[field * 96 : field * 96 + 96, :] = state[
                pl.ds(pl.multiple_of(field * ROWS + start * NY, 32), 96), :
            ]
        for out, start in ((y_one, y_starts[0]), (y_two, y_starts[1])):
            for layer in range(3):
                row = (field * 3 + layer) * 16
                out[row : row + 16, :] = state[pl.ds(field * ROWS + start + layer, 16, stride=NY), :]

    offset_y = iota((8, 128), 0).astype(F32) - 3.5
    fastest = jnp.zeros((8, 128), F32)
    sums, sums_x, sums_y = [], [], []
    for tx in range(2):
        for ty in range(4):
            total = total_x = None
            for x in range(8):
                row = (tx * 8 + x) * NY + ty * 8
                q = [state[f * ROWS + row : f * ROWS + row + 8, :] for f in range(5)]
                inverse = reciprocal(q[0])
                largest = jnp.maximum(jnp.maximum(jnp.abs(q[1]), jnp.abs(q[2])), jnp.abs(q[3]))
                fastest = jnp.maximum(fastest, largest * inverse + sound_of(q, inverse))
                weighted = q[0] * (x - 3.5)
                total = q[0] if total is None else total + q[0]
                total_x = weighted if total_x is None else total_x + weighted
            sums.append(jnp.sum(total, axis=0, keepdims=True))
            sums_x.append(jnp.sum(total_x, axis=0, keepdims=True))
            sums_y.append(jnp.sum(total * offset_y, axis=0, keepdims=True))
    rows = jnp.concatenate(sums + sums_x + sums_y, axis=0)
    z = iota((128, 128), 0)
    pick = (z // 8 == iota((128, 128), 1) % 16).astype(F32)
    by_z = pick * ((z % 8).astype(F32) - 3.5)
    folded = jnp.dot(rows, pick, precision=HIGH, preferred_element_type=F32)
    folded_z = jnp.dot(rows[0:8], by_z, precision=HIGH, preferred_element_type=F32)
    mass = fold_rows(folded[0:8], 16)
    dipole = [fold_rows(folded[8:16], 16), fold_rows(folded[16:24], 16), fold_rows(folded_z, 16)]

    lane = iota((1, 128), 1)
    odd = [lane // 64, lane // 16 % 2, lane % 2]
    shifted = [d + 4.0 * (2 * o - 1).astype(F32) * mass for d, o in zip(dipole, odd, strict=True)]
    t = iota((128, 128), 0)
    parent = t // 32 % 2 * 8 + t % 16 // 2
    pick = (parent == iota((128, 128), 1) % 16).astype(F32)
    families = jnp.concatenate([mass] + shifted + [jnp.zeros((4, 128), F32)], axis=0)
    families = jnp.dot(families, pick, precision=HIGH, preferred_element_type=F32)
    last = jnp.where(lane < 64, fold_rows(families, 16), jnp.max(fastest))
    five = jnp.concatenate([mass] + dipole + [last], axis=0)
    many = jnp.concatenate([five] * 8, axis=0)
    for copy in range(16):
        sent[copy * 40 : copy * 40 + 40, :] = many


def faces(far_left, left, right, far_right):
    value = (7.0 / 12.0) * (left + right) - (1.0 / 12.0) * (far_left + far_right)
    return jnp.minimum(jnp.maximum(value, jnp.minimum(left, right)), jnp.maximum(left, right))


def upper_and_lower(centre, above, below):
    up, down = above - centre, below - centre
    most_up, most_down = 2.0 * jnp.abs(down), 2.0 * jnp.abs(up)
    upper = centre + jnp.minimum(jnp.maximum(up, -most_up), most_up)
    lower = centre + jnp.minimum(jnp.maximum(down, -most_down), most_down)
    return upper, lower


def flux_of(q, k):
    inverse = reciprocal(q[0])
    velocity = q[1 + k] * inverse
    kinetic = (q[1] * q[1] + q[2] * q[2] + q[3] * q[3]) * inverse
    pressure = (2.0 / 3.0) * q[4] - (1.0 / 3.0) * kinetic
    out = [q[1 + k]] + [q[1 + c] * velocity for c in range(3)] + [(q[4] + pressure) * velocity]
    out[1 + k] = out[1 + k] + pressure
    return out


def twice_flux(left, right, speed, k):
    from_left, from_right = flux_of(left, k), flux_of(right, k)
    return [
        (a + b) - speed * (r - l) for a, b, l, r in zip(from_left, from_right, left, right, strict=True)
    ]


def sweep(load, speed_at, store, length, k):
    window = [[load(f, i) for f in range(5)] for i in (-3, -2, -1)]
    above_old = upper_old = speed_old = flux_old = None
    for i in range(-2, length + 1):
        window.append([load(f, i + 2) for f in range(5)])
        far_left, left, right, far_right = window[-4:]
        above = [faces(*each) for each in zip(far_left, left, right, far_right, strict=True)]
        if above_old is not None:
            pairs = [upper_and_lower(*each) for each in zip(left, above, above_old, strict=True)]
            upper, lower = [p[0] for p in pairs], [p[1] for p in pairs]
            speed = speed_at(i, left)
            if upper_old is not None:
                flux = twice_flux(upper_old, lower, jnp.maximum(speed_old, speed), k)
                if flux_old is not None:
                    store(i - 1, [a - b for a, b in zip(flux, flux_old, strict=True)])
                flux_old = flux
            upper_old, speed_old = upper, speed
        above_old = above


def shift_up(values, lane):
    return jnp.where(lane == NZ - 1, values, pltpu.roll(values, NZ - 1, 1))


def shift_down(values, lane):
    return jnp.where(lane == 0, values, pltpu.roll(values, 1, 1))


def divergence_kernel(
    place, state, x_one, x_two, y_one, y_two, fine_pairs, fine_count, coarse_pairs,
    out, fine_uses, coarse_uses, inverse_of, sound, x_low, x_high, y_low, y_high,
):
    morton, octant = place[0], place[1]
    morton_last, oct_last = place[2] - 1, place[3] - 1
    lane = iota((8, 128), 1)

    for field in range(5):
        edges = [state[field * ROWS : field * ROWS + NY, :], state[field * ROWS + ROWS - NY : field * ROWS + ROWS, :]]
        for layer in range(3):
            row = (field * 3 + layer) * NY
            one, two = x_one[row : row + NY, :], x_two[row : row + NY, :]
            even = morton % 2 == 0
            x_low[row : row + NY, :] = jnp.where(morton == 0, edges[0], jnp.where(even, two, one))
            x_high[row : row + NY, :] = jnp.where(morton == morton_last, edges[1], jnp.where(even, one, two))
        edges = [state[pl.ds(field * ROWS + y, NX, stride=NY), :] for y in (0, NY - 1)]
        for layer in range(3):
            row = (field * 3 + layer) * NX
            one, two = y_one[row : row + NX, :], y_two[row : row + NX, :]
            even = octant % 2 == 0
            y_low[row : row + NX, :] = jnp.where(octant == 0, edges[0], jnp.where(even, two, one))
            y_high[row : row + NX, :] = jnp.where(octant == oct_last, edges[1], jnp.where(even, one, two))

    def along_z(step, _):
        row = pl.multiple_of(step * 8, 8)
        q = [state[pl.ds(pl.multiple_of(f * ROWS + row, 8), 8), :] for f in range(5)]
        inverse = reciprocal(q[0])
        speed_of_sound = sound_of(q, inverse)
        inverse_of[pl.ds(row, 8), :] = inverse
        sound[pl.ds(row, 8), :] = speed_of_sound
        speed = jnp.abs(q[3]) * inverse + speed_of_sound
        speed = jnp.maximum(speed, shift_up(speed, lane))
        upper, lower = [], []
        for values in q:
            right = shift_up(values, lane)
            above = faces(shift_down(values, lane), values, right, shift_up(right, lane))
            below = jnp.where(lane == 0, values, pltpu.roll(above, 1, 1))
            u, l = upper_and_lower(values, above, below)
            upper.append(u)
            lower.append(jnp.where(lane == NZ - 1, values, pltpu.roll(l, NZ - 1, 1)))
        flux = twice_flux(upper, lower, speed, 2)
        first = [2.0 * each for each in flux_of(q, 2)]
        for f in range(5):
            below = jnp.where(lane == 0, first[f], pltpu.roll(flux[f], 1, 1))
            out[pl.ds(pl.multiple_of(f * ROWS + row, 8), 8), :] = flux[f] - below
        return 0

    lax.fori_loop(0, ROWS // 8, along_z, 0, unroll=2)

    def along_x(step, _):
        column = pl.multiple_of(step * 8, 8)

        def rows(f, i):
            return pl.ds(pl.multiple_of(f * ROWS + i * NY + column, 8), 8)

        def load(f, i):
            if i < 0:
                return x_low[pl.ds(pl.multiple_of((f * 3 + i + 3) * NY + column, 8), 8), :]
            if i >= NX:
                return x_high[pl.ds(pl.multiple_of((f * 3 + i - NX) * NY + column, 8), 8), :]
            return state[rows(f, i), :]

        def speed_at(i, q):
            if 0 <= i < NX:
                inverse, own = inverse_of[rows(0, i), :], sound[rows(0, i), :]
            else:
                inverse = reciprocal(q[0])
                own = sound_of(q, inverse)
            return jnp.abs(q[1]) * inverse + own

        def store(i, values):
            for f in range(5):
                out[rows(f, i), :] = out[rows(f, i), :] + values[f]

        sweep(load, speed_at, store, NX, 0)
        return 0

    lax.fori_loop(0, NY // 8, along_x, 0)

    def along_y(step, _):
        start = pl.multiple_of(step * 8, 8)

        def rows(f, i):
            return pl.ds(f * ROWS + start * NY + i, 8, stride=NY)

        def load(f, i):
            if i < 0:
                return y_low[pl.ds(pl.multiple_of((f * 3 + i + 3) * NX + start, 8), 8), :]
            if i >= NY:
                return y_high[pl.ds(pl.multiple_of((f * 3 + i - NY) * NX + start, 8), 8), :]
            return state[rows(f, i), :]

        def speed_at(i, q):
            if 0 <= i < NY:
                inverse, own = inverse_of[rows(0, i), :], sound[rows(0, i), :]
            else:
                inverse = reciprocal(q[0])
                own = sound_of(q, inverse)
            return jnp.abs(q[2]) * inverse + own

        def store(i, values):
            for f in range(5):
                out[rows(f, i), :] = out[rows(f, i), :] + values[f]

        sweep(load, speed_at, store, NY, 1)
        return 0

    lax.fori_loop(0, NX // 8, along_y, 0)

    codes = jnp.concatenate([fine_pairs[...].astype(F32)] * 4, axis=1).T[0:32]
    spread = (iota((16, 128), 1) % 16 == iota((16, 128), 0)).astype(F32)
    used = fold_rows(
        jnp.dot(fine_count[...].astype(F32), spread, precision=HIGH, preferred_element_type=F32), 16
    )
    codes = jnp.where(iota((32, 128), 0).astype(F32) < used, codes, -1000.0)
    down = 25.0 * iota((8, 128), 0).astype(F32)
    codes = [jnp.broadcast_to(codes[j : j + 1], (8, 128)) - down for j in range(32)]
    for plane in range(25):
        count = jnp.zeros((8, 128), F32)
        for each in codes:
            count = count + jnp.where(each == plane, 1.0, 0.0)
        fine_uses[plane * 8 : plane * 8 + 8, :] = count

    for half in range(2):
        named = coarse_pairs[half * 8 : half * 8 + 8, :]
        named = [jnp.broadcast_to(named[:, j : j + 1], (8, 128)) - 16 * lane for j in range(32)]
        for lp in range(16):
            count = jnp.zeros((8, 128), F32)
            for each in named:
                count = count + jnp.where(each == lp, 1.0, 0.0)
            row = (lp * 2 + half) * 8
            coarse_uses[row : row + 8, :] = count


def tensors(r, square):
    square = jnp.maximum(square, 1.0)
    cube = 1.0 / (square * jnp.sqrt(square))
    three = 3.0 * cube / square
    scaled = [three * each for each in r]
    pull = [each * cube for each in r]
    tide = [scaled[i] * r[j] - cube if i == j else scaled[i] * r[j] for i, j in SYM]
    return pull, tide


def add_terms(totals, uses, r, square, mass, dipole):
    pull, tide = tensors(r, square)
    mass = uses * mass
    dipole = [uses * d for d in dipole]
    for i in range(3):
        term = mass * pull[i]
        for j in range(3):
            term = term - tide[sym(i, j)] * dipole[j]
        totals[i] = totals[i] + term
    for e in range(6):
        totals[3 + e] = totals[3 + e] + mass * tide[e]


def far_fields(place, uses_fine, uses_coarse, got, around):
    morton, octant = place[0], place[1]
    mortons, octs = place[2], place[3]
    lane = iota((8, 128), 1)
    lane_row = iota((1, 128), 1)

    rows = jnp.concatenate([got[pl.ds(g * 8 * SENT + 4, 8, stride=SENT), :] for g in range(16)], axis=0)
    time_step = COURANT / jnp.max(rows[:, 64:128])
    moments = rows.T
    target_z = iota((8, 128), 0)
    rx = 16.0 * (lane // 4 - morton).astype(F32)
    coarse = []
    for half in range(2):
        totals = [jnp.zeros((8, 128), F32) for _ in range(9)]
        for lp in range(16):
            ry = 16.0 * (lane % 4 * 2 + lp // 8 - (2 * octant + half)).astype(F32)
            rz = 16.0 * (lp % 8 - target_z).astype(F32)
            own = [jnp.broadcast_to(moments[m * 16 + lp : m * 16 + lp + 1], (8, 128)) for m in range(4)]
            row = (lp * 2 + half) * 8
            add_terms(totals, uses_coarse[row : row + 8, :], (rx, ry, rz), rx * rx + ry * ry + rz * rz, own[0], own[1:])
        coarse.append([jnp.sum(each, axis=1, keepdims=True) for each in totals])
    result = []
    for e in range(9):
        column = jnp.where(lane // 32 % 2 == 0, coarse[0][e], coarse[1][e])
        column = jnp.where(lane % 16 // 2 == iota((8, 128), 0), column, 0.0)
        result.append(jnp.sum(column, axis=0, keepdims=True))
    side = [4.0 * (2 * s - 1).astype(F32) for s in (lane_row // 64, lane_row // 16 % 2, lane_row % 2)]
    for i in range(3):
        for j in range(3):
            result[i] = result[i] + result[3 + sym(i, j)] * side[j]

    blocks = []
    for dy in (-1, 0, 1):
        block = []
        for dx in (-1, 0, 1):
            at_x, at_y = morton + dx, octant + dy
            inside = (at_x >= 0) & (at_x < mortons) & (at_y >= 0) & (at_y < octs)
            device = jnp.clip(at_x, 0, mortons - 1) * octs + jnp.clip(at_y, 0, octs - 1)
            for m in range(4):
                block.append(jnp.where(inside, got[pl.ds(device * SENT + m, 1), :], 0.0))
        blocks.append(jnp.concatenate(block + [jnp.zeros((4, 128), F32)], axis=0))
    wide = iota((16, 128), 1)
    around[...] = jnp.zeros(around.shape, F32)
    for oy in range(-2, 3):
        if oy == 0:
            moved = blocks[1]
        else:
            moved = pltpu.roll(blocks[1], (-16 * oy) % 128, 1)
            if oy > 0:
                moved = jnp.where(wide // 16 % 4 + oy > 3, pltpu.roll(blocks[2], (64 - 16 * oy) % 128, 1), moved)
            else:
                moved = jnp.where(wide // 16 % 4 + oy < 0, pltpu.roll(blocks[0], (-64 - 16 * oy) % 128, 1), moved)
        swapped = pltpu.roll(moved, 64, 1)
        for m in range(4):
            low, own, high = [(moved[d * 4 + m : d * 4 + m + 1], swapped[d * 4 + m : d * 4 + m + 1]) for d in range(3)]
            first = lane_row < 64
            lines = [
                low[0], jnp.where(first, low[1], own[1]), own[0], jnp.where(first, own[1], high[1]), high[0],
            ]
            row = (m * 5 + oy + 2) * 8
            around[row : row + 5, :] = jnp.concatenate(lines, axis=0)
    totals = [jnp.zeros((8, 128), F32) for _ in range(9)]
    rx = 8.0 * (iota((8, 128), 0) - 2).astype(F32)
    square_x = rx * rx
    for oy in range(-2, 3):
        base = [around[(m * 5 + oy + 2) * 8 : (m * 5 + oy + 2) * 8 + 8, :] for m in range(4)]
        for oz in range(-2, 3):
            moved = base
            if oz:
                ok = (lane % 16 + oz >= 0) & (lane % 16 + oz < 16)
                moved = [jnp.where(ok, pltpu.roll(each, (-oz) % 128, 1), 0.0) for each in base]
            plane = ((oy + 2) * 5 + oz + 2) * 8
            add_terms(
                totals, uses_fine[plane : plane + 8, :], (rx, 8.0 * oy, 8.0 * oz),
                square_x + (64.0 * oy * oy + 64.0 * oz * oz), moved[0], moved[1:],
            )
    for e in range(9):
        result[e] = GRAVITY * (result[e] + jnp.sum(totals[e], axis=0, keepdims=True))
    return result, time_step


def update_kernel(place, state, twice, uses_fine, uses_coarse, got, new, gravity, around, field, step_size):
    slab = pl.program_id(0)
    layers = state.shape[1] // NY

    @pl.when(slab == 0)
    def _():
        result, time_step = far_fields(place, uses_fine, uses_coarse, got, around)
        step_size[0] = time_step
        keep = iota((8, 128), 1) // 16 == iota((8, 128), 0)
        spread = (iota((128, 128), 0) % 16 == iota((128, 128), 1) // 8).astype(F32)
        rows = jnp.concatenate([jnp.where(keep, each, 0.0) for each in result], axis=0)
        rows = jnp.dot(rows, spread, precision=HIGH, preferred_element_type=F32)
        rows = [rows[e * 8 : e * 8 + 8] for e in range(9)]
        offset_z = (iota((8, 128), 1) % 8).astype(F32) - 3.5
        for i in range(3):
            field[i * 8 : i * 8 + 8, :] = rows[i] + rows[3 + sym(i, 2)] * offset_z
            field[(3 + i) * 8 : (3 + i) * 8 + 8, :] = rows[3 + sym(i, 0)]
            field[(6 + i) * 8 : (6 + i) * 8 + 8, :] = rows[3 + sym(i, 1)]

    time_step = step_size[0]
    half = 0.5 * time_step
    offset_y = iota((8, 128), 0).astype(F32) - 3.5
    for ty in range(4):
        tx = slab * layers // 8
        at = tx * 4 + ty
        base = [
            field[pl.ds(i * 8 + at, 1), :] + field[pl.ds((6 + i) * 8 + at, 1), :] * offset_y for i in range(3)
        ]
        slope = [field[pl.ds((3 + i) * 8 + at, 1), :] for i in range(3)]
        for layer in range(layers):
            offset_x = ((slab * layers + layer) % 8).astype(F32) - 3.5
            row = layer * NY + ty * 8
            q = [state[f, row : row + 8, :] for f in range(5)]
            pull = [base[i] + slope[i] * offset_x for i in range(3)]
            for i in range(3):
                gravity[i, row : row + 8, :] = pull[i]
            moved = [q[f] - half * twice[f, row : row + 8, :] for f in range(5)]
            new[0, row : row + 8, :] = moved[0]
            weight = time_step * q[0]
            for i in range(3):
                new[1 + i, row : row + 8, :] = moved[1 + i] + weight * pull[i]
            gain = q[1] * pull[0] + q[2] * pull[1] + q[3] * pull[2]
            new[4, row : row + 8, :] = moved[4] + time_step * gain


def whole(count):
    return [pl.BlockSpec(memory_space=pltpu.SMEM)] + [pl.BlockSpec(memory_space=pltpu.VMEM)] * count


LIMIT = pltpu.CompilerParams(vmem_limit_bytes=48 * 1024 * 1024)


def shaped(*shape):
    return jax.ShapeDtypeStruct(shape, F32)


def prepare(place, rows):
    return pl.pallas_call(
        prepare_kernel,
        out_shape=[shaped(128 * SENT, 128), shaped(480, 128), shaped(480, 128), shaped(240, 128), shaped(240, 128)],
        in_specs=whole(1),
        out_specs=[pl.BlockSpec(memory_space=pltpu.VMEM)] * 5,
        compiler_params=LIMIT,
    )(place, rows)


def diverge(place, rows, halos, fine_pairs, fine_count, coarse_pairs):
    return pl.pallas_call(
        divergence_kernel,
        out_shape=[shaped(5 * ROWS, 128), shaped(200, 128), shaped(256, 128)],
        in_specs=whole(8),
        out_specs=[pl.BlockSpec(memory_space=pltpu.VMEM)] * 3,
        scratch_shapes=[pltpu.VMEM((ROWS, 128), F32)] * 2
        + [pltpu.VMEM((480, 128), F32)] * 2
        + [pltpu.VMEM((240, 128), F32)] * 2,
        compiler_params=LIMIT,
    )(place, rows, *halos, fine_pairs, fine_count, coarse_pairs)


def update(place, rows, twice, uses_fine, uses_coarse, got):
    slabs = 4
    part = ROWS // slabs
    at_slab = lambda i: (0, i, 0)
    at_start = lambda i: (0, 0)
    return pl.pallas_call(
        update_kernel,
        grid=(slabs,),
        out_shape=[shaped(5, ROWS, 128), shaped(3, ROWS, 128)],
        in_specs=[
            pl.BlockSpec(memory_space=pltpu.SMEM),
            pl.BlockSpec((5, part, 128), at_slab),
            pl.BlockSpec((5, part, 128), at_slab),
            pl.BlockSpec((200, 128), at_start),
            pl.BlockSpec((256, 128), at_start),
            pl.BlockSpec((128 * SENT, 128), at_start),
        ],
        out_specs=[pl.BlockSpec((5, part, 128), at_slab), pl.BlockSpec((3, part, 128), at_slab)],
        scratch_shapes=[pltpu.VMEM((160, 128), F32), pltpu.VMEM((72, 128), F32), pltpu.SMEM((1,), F32)],
        compiler_params=LIMIT,
    )(place, rows.reshape(5, ROWS, 128), twice.reshape(5, ROWS, 128), uses_fine, uses_coarse, got)


def local(state, fine_pairs, fine_count, coarse_pairs):
    mortons, octs = lax.axis_size("morton"), lax.axis_size("oct")
    place = jnp.stack([lax.axis_index("morton"), lax.axis_index("oct"), mortons, octs]).astype(jnp.int32)
    rows = state.reshape(5 * ROWS, 128)
    sent, x_one, x_two, y_one, y_two = prepare(place, rows)

    def swap(values, axis, devices, first):
        pairs = [(i, i + 1) for i in range(first, devices - 1, 2)]
        return lax.ppermute(values, axis, pairs + [(j, i) for i, j in pairs])

    halos = [
        swap(x_one, "morton", mortons, 0),
        swap(x_two, "morton", mortons, 1),
        swap(y_one, "oct", octs, 0),
        swap(y_two, "oct", octs, 1),
    ]
    got = lax.all_to_all(sent.reshape(mortons * octs, 1, SENT * 128), AXES, 0, 0, tiled=True)
    twice, uses_fine, uses_coarse = diverge(
        place, rows, halos, fine_pairs.reshape(128, 32), fine_count.reshape(8, 16), coarse_pairs.reshape(16, 32)
    )
    new, gravity = update(place, rows, twice, uses_fine, uses_coarse, got.reshape(mortons * octs * SENT, 128))
    return new.reshape(state.shape), gravity.reshape(3, NX, NY, NZ)


def solution(mesh):
    in_specs = (
        P(None, "morton", "oct", None),
        P("morton", "oct", None, None),
        P("morton", "oct", None),
        P("morton", "oct", None, None),
    )
    out_specs = (P(None, "morton", "oct", None), P(None, "morton", "oct", None))
    return jax.shard_map(local, mesh=mesh, in_specs=in_specs, out_specs=out_specs, check_vma=False)
```

```python
import functools

import jax
import jax.numpy as jnp
from jax import lax
from jax.experimental import pallas as pl
from jax.experimental.pallas import tpu as pltpu
from jax.sharding import PartitionSpec as P

ADIABATIC = 5.0 / 3.0
COURANT = 0.2
GRAVITY = 1.0
AXES = ("morton", "oct")
F32 = jnp.float32
HIGH = lax.Precision.HIGHEST

NX, NY, NZ = 16, 32, 128
ROWS = NX * NY
PITCH = 33
TALL = 144
SENT = 5
SYM = ((0, 0), (0, 1), (0, 2), (1, 1), (1, 2), (2, 2))


def iota(shape, dim):
    return lax.broadcasted_iota(jnp.int32, shape, dim)


def sym(i, j):
    return SYM.index((min(i, j), max(i, j)))


def reciprocal(x):
    guess = pl.reciprocal(x, approx=True)
    return guess * (2.0 - x * guess)


def sound_of(q, inverse):
    kinetic = (q[1] * q[1] + q[2] * q[2] + q[3] * q[3]) * inverse
    pressure = (2.0 / 3.0) * q[4] - (1.0 / 3.0) * kinetic
    return jnp.sqrt(ADIABATIC * pressure * inverse)


def fold_rows(values, group):
    keep = iota(values.shape, 1) // group == iota(values.shape, 0)
    return jnp.sum(jnp.where(keep, values, 0.0), axis=0, keepdims=True)


def moments_kernel(state, sent, rows, arrived):
    part = ROWS // 4
    copies = [
        pltpu.make_async_copy(
            state.at[:, pl.ds(c * part, part), :], rows.at[:, pl.ds(c * part, part), :], arrived.at[c]
        )
        for c in range(4)
    ]
    for copy in copies:
        copy.start()
    offset_y = iota((8, 128), 0).astype(F32) - 3.5
    fastest = jnp.zeros((8, 128), F32)
    sums, sums_x, sums_y = [], [], []
    for tx in range(2):
        totals, totals_x = [jnp.zeros((8, 128), F32)] * 4, [jnp.zeros((8, 128), F32)] * 4
        for half in range(2):
            copies[tx * 2 + half].wait()
            for x in range(half * 4, half * 4 + 4):
                for ty in range(4):
                    row = (tx * 8 + x) * NY + ty * 8
                    q = [rows[f, row : row + 8, :] for f in range(5)]
                    inverse = reciprocal(q[0])
                    speed_of_sound = sound_of(q, inverse)
                    largest = jnp.maximum(jnp.maximum(jnp.abs(q[1]), jnp.abs(q[2])), jnp.abs(q[3]))
                    fastest = jnp.maximum(fastest, largest * inverse + speed_of_sound)
                    totals[ty] = totals[ty] + q[0]
                    totals_x[ty] = totals_x[ty] + q[0] * (x - 3.5)
        for ty in range(4):
            sums.append(jnp.sum(totals[ty], axis=0, keepdims=True))
            sums_x.append(jnp.sum(totals_x[ty], axis=0, keepdims=True))
            sums_y.append(jnp.sum(totals[ty] * offset_y, axis=0, keepdims=True))
    lines = jnp.concatenate(sums + sums_x + sums_y, axis=0)
    z = iota((128, 128), 0)
    pick = (z // 8 == iota((128, 128), 1) % 16).astype(F32)
    by_z = pick * ((z % 8).astype(F32) - 3.5)
    folded = jnp.dot(lines, pick, precision=HIGH, preferred_element_type=F32)
    folded_z = jnp.dot(lines[0:8], by_z, precision=HIGH, preferred_element_type=F32)
    mass = fold_rows(folded[0:8], 16)
    dipole = [fold_rows(folded[8:16], 16), fold_rows(folded[16:24], 16), fold_rows(folded_z, 16)]

    lane = iota((1, 128), 1)
    odd = [lane // 64, lane // 16 % 2, lane % 2]
    shifted = [d + 4.0 * (2 * o - 1).astype(F32) * mass for d, o in zip(dipole, odd, strict=True)]
    t = iota((128, 128), 0)
    parent = t // 32 % 2 * 8 + t % 16 // 2
    pick = (parent == iota((128, 128), 1) % 16).astype(F32)
    families = jnp.concatenate([mass] + shifted + [jnp.zeros((4, 128), F32)], axis=0)
    families = jnp.dot(families, pick, precision=HIGH, preferred_element_type=F32)
    last = jnp.where(lane < 64, fold_rows(families, 16), jnp.max(fastest))
    five = jnp.concatenate([mass] + dipole + [last], axis=0)
    many = jnp.concatenate([five] * 8, axis=0)
    for copy in range(16):
        sent[copy * 40 : copy * 40 + 40, :] = many


def faces(far_left, left, right, far_right):
    value = (7.0 / 12.0) * (left + right) - (1.0 / 12.0) * (far_left + far_right)
    return jnp.minimum(jnp.maximum(value, jnp.minimum(left, right)), jnp.maximum(left, right))


def upper_and_lower(centre, above, below):
    up, down = above - centre, below - centre
    most_up, most_down = 2.0 * jnp.abs(down), 2.0 * jnp.abs(up)
    upper = centre + jnp.minimum(jnp.maximum(up, -most_up), most_up)
    lower = centre + jnp.minimum(jnp.maximum(down, -most_down), most_down)
    return upper, lower


def flux_of(q, k):
    inverse = reciprocal(q[0])
    velocity = q[1 + k] * inverse
    kinetic = (q[1] * q[1] + q[2] * q[2] + q[3] * q[3]) * inverse
    pressure = (2.0 / 3.0) * q[4] - (1.0 / 3.0) * kinetic
    out = [q[1 + k]] + [q[1 + c] * velocity for c in range(3)] + [(q[4] + pressure) * velocity]
    out[1 + k] = out[1 + k] + pressure
    return out


def twice_flux(left, right, speed, k):
    from_left, from_right = flux_of(left, k), flux_of(right, k)
    return [
        (a + b) - speed * (r - l) for a, b, l, r in zip(from_left, from_right, left, right, strict=True)
    ]


def sweep(load, speed_at, store, length, k):
    window = [[load(f, i) for f in range(5)] for i in (-3, -2, -1)]
    above_old = upper_old = speed_old = flux_old = None
    for i in range(-2, length + 1):
        window.append([load(f, i + 2) for f in range(5)])
        far_left, left, right, far_right = window[-4:]
        above = [faces(*each) for each in zip(far_left, left, right, far_right, strict=True)]
        if above_old is not None:
            pairs = [upper_and_lower(*each) for each in zip(left, above, above_old, strict=True)]
            upper, lower = [p[0] for p in pairs], [p[1] for p in pairs]
            speed = speed_at(i, left)
            if upper_old is not None:
                flux = twice_flux(upper_old, lower, jnp.maximum(speed_old, speed), k)
                if flux_old is not None:
                    store(i - 1, [a - b for a, b in zip(flux, flux_old, strict=True)])
                flux_old = flux
            upper_old, speed_old = upper, speed
        above_old = above


def sides(one, two, low, high, rank, last, edges, length):
    even = rank % 2 == 0
    for field in range(5):
        first, final = edges(field)
        for layer in range(3):
            row = (field * 3 + layer) * length
            a, b = one[row : row + length, :], two[row : row + length, :]
            low[row : row + length, :] = jnp.where(rank == 0, first, jnp.where(even, b, a))
            high[row : row + length, :] = jnp.where(rank == last, final, jnp.where(even, a, b))


def split_kernel(place, state, x_one, x_two, y_one, y_two, padded, inverse_of, sound):
    even, oct_even = place[0] % 2 == 0, place[1] % 2 == 0
    x_starts = (jnp.where(even, NX - 3, 0), jnp.where(even, 0, NX - 3))
    y_starts = (jnp.where(oct_even, NY - 3, 0), jnp.where(oct_even, 0, NY - 3))
    for f in range(5):
        for out, start in ((x_one, x_starts[0]), (x_two, x_starts[1])):
            out[f * 96 : f * 96 + 96, :] = state[pl.ds(pl.multiple_of(f * ROWS + start * NY, 32), 96), :]
    for x in range(NX):
        for y in range(0, NY, 8):
            row = x * NY + y
            q = [state[f * ROWS + row : f * ROWS + row + 8, :] for f in range(5)]
            inverse = reciprocal(q[0])
            at = x * PITCH + y
            for f in range(5):
                padded[f * NX * PITCH + at : f * NX * PITCH + at + 8, :] = q[f]
            inverse_of[at : at + 8, :] = inverse
            sound[at : at + 8, :] = sound_of(q, inverse)
    for f in range(5):
        for out, start in ((y_one, y_starts[0]), (y_two, y_starts[1])):
            for layer in range(3):
                row = (f * 3 + layer) * 16
                out[row : row + 16, :] = padded[pl.ds(f * NX * PITCH + start + layer, 16, stride=PITCH), :]


def turn_kernel(place, state, fine_pairs, fine_count, coarse_pairs, turned, fine_uses, coarse_uses):
    def turn(step, _):
        flat = state[pl.ds(pl.multiple_of(step * 128, 128), 128), :].T
        base = pl.multiple_of(step * TALL, 8)
        turned[pl.ds(base + 8, 128), :] = flat
        turned[pl.ds(base, 8), :] = jnp.broadcast_to(flat[0:1], (8, 128))
        turned[pl.ds(base + 136, 8), :] = jnp.broadcast_to(flat[127:128], (8, 128))
        return 0

    lax.fori_loop(0, 20, turn, 0, unroll=4)
    lane = iota((8, 128), 1)
    codes = jnp.concatenate([fine_pairs[...].astype(F32)] * 4, axis=1).T[0:32]
    spread = (iota((16, 128), 1) % 16 == iota((16, 128), 0)).astype(F32)
    used = fold_rows(
        jnp.dot(fine_count[...].astype(F32), spread, precision=HIGH, preferred_element_type=F32), 16
    )
    codes = jnp.where(iota((32, 128), 0).astype(F32) < used, codes, -1000.0)
    down = 25.0 * iota((8, 128), 0).astype(F32)
    codes = [jnp.broadcast_to(codes[j : j + 1], (8, 128)) - down for j in range(32)]
    for plane in range(25):
        count = jnp.zeros((8, 128), F32)
        for each in codes:
            count = count + jnp.where(each == plane, 1.0, 0.0)
        fine_uses[plane * 8 : plane * 8 + 8, :] = count

    lane = iota((8, 128), 1)
    device = lane % place[2] * place[3] + lane // place[2]
    for half in range(2):
        named = coarse_pairs[half * 8 : half * 8 + 8, :]
        named = [jnp.broadcast_to(named[:, j : j + 1], (8, 128)) - 16 * device for j in range(32)]
        for lp in range(16):
            count = jnp.zeros((8, 128), F32)
            for each in named:
                count = count + jnp.where(each == lp, 1.0, 0.0)
            row = (lp * 2 + half) * 8
            coarse_uses[row : row + 8, :] = count


def along_z_kernel(turned, changes):
    def column(step, _):
        def load(f, i):
            return turned[pl.ds(pl.multiple_of((f * 4 + step) * TALL, 8) + 8 + i, 8, stride=16), :]

        def speed_at(i, q):
            inverse = reciprocal(q[0])
            return jnp.abs(q[3]) * inverse + sound_of(q, inverse)

        def store(i, values):
            for f in range(5):
                changes[pl.ds(pl.multiple_of((f * 4 + step) * 128, 8) + i, 8, stride=16), :] = values[f]

        sweep(load, speed_at, store, 16, 2)
        return 0

    lax.fori_loop(0, 4, column, 0)


def along_x_kernel(place, state, x_one, x_two, inverse_of, sound, others, out, low, high):
    def edges(f):
        return state[f * ROWS : f * ROWS + NY, :], state[f * ROWS + ROWS - NY : f * ROWS + ROWS, :]

    sides(x_one, x_two, low, high, place[0], place[2] - 1, edges, NY)

    def column(step, _):
        start = pl.multiple_of(step * 8, 8)

        def rows(f, i):
            return pl.ds(pl.multiple_of(f * ROWS + i * NY + start, 8), 8)

        def load(f, i):
            if i < 0:
                return low[pl.ds(pl.multiple_of((f * 3 + i + 3) * NY + start, 8), 8), :]
            if i >= NX:
                return high[pl.ds(pl.multiple_of((f * 3 + i - NX) * NY + start, 8), 8), :]
            return state[rows(f, i), :]

        def speed_at(i, q):
            if 0 <= i < NX:
                at = pl.ds(i * PITCH + start, 8)
                inverse, own = inverse_of[at, :], sound[at, :]
            else:
                inverse = reciprocal(q[0])
                own = sound_of(q, inverse)
            return jnp.abs(q[1]) * inverse + own

        def store(i, values):
            for f in range(5):
                out[rows(f, i), :] = others[rows(f, i), :] + values[f]

        sweep(load, speed_at, store, NX, 0)
        return 0

    lax.fori_loop(0, NY // 8, column, 0)


def along_y_kernel(place, padded, y_one, y_two, inverse_of, sound, changes, out, low, high, by_y):
    def edges(f):
        return [padded[pl.ds(f * NX * PITCH + y, NX, stride=PITCH), :] for y in (0, NY - 1)]

    sides(y_one, y_two, low, high, place[1], place[3] - 1, edges, NX)

    def column(step, _):
        start = pl.multiple_of(step * 8, 8)

        def rows(f, i):
            return pl.ds((f * NX + start) * PITCH + i, 8, stride=PITCH)

        def load(f, i):
            if i < 0:
                return low[pl.ds(pl.multiple_of((f * 3 + i + 3) * NX + start, 8), 8), :]
            if i >= NY:
                return high[pl.ds(pl.multiple_of((f * 3 + i - NY) * NX + start, 8), 8), :]
            return padded[rows(f, i), :]

        def speed_at(i, q):
            if 0 <= i < NY:
                inverse, own = inverse_of[rows(0, i), :], sound[rows(0, i), :]
            else:
                inverse = reciprocal(q[0])
                own = sound_of(q, inverse)
            return jnp.abs(q[2]) * inverse + own

        def store(i, values):
            for f in range(5):
                by_y[rows(f, i), :] = values[f]

        for f in range(5):
            for half in range(2):
                block = pl.multiple_of(f * ROWS + (step * 2 + half) * 128, 128)
                out[pl.ds(block, 128), :] = changes[pl.ds(block, 128), :].T
        sweep(load, speed_at, store, NY, 1)
        return 0

    lax.fori_loop(0, NX // 8, column, 0)

    def total(x, _):
        for f in range(5):
            for y in range(0, NY, 8):
                row = pl.ds(pl.multiple_of(f * ROWS + x * NY + y, 8), 8)
                out[row, :] = out[row, :] + by_y[pl.ds((f * NX + x) * PITCH + y, 8), :]
        return 0

    lax.fori_loop(0, NX, total, 0, unroll=2)


def tensors(r, square):
    square = jnp.maximum(square, 1.0)
    cube = 1.0 / (square * jnp.sqrt(square))
    three = 3.0 * cube / square
    scaled = [three * each for each in r]
    pull = [each * cube for each in r]
    tide = [scaled[i] * r[j] - cube if i == j else scaled[i] * r[j] for i, j in SYM]
    return pull, tide


def add_terms(totals, uses, r, square, mass, dipole):
    pull, tide = tensors(r, square)
    mass = uses * mass
    dipole = [uses * d for d in dipole]
    for i in range(3):
        term = mass * pull[i]
        for j in range(3):
            term = term - tide[sym(i, j)] * dipole[j]
        totals[i] = totals[i] + term
    for e in range(6):
        totals[3 + e] = totals[3 + e] + mass * tide[e]


def far_fields(place, uses_fine, uses_coarse, got, around):
    morton, octant = place[0], place[1]
    mortons, octs = place[2], place[3]
    lane = iota((8, 128), 1)
    lane_row = iota((1, 128), 1)

    rows = jnp.concatenate([got[pl.ds(g * 8 * SENT + 4, 8, stride=SENT), :] for g in range(16)], axis=0)
    time_step = COURANT / jnp.max(rows[:, 64:128])
    moments = rows.T
    target_z = iota((8, 128), 0)
    rx = 16.0 * (lane % mortons - morton).astype(F32)
    coarse = []
    for half in range(2):
        totals = [jnp.zeros((8, 128), F32) for _ in range(9)]
        for lp in range(16):
            ry = 16.0 * (lane // mortons * 2 + lp // 8 - (2 * octant + half)).astype(F32)
            rz = 16.0 * (lp % 8 - target_z).astype(F32)
            own = [jnp.broadcast_to(moments[m * 16 + lp : m * 16 + lp + 1], (8, 128)) for m in range(4)]
            row = (lp * 2 + half) * 8
            add_terms(totals, uses_coarse[row : row + 8, :], (rx, ry, rz), rx * rx + ry * ry + rz * rz, own[0], own[1:])
        coarse.append([jnp.sum(each, axis=1, keepdims=True) for each in totals])
    result = []
    for e in range(9):
        column = jnp.where(lane // 32 % 2 == 0, coarse[0][e], coarse[1][e])
        column = jnp.where(lane % 16 // 2 == iota((8, 128), 0), column, 0.0)
        result.append(jnp.sum(column, axis=0, keepdims=True))
    side = [4.0 * (2 * s - 1).astype(F32) for s in (lane_row // 64, lane_row // 16 % 2, lane_row % 2)]
    for i in range(3):
        for j in range(3):
            result[i] = result[i] + result[3 + sym(i, j)] * side[j]

    blocks = []
    for dy in (-1, 0, 1):
        block = []
        for dx in (-1, 0, 1):
            at_x, at_y = morton + dx, octant + dy
            inside = (at_x >= 0) & (at_x < mortons) & (at_y >= 0) & (at_y < octs)
            device = jnp.clip(at_y, 0, octs - 1) * mortons + jnp.clip(at_x, 0, mortons - 1)
            for m in range(4):
                block.append(jnp.where(inside, got[pl.ds(device * SENT + m, 1), :], 0.0))
        blocks.append(jnp.concatenate(block + [jnp.zeros((4, 128), F32)], axis=0))
    wide = iota((16, 128), 1)
    around[...] = jnp.zeros(around.shape, F32)
    for oy in range(-2, 3):
        if oy == 0:
            moved = blocks[1]
        else:
            moved = pltpu.roll(blocks[1], (-16 * oy) % 128, 1)
            if oy > 0:
                moved = jnp.where(wide // 16 % 4 + oy > 3, pltpu.roll(blocks[2], (64 - 16 * oy) % 128, 1), moved)
            else:
                moved = jnp.where(wide // 16 % 4 + oy < 0, pltpu.roll(blocks[0], (-64 - 16 * oy) % 128, 1), moved)
        swapped = pltpu.roll(moved, 64, 1)
        for m in range(4):
            low, own, high = [(moved[d * 4 + m : d * 4 + m + 1], swapped[d * 4 + m : d * 4 + m + 1]) for d in range(3)]
            first = lane_row < 64
            lines = [
                low[0], jnp.where(first, low[1], own[1]), own[0], jnp.where(first, own[1], high[1]), high[0],
            ]
            row = (m * 5 + oy + 2) * 8
            around[row : row + 5, :] = jnp.concatenate(lines, axis=0)
    totals = [jnp.zeros((8, 128), F32) for _ in range(9)]
    rx = 8.0 * (iota((8, 128), 0) - 2).astype(F32)
    square_x = rx * rx
    for oy in range(-2, 3):
        base = [around[(m * 5 + oy + 2) * 8 : (m * 5 + oy + 2) * 8 + 8, :] for m in range(4)]
        for oz in range(-2, 3):
            moved = base
            if oz:
                ok = (lane % 16 + oz >= 0) & (lane % 16 + oz < 16)
                moved = [jnp.where(ok, pltpu.roll(each, (-oz) % 128, 1), 0.0) for each in base]
            plane = ((oy + 2) * 5 + oz + 2) * 8
            add_terms(
                totals, uses_fine[plane : plane + 8, :], (rx, 8.0 * oy, 8.0 * oz),
                square_x + (64.0 * oy * oy + 64.0 * oz * oz), moved[0], moved[1:],
            )
    for e in range(9):
        result[e] = GRAVITY * (result[e] + jnp.sum(totals[e], axis=0, keepdims=True))
    return result, time_step


def update_kernel(place, state, twice, uses_fine, uses_coarse, got, new, gravity, around, field, step_size):
    slab = pl.program_id(0)
    layers = state.shape[1] // NY

    @pl.when(slab == 0)
    def _():
        result, time_step = far_fields(place, uses_fine, uses_coarse, got, around)
        step_size[0] = time_step
        keep = iota((8, 128), 1) // 16 == iota((8, 128), 0)
        spread = (iota((128, 128), 0) % 16 == iota((128, 128), 1) // 8).astype(F32)
        rows = jnp.concatenate([jnp.where(keep, each, 0.0) for each in result], axis=0)
        rows = jnp.dot(rows, spread, precision=HIGH, preferred_element_type=F32)
        rows = [rows[e * 8 : e * 8 + 8] for e in range(9)]
        offset_z = (iota((8, 128), 1) % 8).astype(F32) - 3.5
        for i in range(3):
            field[i * 8 : i * 8 + 8, :] = rows[i] + rows[3 + sym(i, 2)] * offset_z
            field[(3 + i) * 8 : (3 + i) * 8 + 8, :] = rows[3 + sym(i, 0)]
            field[(6 + i) * 8 : (6 + i) * 8 + 8, :] = rows[3 + sym(i, 1)]

    time_step = step_size[0]
    half = 0.5 * time_step
    offset_y = iota((8, 128), 0).astype(F32) - 3.5
    for ty in range(4):
        tx = slab * layers // 8
        at = tx * 4 + ty
        base = [
            field[pl.ds(i * 8 + at, 1), :] + field[pl.ds((6 + i) * 8 + at, 1), :] * offset_y for i in range(3)
        ]
        slope = [field[pl.ds((3 + i) * 8 + at, 1), :] for i in range(3)]
        for layer in range(layers):
            offset_x = ((slab * layers + layer) % 8).astype(F32) - 3.5
            row = layer * NY + ty * 8
            q = [state[f, row : row + 8, :] for f in range(5)]
            pull = [base[i] + slope[i] * offset_x for i in range(3)]
            for i in range(3):
                gravity[i, row : row + 8, :] = pull[i]
            moved = [q[f] - half * twice[f, row : row + 8, :] for f in range(5)]
            new[0, row : row + 8, :] = moved[0]
            weight = time_step * q[0]
            for i in range(3):
                new[1 + i, row : row + 8, :] = moved[1 + i] + weight * pull[i]
            gain = q[1] * pull[0] + q[2] * pull[1] + q[3] * pull[2]
            new[4, row : row + 8, :] = moved[4] + time_step * gain


VMEM = pl.BlockSpec(memory_space=pltpu.VMEM)
SMEM = pl.BlockSpec(memory_space=pltpu.SMEM)
LIMIT = pltpu.CompilerParams(vmem_limit_bytes=12 * 1024 * 1024)
SMALL = pl.CostEstimate(flops=1000, bytes_accessed=1000, transcendentals=0)


def shaped(*shape):
    return jax.ShapeDtypeStruct(shape, F32)


def call(kernel, outs, scratch, *args):
    return pl.pallas_call(
        kernel,
        out_shape=[shaped(rows, 128) for rows in outs],
        in_specs=[SMEM if a.shape == (4,) else VMEM for a in args],
        out_specs=[VMEM] * len(outs),
        scratch_shapes=[pltpu.VMEM((rows, 128), F32) for rows in scratch],
        compiler_params=LIMIT,
        cost_estimate=SMALL,
    )(*args)


def moments_of(fields):
    return pl.pallas_call(
        moments_kernel,
        out_shape=shaped(128 * SENT, 128),
        in_specs=[pl.BlockSpec(memory_space=pltpu.HBM)],
        out_specs=VMEM,
        scratch_shapes=[pltpu.VMEM((5, ROWS, 128), F32), pltpu.SemaphoreType.DMA((4,))],
        compiler_params=LIMIT,
        cost_estimate=SMALL,
    )(fields)


def update(place, rows, twice, uses_fine, uses_coarse, got):
    slabs = 4
    part = ROWS // slabs
    at_slab = lambda i: (0, i, 0)
    at_start = lambda i: (0, 0)
    return pl.pallas_call(
        update_kernel,
        grid=(slabs,),
        out_shape=[shaped(5, ROWS, 128), shaped(3, ROWS, 128)],
        in_specs=[
            pl.BlockSpec(memory_space=pltpu.SMEM),
            pl.BlockSpec((5, part, 128), at_slab),
            pl.BlockSpec((5, part, 128), at_slab),
            pl.BlockSpec((200, 128), at_start),
            pl.BlockSpec((256, 128), at_start),
            pl.BlockSpec((128 * SENT, 128), at_start),
        ],
        out_specs=[pl.BlockSpec((5, part, 128), at_slab), pl.BlockSpec((3, part, 128), at_slab)],
        scratch_shapes=[pltpu.VMEM((160, 128), F32), pltpu.VMEM((72, 128), F32), pltpu.SMEM((1,), F32)],
        compiler_params=LIMIT,
    )(place, rows.reshape(5, ROWS, 128), twice.reshape(5, ROWS, 128), uses_fine, uses_coarse, got)


def local(state, fine_pairs, fine_count, coarse_pairs):
    mortons, octs = lax.axis_size("morton"), lax.axis_size("oct")
    place = jnp.stack([lax.axis_index("morton"), lax.axis_index("oct"), mortons, octs]).astype(jnp.int32)
    many = NX * PITCH

    def swap(values, pair):
        pairs = [(m, o) for m in range(mortons) for o in range(octs)]
        index = lambda place: place[0] * octs + place[1]
        return lax.ppermute(values, AXES, [(index(p), index(pair(*p))) for p in pairs])

    def other(i):
        return (i - 1 ^ 1) + 1

    sent = moments_of(pltpu.with_memory_space_constraint(state.reshape(5, ROWS, 128), pltpu.HBM))
    got = lax.all_to_all(sent.reshape(mortons * octs, 1, SENT * 128), AXES[::-1], 0, 0, tiled=True)
    rows = state.reshape(5 * ROWS, 128)
    rows, _ = lax.optimization_barrier((rows, sent))
    x_one, x_two, y_one, y_two, padded, inverse_of, sound = call(
        split_kernel, [480, 480, 240, 240, 5 * many, many, many], [], place, rows
    )
    y_one = swap(y_one, lambda m, o: (m, o ^ 1))
    y_two = swap(y_two, lambda m, o: (m, other(o)) if 0 < o < octs - 1 else (m ^ 4, o))
    x_one = swap(x_one, lambda m, o: (m ^ 1, o))
    turned, uses_fine, uses_coarse = call(
        turn_kernel, [20 * TALL, 200, 256], [],
        place, rows, fine_pairs.reshape(128, 32), fine_count.reshape(8, 16), coarse_pairs.reshape(16, 32),
    )
    x_two = swap(x_two, lambda m, o: (other(m), o) if 0 < m < mortons - 1 else (m, o ^ 1))
    (changes,) = call(along_z_kernel, [5 * ROWS], [], turned)
    (twice,) = call(
        along_y_kernel, [5 * ROWS], [240, 240, 5 * many],
        place, padded, y_one, y_two, inverse_of, sound, changes,
    )
    (twice,) = call(along_x_kernel, [5 * ROWS], [480, 480], place, rows, x_one, x_two, inverse_of, sound, twice)
    new, gravity = update(place, rows, twice, uses_fine, uses_coarse, got.reshape(mortons * octs * SENT, 128))
    return new.reshape(state.shape), gravity.reshape(3, NX, NY, NZ)


def solution(mesh):
    in_specs = (
        P(None, "morton", "oct", None),
        P("morton", "oct", None, None),
        P("morton", "oct", None),
        P("morton", "oct", None, None),
    )
    out_specs = (P(None, "morton", "oct", None), P(None, "morton", "oct", None))
    return jax.shard_map(local, mesh=mesh, in_specs=in_specs, out_specs=out_specs, check_vma=False)
```

```python
import functools

import functools

import jax
import jax.numpy as jnp
from jax import lax
from jax.experimental import pallas as pl
from jax.experimental.pallas import tpu as pltpu
from jax.sharding import PartitionSpec as P

ADIABATIC = 5.0 / 3.0
COURANT = 0.2
GRAVITY = 1.0
AXES = ("morton", "oct")
F32 = jnp.float32
HIGH = lax.Precision.HIGHEST

NX, NY, NZ = 16, 32, 128
ROWS = NX * NY
PITCH = 33
TALL = 144
SENT = 5
SYM = ((0, 0), (0, 1), (0, 2), (1, 1), (1, 2), (2, 2))


def iota(shape, dim):
    return lax.broadcasted_iota(jnp.int32, shape, dim)


def sym(i, j):
    return SYM.index((min(i, j), max(i, j)))


def reciprocal(x):
    return pl.reciprocal(x, approx=True)


def sound_of(q, inverse):
    kinetic = (q[1] * q[1] + q[2] * q[2] + q[3] * q[3]) * inverse
    pressure = (2.0 / 3.0) * q[4] - (1.0 / 3.0) * kinetic
    square = ADIABATIC * pressure * inverse
    return square * lax.rsqrt(square)


def fold_rows(values, group):
    keep = iota(values.shape, 1) // group == iota(values.shape, 0)
    return jnp.sum(jnp.where(keep, values, 0.0), axis=0, keepdims=True)


def moments_kernel(
    place, state, sent, x_one, x_two, y_one, y_two, rows, near_sent, near_one, near_two, arrived, taken, written
):
    part = ROWS // 4
    copies = [
        pltpu.make_async_copy(
            state.at[:, pl.ds(c * part, part), :], rows.at[:, pl.ds(c * part, part), :], arrived.at[c]
        )
        for c in range(4)
    ]
    even, oct_even = place[0] % 2 == 0, place[1] % 2 == 0
    x_starts = (jnp.where(even, NX - 3, 0), jnp.where(even, 0, NX - 3))
    y_starts = (jnp.where(oct_even, NY - 3, 0), jnp.where(oct_even, 0, NY - 3))
    edges = [
        pltpu.make_async_copy(
            rows.at[f, pl.ds(pl.multiple_of(start * NY, 32), 96), :], out.at[pl.ds(f * 96, 96), :], taken.at[n, f]
        )
        for n, (out, start) in enumerate(((x_one, x_starts[0]), (x_two, x_starts[1])))
        for f in range(5)
    ]
    for copy in copies:
        copy.start()
    offset_y = iota((8, 128), 0).astype(F32) - 3.5
    fastest = jnp.zeros((8, 128), F32)
    sums, sums_x, sums_y = [], [], []
    for tx in range(2):
        totals, totals_x = [jnp.zeros((8, 128), F32)] * 4, [jnp.zeros((8, 128), F32)] * 4
        for half in range(2):
            copies[tx * 2 + half].wait()
            for x in range(half * 4, half * 4 + 4):
                for ty in range(4):
                    row = (tx * 8 + x) * NY + ty * 8
                    q = [rows[f, row : row + 8, :] for f in range(5)]
                    inverse = reciprocal(q[0])
                    speed_of_sound = sound_of(q, inverse)
                    largest = jnp.maximum(jnp.maximum(jnp.abs(q[1]), jnp.abs(q[2])), jnp.abs(q[3]))
                    fastest = jnp.maximum(fastest, largest * inverse + speed_of_sound)
                    totals[ty] = totals[ty] + q[0]
                    totals_x[ty] = totals_x[ty] + q[0] * (x - 3.5)
        for ty in range(4):
            sums.append(jnp.sum(totals[ty], axis=0, keepdims=True))
            sums_x.append(jnp.sum(totals_x[ty], axis=0, keepdims=True))
            sums_y.append(jnp.sum(totals[ty] * offset_y, axis=0, keepdims=True))
    for copy in edges:
        copy.start()
    for out, start in ((near_one, y_starts[0]), (near_two, y_starts[1])):
        for f in range(5):
            for x in range(NX):
                row = (f * NX + x) * 3
                out[row : row + 3, :] = rows[f, pl.ds(x * NY + start, 3), :]
    writes = [
        pltpu.make_async_copy(near, out, written.at[n])
        for n, (near, out) in enumerate(((near_one, y_one), (near_two, y_two), (near_sent, sent)))
    ]
    writes[0].start()
    writes[1].start()
    lines = jnp.concatenate(sums + sums_x + sums_y, axis=0)
    z = iota((128, 128), 0)
    pick = (z // 8 == iota((128, 128), 1) % 16).astype(F32)
    by_z = pick * ((z % 8).astype(F32) - 3.5)
    folded = jnp.dot(lines, pick, precision=HIGH, preferred_element_type=F32)
    folded_z = jnp.dot(lines[0:8], by_z, precision=HIGH, preferred_element_type=F32)
    mass = fold_rows(folded[0:8], 16)
    dipole = [fold_rows(folded[8:16], 16), fold_rows(folded[16:24], 16), fold_rows(folded_z, 16)]

    lane = iota((1, 128), 1)
    odd = [lane // 64, lane // 16 % 2, lane % 2]
    shifted = [d + 4.0 * (2 * o - 1).astype(F32) * mass for d, o in zip(dipole, odd, strict=True)]
    t = iota((128, 128), 0)
    parent = t // 32 % 2 * 8 + t % 16 // 2
    pick = (parent == iota((128, 128), 1) % 16).astype(F32)
    families = jnp.concatenate([mass] + shifted + [jnp.zeros((4, 128), F32)], axis=0)
    families = jnp.dot(families, pick, precision=HIGH, preferred_element_type=F32)
    last = jnp.where(lane < 64, fold_rows(families, 16), jnp.max(fastest))
    five = jnp.concatenate([mass] + dipole + [last], axis=0)
    many = jnp.concatenate([five] * 8, axis=0)
    for copy in range(16):
        near_sent[copy * 40 : copy * 40 + 40, :] = many
    writes[2].start()
    for copy in edges + writes:
        copy.wait()


def rise(before, here, after):
    value = 0.5 * here + (1.0 / 12.0) * (before - after)
    return jnp.minimum(jnp.maximum(value, jnp.minimum(here, 0.0)), jnp.maximum(here, 0.0))


def upper_and_lower(centre, up, down):
    most_up, most_down = jnp.abs(down + down), jnp.abs(up + up)
    upper = centre + jnp.minimum(jnp.maximum(up, -most_up), most_up)
    lower = centre + jnp.minimum(jnp.maximum(down, -most_down), most_down)
    return upper, lower


def flux_of(q, k):
    inverse = reciprocal(q[0])
    velocity = q[1 + k] * inverse
    kinetic = (q[1] * q[1] + q[2] * q[2] + q[3] * q[3]) * inverse
    pressure = (2.0 / 3.0) * q[4] - (1.0 / 3.0) * kinetic
    out = [q[1 + k]] + [q[1 + c] * velocity for c in range(3)] + [(q[4] + pressure) * velocity]
    out[1 + k] = out[1 + k] + pressure
    return out


def twice_flux(left, right, speed, k):
    from_left, from_right = flux_of(left, k), flux_of(right, k)
    return [
        (a + b) - speed * (r - l) for a, b, l, r in zip(from_left, from_right, left, right, strict=True)
    ]


def sweep(load, speed_at, store, length, k, beside=()):
    beside = list(beside)
    share = -(-len(beside) // length)
    last = [load(f, -1) for f in range(5)]
    steps = [[load(f, i + 1) - load(f, i) for f in range(5)] for i in (-3, -2)]
    cell = [load(f, -2) for f in range(5)], last
    ups = upper_old = speed_old = flux_old = None
    for i in range(-2, length + 1):
        ahead = [load(f, i + 2) for f in range(5)]
        steps.append([a - b for a, b in zip(ahead, cell[1], strict=True)])
        now = [rise(*each) for each in zip(*steps, strict=True)]
        if ups is not None:
            downs = [u - d for u, d in zip(ups, steps[0], strict=True)]
            pairs = [upper_and_lower(*each) for each in zip(cell[0], now, downs, strict=True)]
            upper, lower = [p[0] for p in pairs], [p[1] for p in pairs]
            speed = speed_at(i, cell[0])
            if upper_old is not None:
                flux = twice_flux(upper_old, lower, jnp.maximum(speed_old, speed), k)
                if flux_old is not None:
                    store(i - 1, [a - b for a, b in zip(flux, flux_old, strict=True)])
                flux_old = flux
            upper_old, speed_old = upper, speed
        for call in beside[:share]:
            call()
        beside = beside[share:]
        ups, cell, steps = now, (cell[1], ahead), steps[1:]
    for call in beside:
        call()


def sides(one, two, low, high, rank):
    even = rank % 2 == 0
    for row in range(0, one.shape[0], 8):
        a, b = one[row : row + 8, :], two[row : row + 8, :]
        low[row : row + 8, :] = jnp.where(even, b, a)
        high[row : row + 8, :] = jnp.where(even, a, b)


def inner_kernel(
    place, state, far_pairs, far_count, far_coarse, by_z, padded, inverse_of, sound, fine_uses, coarse_uses,
    turned_even, turned_odd, changes_even, changes_odd, fine_pairs, fine_count, coarse_pairs, arrived,
):
    turned, changes = (turned_even, turned_odd), (changes_even, changes_odd)

    def turn(block, f):
        into, base = turned[block % 2], f * TALL
        flat = state[f * ROWS + block * 128 : f * ROWS + block * 128 + 128, :].T
        into[base + 8 : base + 136, :] = flat
        into[base : base + 8, :] = jnp.broadcast_to(flat[0:1], (8, 128))
        into[base + 136 : base + 144, :] = jnp.broadcast_to(flat[127:128], (8, 128))

    def turn_back(block, f):
        flat = changes[block % 2][f * 128 : f * 128 + 128, :]
        by_z[f * ROWS + block * 128 : f * ROWS + block * 128 + 128, :] = flat.T

    def along_z(block, beside):
        source, into = turned[block % 2], changes[block % 2]

        def load(f, i):
            return source[pl.ds(f * TALL + 8 + i, 8, stride=16), :]

        def speed_at(i, q):
            inverse = reciprocal(q[0])
            return jnp.abs(q[3]) * inverse + sound_of(q, inverse)

        def store(i, values):
            for f in range(5):
                into[pl.ds(f * 128 + i, 8, stride=16), :] = values[f]

        sweep(load, speed_at, store, 16, 2, beside)

    reads = [
        pltpu.make_async_copy(source, into, arrived.at[n])
        for n, (source, into) in enumerate(
            ((far_pairs, fine_pairs), (far_count, fine_count), (far_coarse, coarse_pairs))
        )
    ]
    for copy in reads:
        copy.start()
    for f in range(5):
        turn(0, f)
    for block in range(4):
        beside = []
        for f in range(5):
            if block < 3:
                beside.append(functools.partial(turn, block + 1, f))
            if block > 0:
                beside.append(functools.partial(turn_back, block - 1, f))
        along_z(block, beside)
    for f in range(5):
        turn_back(3, f)
    for copy in reads:
        copy.wait()
    codes = jnp.concatenate([fine_pairs[...].astype(F32)] * 4, axis=1).T[0:32]
    spread = (iota((16, 128), 1) % 16 == iota((16, 128), 0)).astype(F32)
    used = fold_rows(
        jnp.dot(fine_count[...].astype(F32), spread, precision=HIGH, preferred_element_type=F32), 16
    )
    codes = jnp.where(iota((32, 128), 0).astype(F32) < used, codes, 1000.0)
    along = jnp.floor((codes + 0.5) * 0.04)
    plane = codes - 25.0 * along
    group = jnp.floor((plane + 0.5) * 0.2)
    one = jnp.left_shift(1, (6.0 * (plane - 5.0 * group)).astype(jnp.int32))
    ones = [jnp.where(group == g, one, 0) for g in range(5)]
    for g in range(5):
        lines = []
        for ox in range(5):
            hits = jnp.where(along == ox, ones[g], 0)
            hits = (hits[0:8] + hits[8:16]) + (hits[16:24] + hits[24:32])
            lines.append(jnp.sum(hits, axis=0, keepdims=True))
        fine_uses[g * 8 : g * 8 + 8, :] = jnp.concatenate(lines + [jnp.zeros((3, 128), jnp.int32)], axis=0)

    slot = iota((8, 128), 1)
    device = slot % place[2] * place[3] + slot // place[2]
    for half in range(2):
        named = coarse_pairs[half * 8 : half * 8 + 8, :]
        coded = named // 16 + named % 4 * (6 * 256) + named // 4 % 4 * 65536
        counts = [jnp.zeros((8, 128), jnp.int32) for _ in range(4)]
        for j in range(32):
            code = jnp.broadcast_to(coded[:, j : j + 1], (8, 128))
            one = jnp.where((code & 255) == device, jnp.left_shift(1, (code >> 8) & 255), 0)
            group = code >> 16
            counts = [each + jnp.where(group == g, one, 0) for g, each in enumerate(counts)]
        for g in range(4):
            coarse_uses[(g * 2 + half) * 8 : (g * 2 + half) * 8 + 8, :] = counts[g]
    for x in range(NX):
        for y in range(0, NY, 8):
            row = x * NY + y
            q = [state[f * ROWS + row : f * ROWS + row + 8, :] for f in range(5)]
            inverse = reciprocal(q[0])
            at = x * PITCH + y
            for f in range(5):
                padded[f * NX * PITCH + at : f * NX * PITCH + at + 8, :] = q[f]
            inverse_of[at : at + 8, :] = inverse
            sound[at : at + 8, :] = sound_of(q, inverse)


def tensors(r, square):
    root = lax.rsqrt(jnp.maximum(square, 1.0))
    cube = root * root * root
    three = 3.0 * cube * (root * root)
    scaled = [three * each for each in r]
    pull = [each * cube for each in r]
    tide = [scaled[i] * r[j] - cube if i == j else scaled[i] * r[j] for i, j in SYM]
    return pull, tide


def add_terms(totals, uses, r, square, mass, dipole):
    pull, tide = tensors(r, square)
    mass = uses * mass
    dipole = [uses * d for d in dipole]
    for i in range(3):
        term = mass * pull[i]
        for j in range(3):
            term = term - tide[sym(i, j)] * dipole[j]
        totals[i] = totals[i] + term
    for e in range(6):
        totals[3 + e] = totals[3 + e] + mass * tide[e]


def far_fields(place, uses_fine, uses_coarse, got, around):
    morton, octant = place[0], place[1]
    mortons, octs = place[2], place[3]
    lane = iota((8, 128), 1)
    lane_row = iota((1, 128), 1)

    rows = jnp.concatenate([got[pl.ds(g * 8 * SENT + 4, 8, stride=SENT), :] for g in range(16)], axis=0)
    time_step = COURANT / jnp.max(rows[:, 64:128])
    moments = rows.T
    target_z = iota((8, 128), 0)
    rx = 16.0 * (lane % mortons - morton).astype(F32)
    coarse = []
    for half in range(2):
        totals = [jnp.zeros((8, 128), F32) for _ in range(9)]
        for lp in range(16):
            ry = 16.0 * (lane // mortons * 2 + lp // 8 - (2 * octant + half)).astype(F32)
            rz = 16.0 * (lp % 8 - target_z).astype(F32)
            own = [jnp.broadcast_to(moments[m * 16 + lp : m * 16 + lp + 1], (8, 128)) for m in range(4)]
            row = (lp // 4 * 2 + half) * 8
            uses = ((uses_coarse[row : row + 8, :] >> (lp % 4 * 6)) & 63).astype(F32)
            add_terms(totals, uses, (rx, ry, rz), rx * rx + ry * ry + rz * rz, own[0], own[1:])
        coarse.append([jnp.sum(each, axis=1, keepdims=True) for each in totals])
    result = []
    for e in range(9):
        column = jnp.where(lane // 32 % 2 == 0, coarse[0][e], coarse[1][e])
        column = jnp.where(lane % 16 // 2 == iota((8, 128), 0), column, 0.0)
        result.append(jnp.sum(column, axis=0, keepdims=True))
    side = [4.0 * (2 * s - 1).astype(F32) for s in (lane_row // 64, lane_row // 16 % 2, lane_row % 2)]
    for i in range(3):
        for j in range(3):
            result[i] = result[i] + result[3 + sym(i, j)] * side[j]

    blocks = []
    for dy in (-1, 0, 1):
        block = []
        for dx in (-1, 0, 1):
            at_x, at_y = morton + dx, octant + dy
            inside = (at_x >= 0) & (at_x < mortons) & (at_y >= 0) & (at_y < octs)
            device = jnp.clip(at_y, 0, octs - 1) * mortons + jnp.clip(at_x, 0, mortons - 1)
            for m in range(4):
                block.append(jnp.where(inside, got[pl.ds(device * SENT + m, 1), :], 0.0))
        blocks.append(jnp.concatenate(block + [jnp.zeros((4, 128), F32)], axis=0))
    wide = iota((16, 128), 1)
    around[...] = jnp.zeros(around.shape, F32)
    for oy in range(-2, 3):
        if oy == 0:
            moved = blocks[1]
        else:
            moved = pltpu.roll(blocks[1], (-16 * oy) % 128, 1)
            if oy > 0:
                moved = jnp.where(wide // 16 % 4 + oy > 3, pltpu.roll(blocks[2], (64 - 16 * oy) % 128, 1), moved)
            else:
                moved = jnp.where(wide // 16 % 4 + oy < 0, pltpu.roll(blocks[0], (-64 - 16 * oy) % 128, 1), moved)
        swapped = pltpu.roll(moved, 64, 1)
        for m in range(4):
            low, own, high = [(moved[d * 4 + m : d * 4 + m + 1], swapped[d * 4 + m : d * 4 + m + 1]) for d in range(3)]
            first = lane_row < 64
            lines = [
                low[0], jnp.where(first, low[1], own[1]), own[0], jnp.where(first, own[1], high[1]), high[0],
            ]
            row = (m * 5 + oy + 2) * 8
            around[row : row + 5, :] = jnp.concatenate(lines, axis=0)
    totals = [jnp.zeros((8, 128), F32) for _ in range(9)]
    rx = 8.0 * (iota((8, 128), 0) - 2).astype(F32)
    square_x = rx * rx
    for oy in range(-2, 3):
        base = [around[(m * 5 + oy + 2) * 8 : (m * 5 + oy + 2) * 8 + 8, :] for m in range(4)]
        for oz in range(-2, 3):
            moved = base
            if oz:
                ok = (lane % 16 + oz >= 0) & (lane % 16 + oz < 16)
                moved = [jnp.where(ok, pltpu.roll(each, (-oz) % 128, 1), 0.0) for each in base]
            uses = ((uses_fine[(oy + 2) * 8 : (oy + 2) * 8 + 8, :] >> ((oz + 2) * 6)) & 63).astype(F32)
            add_terms(
                totals, uses, (rx, 8.0 * oy, 8.0 * oz),
                square_x + (64.0 * oy * oy + 64.0 * oz * oz), moved[0], moved[1:],
            )
    for e in range(9):
        result[e] = GRAVITY * (result[e] + jnp.sum(totals[e], axis=0, keepdims=True))
    return result, time_step


def along_y_kernel(place, padded, inverse_of, sound, y_one, y_two, by_z, out, low, high, by_y):
    sides(y_one, y_two, low, high, place[1])

    def edge(beyond, y):
        for f in range(5):
            cells = padded[pl.ds(f * NX * PITCH + y, NX, stride=PITCH), :]
            for layer in range(3):
                beyond[pl.ds(f * NX * 3 + layer, NX, stride=3), :] = cells

    pl.when(place[1] == 0)(lambda: edge(low, 0))
    pl.when(place[1] == place[3] - 1)(lambda: edge(high, NY - 1))

    def column(step, _):
        start = pl.multiple_of(step * 8, 8)

        def rows(f, i):
            return pl.ds((f * NX + start) * PITCH + i, 8, stride=PITCH)

        def load(f, i):
            if i < 0:
                return low[pl.ds((f * NX + start) * 3 + i + 3, 8, stride=3), :]
            if i >= NY:
                return high[pl.ds((f * NX + start) * 3 + i - NY, 8, stride=3), :]
            return padded[rows(f, i), :]

        def speed_at(i, q):
            if 0 <= i < NY:
                return jnp.abs(q[2]) * inverse_of[rows(0, i), :] + sound[rows(0, i), :]
            inverse = reciprocal(q[0])
            return jnp.abs(q[2]) * inverse + sound_of(q, inverse)

        def store(i, values):
            for f in range(5):
                by_y[rows(f, i), :] = values[f]

        sweep(load, speed_at, store, NY, 1)
        return 0

    lax.fori_loop(0, NX // 8, column, 0)

    def total(x, _):
        for f in range(5):
            for y in range(0, NY, 8):
                row = pl.ds(pl.multiple_of(f * ROWS + x * NY + y, 8), 8)
                out[row, :] = by_z[row, :] + by_y[pl.ds((f * NX + x) * PITCH + y, 8), :]
        return 0

    lax.fori_loop(0, NX, total, 0, unroll=2)


def outer_kernel(
    place, state, x_one, x_two, others, uses_fine, uses_coarse, got, new, gravity,
    low, high, around, field, made, pulls, written,
):
    sides(x_one, x_two, low, high, place[0])

    def edge(beyond, x):
        for f in range(5):
            cells = state[f * ROWS + x * NY : f * ROWS + x * NY + NY, :]
            for layer in range(3):
                beyond[(f * 3 + layer) * NY : (f * 3 + layer) * NY + NY, :] = cells

    pl.when(place[0] == 0)(lambda: edge(low, 0))
    pl.when(place[0] == place[2] - 1)(lambda: edge(high, NX - 1))
    result, time_step = far_fields(place, uses_fine, uses_coarse, got, around)
    half_step = 0.5 * time_step
    keep = iota((8, 128), 1) // 16 == iota((8, 128), 0)
    spread = (iota((128, 128), 0) % 16 == iota((128, 128), 1) // 8).astype(F32)
    lines = jnp.concatenate([jnp.where(keep, each, 0.0) for each in result], axis=0)
    lines = jnp.dot(lines, spread, precision=HIGH, preferred_element_type=F32)
    lines = [lines[e * 8 : e * 8 + 8] for e in range(9)]
    offset_z = (iota((8, 128), 1) % 8).astype(F32) - 3.5
    for i in range(3):
        field[i * 8 : i * 8 + 8, :] = lines[i] + lines[3 + sym(i, 2)] * offset_z
        field[(3 + i) * 8 : (3 + i) * 8 + 8, :] = lines[3 + sym(i, 0)]
        field[(6 + i) * 8 : (6 + i) * 8 + 8, :] = lines[3 + sym(i, 1)]
    offset_y = iota((8, 128), 0).astype(F32) - 3.5

    def writes(step):
        rows = pl.ds(pl.multiple_of(step * 8, 8), 8)
        return [
            pltpu.make_async_copy(made.at[:, :, rows, :], new.at[:, :, rows, :], written.at[0, step]),
            pltpu.make_async_copy(pulls.at[:, :, rows, :], gravity.at[:, :, rows, :], written.at[1, step]),
        ]

    def along_x(step, _):
        start = pl.multiple_of(step * 8, 8)

        def rows(f, i):
            return pl.ds(pl.multiple_of(f * ROWS + i * NY + start, 8), 8)

        def load(f, i):
            if i < 0:
                return low[pl.ds(pl.multiple_of((f * 3 + i + 3) * NY + start, 8), 8), :]
            if i >= NX:
                return high[pl.ds(pl.multiple_of((f * 3 + i - NX) * NY + start, 8), 8), :]
            return state[rows(f, i), :]

        lines = []
        for tx in range(2):
            at = [field[pl.ds(e * 8 + tx * 4 + step, 1), :] for e in range(9)]
            lines.append(([at[e] + at[6 + e] * offset_y for e in range(3)], at[3:6]))

        def store(i, values):
            base, slope = lines[i // 8]
            q = [state[rows(f, i), :] for f in range(5)]
            pull = [base[e] + slope[e] * (i % 8 - 3.5) for e in range(3)]
            moved = []
            for f in range(5):
                moved.append(q[f] - half_step * (values[f] + others[rows(f, i), :]))
            weight = time_step * q[0]
            gain = q[1] * pull[0] + q[2] * pull[1] + q[3] * pull[2]
            made[0, i, pl.ds(start, 8), :] = moved[0]
            for e in range(3):
                pulls[e, i, pl.ds(start, 8), :] = pull[e]
                made[1 + e, i, pl.ds(start, 8), :] = moved[1 + e] + weight * pull[e]
            made[4, i, pl.ds(start, 8), :] = moved[4] + time_step * gain

        def speed_at(i, q):
            inverse = reciprocal(q[0])
            return jnp.abs(q[1]) * inverse + sound_of(q, inverse)

        sweep(load, speed_at, store, NX, 0)
        for copy in writes(step):
            copy.start()
        return 0

    lax.fori_loop(0, NY // 8, along_x, 0)
    for step in range(NY // 8):
        for copy in writes(step):
            copy.wait()


VMEM = pl.BlockSpec(memory_space=pltpu.VMEM)
SMEM = pl.BlockSpec(memory_space=pltpu.SMEM)
FAR = pl.BlockSpec(memory_space=pltpu.HBM)
LIMIT = pltpu.CompilerParams(vmem_limit_bytes=12 * 1024 * 1024)
SMALL = pl.CostEstimate(flops=1000, bytes_accessed=1000, transcendentals=0)


def far(values):
    return pltpu.with_memory_space_constraint(values, pltpu.HBM)


def call(kernel, outs, scratch, *args, sources=None, far_outs=(), whole_numbers=()):
    shapes = [(o, 128) if isinstance(o, int) else o for o in outs]
    return pl.pallas_call(
        kernel,
        out_shape=[
            pltpu.HBM(s, F32) if n in far_outs else jax.ShapeDtypeStruct(s, jnp.int32 if n in whole_numbers else F32)
            for n, s in enumerate(shapes)
        ],
        in_specs=[SMEM] + (sources or [VMEM] * (len(args) - 1)),
        out_specs=[FAR if n in far_outs else VMEM for n in range(len(outs))],
        scratch_shapes=[pltpu.VMEM((s, 128), F32) if isinstance(s, int) else s for s in scratch],
        compiler_params=LIMIT,
        cost_estimate=SMALL,
    )(*args)


def local(state, fine_pairs, fine_count, coarse_pairs):
    mortons, octs = lax.axis_size("morton"), lax.axis_size("oct")
    place = jnp.stack([lax.axis_index("morton"), lax.axis_index("oct"), mortons, octs]).astype(jnp.int32)
    many = NX * PITCH

    def swap(values, pair):
        pairs = [(m, o) for m in range(mortons) for o in range(octs)]
        index = lambda place: place[0] * octs + place[1]
        return lax.ppermute(values, AXES, [(index(p), index(pair(*p))) for p in pairs])

    def other(i):
        return (i - 1 ^ 1) + 1

    block = pltpu.VMEM((5, ROWS, 128), F32)
    sent, x_one, x_two, y_one, y_two = call(
        moments_kernel, [128 * SENT, 480, 480, 240, 240],
        [block, 128 * SENT, 240, 240, pltpu.SemaphoreType.DMA((4,)), pltpu.SemaphoreType.DMA((2, 5)),
         pltpu.SemaphoreType.DMA((3,))],
        place, far(state.reshape(5, ROWS, 128)), sources=[FAR], far_outs=range(5),
    )
    got = lax.all_to_all(sent.reshape(mortons * octs, 1, SENT * 128), AXES[::-1], 0, 0, tiled=True)
    x_one = swap(x_one, lambda m, o: (m ^ 1, o))
    x_two = swap(x_two, lambda m, o: (other(m), o) if 0 < m < mortons - 1 else (m, o ^ 1))
    y_one = swap(y_one, lambda m, o: (m, o ^ 1))
    y_two = swap(y_two, lambda m, o: (m, other(o)) if 0 < o < octs - 1 else (m, octs - 1 - o))
    rows = state.reshape(5 * ROWS, 128)
    rows, sent = lax.optimization_barrier((rows, sent))
    by_z, padded, inverse_of, sound, uses_fine, uses_coarse = call(
        inner_kernel, [5 * ROWS, 5 * many, many, many, 40, 64],
        [5 * TALL, 5 * TALL, 640, 640, pltpu.VMEM((128, 32), jnp.int32), pltpu.VMEM((8, 16), jnp.int32),
         pltpu.VMEM((16, 32), jnp.int32), pltpu.SemaphoreType.DMA((3,))],
        place, rows, far(fine_pairs.reshape(128, 32)), far(fine_count.reshape(8, 16)), far(coarse_pairs.reshape(16, 32)),
        sources=[VMEM, FAR, FAR, FAR], whole_numbers=(4, 5),
    )
    (others,) = call(
        along_y_kernel, [5 * ROWS], [240, 240, 5 * many], place, padded, inverse_of, sound, y_one, y_two, by_z
    )
    return call(
        outer_kernel, [(5, NX, NY, NZ), (3, NX, NY, NZ)],
        [480, 480, 160, 72, pltpu.VMEM((5, NX, NY, NZ), F32), pltpu.VMEM((3, NX, NY, NZ), F32),
         pltpu.SemaphoreType.DMA((2, 4))],
        place, rows, x_one, x_two, others, uses_fine, uses_coarse, got.reshape(mortons * octs * SENT, 128),
        far_outs=range(2),
    )


def solution(mesh):
    in_specs = (
        P(None, "morton", "oct", None),
        P("morton", "oct", None, None),
        P("morton", "oct", None),
        P("morton", "oct", None, None),
    )
    out_specs = (P(None, "morton", "oct", None), P(None, "morton", "oct", None))
    return jax.shard_map(local, mesh=mesh, in_specs=in_specs, out_specs=out_specs, check_vma=False)
```

```python
import functools

import functools

import jax
import jax.numpy as jnp
from jax import lax
from jax.experimental import pallas as pl
from jax.experimental.pallas import tpu as pltpu
from jax.sharding import PartitionSpec as P

ADIABATIC = 5.0 / 3.0
COURANT = 0.2
GRAVITY = 1.0
AXES = ("morton", "oct")
F32 = jnp.float32
HIGH = lax.Precision.HIGHEST

NX, NY, NZ = 16, 32, 128
ROWS = NX * NY
PITCH = 33
TALL = 144
RIM = 17
SENT = 5
SYM = ((0, 0), (0, 1), (0, 2), (1, 1), (1, 2), (2, 2))


def iota(shape, dim):
    return lax.broadcasted_iota(jnp.int32, shape, dim)


def sym(i, j):
    return SYM.index((min(i, j), max(i, j)))


def reciprocal(x):
    return pl.reciprocal(x, approx=True)


def sound_of(q, inverse):
    kinetic = (q[1] * q[1] + q[2] * q[2] + q[3] * q[3]) * inverse
    pressure = (2.0 / 3.0) * q[4] - (1.0 / 3.0) * kinetic
    square = ADIABATIC * pressure * inverse
    return square * lax.rsqrt(square)


def fold_rows(values, group):
    keep = iota(values.shape, 1) // group == iota(values.shape, 0)
    return jnp.sum(jnp.where(keep, values, 0.0), axis=0, keepdims=True)


def moments_kernel(
    place, state, sent, x_one, x_two, y_one, y_two, rows, near_sent, near_one, near_two, arrived, taken, written
):
    part = ROWS // 4
    copies = [
        pltpu.make_async_copy(
            state.at[:, pl.ds(c * part, part), :], rows.at[:, pl.ds(c * part, part), :], arrived.at[c]
        )
        for c in range(4)
    ]
    even, oct_even = place[0] % 2 == 0, place[1] % 2 == 0
    x_starts = (jnp.where(even, 0, NX - 3), jnp.where(even, NX - 3, 0))
    y_starts = (jnp.where(oct_even, NY - 3, 0), jnp.where(oct_even, 0, NY - 3))
    edges = [
        pltpu.make_async_copy(
            rows.at[f, pl.ds(pl.multiple_of(start * NY, 32), 96), :], out.at[pl.ds(f * 96, 96), :], taken.at[n, f]
        )
        for n, (out, start) in enumerate(((x_one, x_starts[0]), (x_two, x_starts[1])))
        for f in range(5)
    ]
    for copy in copies:
        copy.start()
    offset_y = iota((8, 128), 0).astype(F32) - 3.5
    fastest = jnp.zeros((8, 128), F32)
    sums, sums_x, sums_y = [], [], []
    for tx in range(2):
        totals, totals_x = [jnp.zeros((8, 128), F32)] * 4, [jnp.zeros((8, 128), F32)] * 4
        for half in range(2):
            copies[tx * 2 + half].wait()
            for x in range(half * 4, half * 4 + 4):
                for ty in range(4):
                    row = (tx * 8 + x) * NY + ty * 8
                    q = [rows[f, row : row + 8, :] for f in range(5)]
                    inverse = reciprocal(q[0])
                    speed_of_sound = sound_of(q, inverse)
                    largest = jnp.maximum(jnp.maximum(jnp.abs(q[1]), jnp.abs(q[2])), jnp.abs(q[3]))
                    fastest = jnp.maximum(fastest, largest * inverse + speed_of_sound)
                    totals[ty] = totals[ty] + q[0]
                    totals_x[ty] = totals_x[ty] + q[0] * (x - 3.5)
        for ty in range(4):
            sums.append(jnp.sum(totals[ty], axis=0, keepdims=True))
            sums_x.append(jnp.sum(totals_x[ty], axis=0, keepdims=True))
            sums_y.append(jnp.sum(totals[ty] * offset_y, axis=0, keepdims=True))
    for copy in edges:
        copy.start()
    for out, start in ((near_one, y_starts[0]), (near_two, y_starts[1])):
        for f in range(5):
            for x in range(NX):
                row = (f * NX + x) * 3
                out[row : row + 3, :] = rows[f, pl.ds(x * NY + start, 3), :]
    writes = [
        pltpu.make_async_copy(near, out, written.at[n])
        for n, (near, out) in enumerate(((near_one, y_one), (near_two, y_two), (near_sent, sent)))
    ]
    writes[0].start()
    writes[1].start()
    lines = jnp.concatenate(sums + sums_x + sums_y, axis=0)
    z = iota((128, 128), 0)
    pick = (z // 8 == iota((128, 128), 1) % 16).astype(F32)
    by_z = pick * ((z % 8).astype(F32) - 3.5)
    folded = jnp.dot(lines, pick, precision=HIGH, preferred_element_type=F32)
    folded_z = jnp.dot(lines[0:8], by_z, precision=HIGH, preferred_element_type=F32)
    mass = fold_rows(folded[0:8], 16)
    dipole = [fold_rows(folded[8:16], 16), fold_rows(folded[16:24], 16), fold_rows(folded_z, 16)]

    lane = iota((1, 128), 1)
    odd = [lane // 64, lane // 16 % 2, lane % 2]
    shifted = [d + 4.0 * (2 * o - 1).astype(F32) * mass for d, o in zip(dipole, odd, strict=True)]
    t = iota((128, 128), 0)
    parent = t // 32 % 2 * 8 + t % 16 // 2
    pick = (parent == iota((128, 128), 1) % 16).astype(F32)
    families = jnp.concatenate([mass] + shifted + [jnp.zeros((4, 128), F32)], axis=0)
    families = jnp.dot(families, pick, precision=HIGH, preferred_element_type=F32)
    last = jnp.where(lane < 64, fold_rows(families, 16), jnp.max(fastest))
    five = jnp.concatenate([mass] + dipole + [last], axis=0)
    many = jnp.concatenate([five] * 8, axis=0)
    for copy in range(16):
        near_sent[copy * 40 : copy * 40 + 40, :] = many
    writes[2].start()
    for copy in edges + writes:
        copy.wait()


def rise(before, here, after):
    value = 0.5 * here + (1.0 / 12.0) * (before - after)
    return jnp.minimum(jnp.maximum(value, jnp.minimum(here, 0.0)), jnp.maximum(here, 0.0))


def upper_and_lower(centre, up, down):
    most_up, most_down = jnp.abs(down + down), jnp.abs(up + up)
    upper = centre + jnp.minimum(jnp.maximum(up, -most_up), most_up)
    lower = centre + jnp.minimum(jnp.maximum(down, -most_down), most_down)
    return upper, lower


def flux_of(q, k):
    inverse = reciprocal(q[0])
    velocity = q[1 + k] * inverse
    kinetic = (q[1] * q[1] + q[2] * q[2] + q[3] * q[3]) * inverse
    pressure = (2.0 / 3.0) * q[4] - (1.0 / 3.0) * kinetic
    out = [q[1 + k]] + [q[1 + c] * velocity for c in range(3)] + [(q[4] + pressure) * velocity]
    out[1 + k] = out[1 + k] + pressure
    return out


def twice_flux(left, right, speed, k):
    from_left, from_right = flux_of(left, k), flux_of(right, k)
    return [
        (a + b) - speed * (r - l) for a, b, l, r in zip(from_left, from_right, left, right, strict=True)
    ]


def sweep(load, speed_at, store, begin, end, k, beside=()):
    beside = list(beside)
    share = -(-len(beside) // (end - begin))
    start = [[load(f, begin + i) for f in range(5)] for i in (-3, -2, -1)]
    steps = [[b - a for a, b in zip(start[i], start[i + 1], strict=True)] for i in range(2)]
    cell = start[1], start[2]
    ups = upper_old = speed_old = flux_old = None
    for i in range(begin - 2, end + 1):
        ahead = [load(f, i + 2) for f in range(5)]
        steps.append([a - b for a, b in zip(ahead, cell[1], strict=True)])
        now = [rise(*each) for each in zip(*steps, strict=True)]
        if ups is not None:
            downs = [u - d for u, d in zip(ups, steps[0], strict=True)]
            pairs = [upper_and_lower(*each) for each in zip(cell[0], now, downs, strict=True)]
            upper, lower = [p[0] for p in pairs], [p[1] for p in pairs]
            speed = speed_at(i, cell[0])
            if upper_old is not None:
                flux = twice_flux(upper_old, lower, jnp.maximum(speed_old, speed), k)
                if flux_old is not None:
                    store(i - 1, [a - b for a, b in zip(flux, flux_old, strict=True)])
                flux_old = flux
            upper_old, speed_old = upper, speed
        for call in beside[:share]:
            call()
        beside = beside[share:]
        ups, cell, steps = now, (cell[1], ahead), steps[1:]
    for call in beside:
        call()


def sides(one, two, low, high, rank):
    even = rank % 2 == 0
    for row in range(0, one.shape[0], 8):
        a, b = one[row : row + 8, :], two[row : row + 8, :]
        low[row : row + 8, :] = jnp.where(even, b, a)
        high[row : row + 8, :] = jnp.where(even, a, b)


def inner_kernel(
    place, state, far_pairs, far_count, far_coarse, out, fine_uses, coarse_uses,
    turned_even, turned_odd, changes_even, changes_odd, padded, inverse_of, sound, by_y,
    fine_pairs, fine_count, coarse_pairs, arrived,
):
    turned, changes = (turned_even, turned_odd), (changes_even, changes_odd)

    def turn(block, f):
        into, base = turned[block % 2], f * TALL
        flat = state[f * ROWS + block * 128 : f * ROWS + block * 128 + 128, :].T
        into[base + 8 : base + 136, :] = flat
        into[base : base + 8, :] = jnp.broadcast_to(flat[0:1], (8, 128))
        into[base + 136 : base + 144, :] = jnp.broadcast_to(flat[127:128], (8, 128))

    def turn_back(block, f):
        flat = changes[block % 2][f * 128 : f * 128 + 128, :]
        out[f * ROWS + block * 128 : f * ROWS + block * 128 + 128, :] = flat.T

    def along_z(block, beside):
        source, into = turned[block % 2], changes[block % 2]

        def load(f, i):
            return source[pl.ds(f * TALL + 8 + i, 8, stride=16), :]

        def speed_at(i, q):
            inverse = reciprocal(q[0])
            return jnp.abs(q[3]) * inverse + sound_of(q, inverse)

        def store(i, values):
            for f in range(5):
                into[pl.ds(f * 128 + i, 8, stride=16), :] = values[f]

        sweep(load, speed_at, store, 0, 16, 2, beside)

    reads = [
        pltpu.make_async_copy(source, into, arrived.at[n])
        for n, (source, into) in enumerate(
            ((far_pairs, fine_pairs), (far_count, fine_count), (far_coarse, coarse_pairs))
        )
    ]
    for copy in reads:
        copy.start()
    for f in range(5):
        turn(0, f)
    for block in range(4):
        beside = []
        for f in range(5):
            if block < 3:
                beside.append(functools.partial(turn, block + 1, f))
            if block > 0:
                beside.append(functools.partial(turn_back, block - 1, f))
        along_z(block, beside)
    for f in range(5):
        turn_back(3, f)
    for copy in reads:
        copy.wait()
    codes = jnp.concatenate([fine_pairs[...].astype(F32)] * 4, axis=1).T[0:32]
    spread = (iota((16, 128), 1) % 16 == iota((16, 128), 0)).astype(F32)
    used = fold_rows(
        jnp.dot(fine_count[...].astype(F32), spread, precision=HIGH, preferred_element_type=F32), 16
    )
    codes = jnp.where(iota((32, 128), 0).astype(F32) < used, codes, 1000.0)
    along = jnp.floor((codes + 0.5) * 0.04)
    plane = codes - 25.0 * along
    group = jnp.floor((plane + 0.5) * 0.2)
    one = jnp.left_shift(1, (6.0 * (plane - 5.0 * group)).astype(jnp.int32))
    ones = [jnp.where(group == g, one, 0) for g in range(5)]
    for g in range(5):
        lines = []
        for ox in range(5):
            hits = jnp.where(along == ox, ones[g], 0)
            hits = (hits[0:8] + hits[8:16]) + (hits[16:24] + hits[24:32])
            lines.append(jnp.sum(hits, axis=0, keepdims=True))
        fine_uses[g * 8 : g * 8 + 8, :] = jnp.concatenate(lines + [jnp.zeros((3, 128), jnp.int32)], axis=0)

    slot = iota((8, 128), 1)
    device = slot % place[2] * place[3] + slot // place[2]
    for half in range(2):
        named = coarse_pairs[half * 8 : half * 8 + 8, :]
        coded = named // 16 + named % 4 * (6 * 256) + named // 4 % 4 * 65536
        counts = [jnp.zeros((8, 128), jnp.int32) for _ in range(4)]
        for j in range(32):
            code = jnp.broadcast_to(coded[:, j : j + 1], (8, 128))
            one = jnp.where((code & 255) == device, jnp.left_shift(1, (code >> 8) & 255), 0)
            group = code >> 16
            counts = [each + jnp.where(group == g, one, 0) for g, each in enumerate(counts)]
        for g in range(4):
            coarse_uses[(g * 2 + half) * 8 : (g * 2 + half) * 8 + 8, :] = counts[g]
    for x in range(NX):
        for y in range(0, NY, 8):
            row = x * NY + y
            q = [state[f * ROWS + row : f * ROWS + row + 8, :] for f in range(5)]
            inverse = reciprocal(q[0])
            at = x * PITCH + y
            for f in range(5):
                padded[f * NX * PITCH + at : f * NX * PITCH + at + 8, :] = q[f]
            inverse_of[at : at + 8, :] = inverse
            sound[at : at + 8, :] = sound_of(q, inverse)

    def along_x(step, _):
        start = pl.multiple_of(step * 8, 8)

        def rows(f, i):
            return pl.ds(pl.multiple_of(f * ROWS + i * NY + start, 8), 8)

        def speed_at(i, q):
            at = pl.ds(i * PITCH + start, 8)
            return jnp.abs(q[1]) * inverse_of[at, :] + sound[at, :]

        def store(i, values):
            for f in range(5):
                out[rows(f, i), :] = out[rows(f, i), :] + values[f]

        sweep(lambda f, i: state[rows(f, i), :], speed_at, store, 3, NX - 3, 0)
        return 0

    lax.fori_loop(0, NY // 8, along_x, 0)

    def along_y(step, _):
        start = pl.multiple_of(step * 8, 8)

        def rows(f, i):
            return pl.ds((f * NX + start) * PITCH + i, 8, stride=PITCH)

        def speed_at(i, q):
            return jnp.abs(q[2]) * inverse_of[rows(0, i), :] + sound[rows(0, i), :]

        def store(i, values):
            for f in range(5):
                by_y[rows(f, i), :] = values[f]

        for i in (0, 1, 2, NY - 3, NY - 2, NY - 1):
            store(i, [jnp.zeros((8, 128), F32)] * 5)
        sweep(lambda f, i: padded[rows(f, i), :], speed_at, store, 3, NY - 3, 1)
        return 0

    lax.fori_loop(0, NX // 8, along_y, 0)

    def total(x, _):
        for f in range(5):
            for y in range(0, NY, 8):
                row = pl.ds(pl.multiple_of(f * ROWS + x * NY + y, 8), 8)
                out[row, :] = out[row, :] + by_y[pl.ds((f * NX + x) * PITCH + y, 8), :]
        return 0

    lax.fori_loop(0, NX, total, 0, unroll=2)


def tensors(r, square):
    root = lax.rsqrt(jnp.maximum(square, 1.0))
    cube = root * root * root
    three = 3.0 * cube * (root * root)
    scaled = [three * each for each in r]
    pull = [each * cube for each in r]
    tide = [scaled[i] * r[j] - cube if i == j else scaled[i] * r[j] for i, j in SYM]
    return pull, tide


def add_terms(totals, uses, r, square, mass, dipole):
    pull, tide = tensors(r, square)
    mass = uses * mass
    dipole = [uses * d for d in dipole]
    for i in range(3):
        term = mass * pull[i]
        for j in range(3):
            term = term - tide[sym(i, j)] * dipole[j]
        totals[i] = totals[i] + term
    for e in range(6):
        totals[3 + e] = totals[3 + e] + mass * tide[e]


def far_fields(place, uses_fine, uses_coarse, got, around):
    morton, octant = place[0], place[1]
    mortons, octs = place[2], place[3]
    lane = iota((8, 128), 1)
    lane_row = iota((1, 128), 1)

    rows = jnp.concatenate([got[pl.ds(g * 8 * SENT + 4, 8, stride=SENT), :] for g in range(16)], axis=0)
    time_step = COURANT / jnp.max(rows[:, 64:128])
    moments = rows.T
    target_z = iota((8, 128), 0)
    rx = 16.0 * (lane % mortons - morton).astype(F32)
    coarse = []
    for half in range(2):
        totals = [jnp.zeros((8, 128), F32) for _ in range(9)]
        for lp in range(16):
            ry = 16.0 * (lane // mortons * 2 + lp // 8 - (2 * octant + half)).astype(F32)
            rz = 16.0 * (lp % 8 - target_z).astype(F32)
            own = [jnp.broadcast_to(moments[m * 16 + lp : m * 16 + lp + 1], (8, 128)) for m in range(4)]
            row = (lp // 4 * 2 + half) * 8
            uses = ((uses_coarse[row : row + 8, :] >> (lp % 4 * 6)) & 63).astype(F32)
            add_terms(totals, uses, (rx, ry, rz), rx * rx + ry * ry + rz * rz, own[0], own[1:])
        coarse.append([jnp.sum(each, axis=1, keepdims=True) for each in totals])
    result = []
    for e in range(9):
        column = jnp.where(lane // 32 % 2 == 0, coarse[0][e], coarse[1][e])
        column = jnp.where(lane % 16 // 2 == iota((8, 128), 0), column, 0.0)
        result.append(jnp.sum(column, axis=0, keepdims=True))
    side = [4.0 * (2 * s - 1).astype(F32) for s in (lane_row // 64, lane_row // 16 % 2, lane_row % 2)]
    for i in range(3):
        for j in range(3):
            result[i] = result[i] + result[3 + sym(i, j)] * side[j]

    blocks = []
    for dy in (-1, 0, 1):
        block = []
        for dx in (-1, 0, 1):
            at_x, at_y = morton + dx, octant + dy
            inside = (at_x >= 0) & (at_x < mortons) & (at_y >= 0) & (at_y < octs)
            device = jnp.clip(at_y, 0, octs - 1) * mortons + jnp.clip(at_x, 0, mortons - 1)
            for m in range(4):
                block.append(jnp.where(inside, got[pl.ds(device * SENT + m, 1), :], 0.0))
        blocks.append(jnp.concatenate(block + [jnp.zeros((4, 128), F32)], axis=0))
    wide = iota((16, 128), 1)
    around[...] = jnp.zeros(around.shape, F32)
    for oy in range(-2, 3):
        if oy == 0:
            moved = blocks[1]
        else:
            moved = pltpu.roll(blocks[1], (-16 * oy) % 128, 1)
            if oy > 0:
                moved = jnp.where(wide // 16 % 4 + oy > 3, pltpu.roll(blocks[2], (64 - 16 * oy) % 128, 1), moved)
            else:
                moved = jnp.where(wide // 16 % 4 + oy < 0, pltpu.roll(blocks[0], (-64 - 16 * oy) % 128, 1), moved)
        swapped = pltpu.roll(moved, 64, 1)
        for m in range(4):
            low, own, high = [(moved[d * 4 + m : d * 4 + m + 1], swapped[d * 4 + m : d * 4 + m + 1]) for d in range(3)]
            first = lane_row < 64
            lines = [
                low[0], jnp.where(first, low[1], own[1]), own[0], jnp.where(first, own[1], high[1]), high[0],
            ]
            row = (m * 5 + oy + 2) * 8
            around[row : row + 5, :] = jnp.concatenate(lines, axis=0)
    totals = [jnp.zeros((8, 128), F32) for _ in range(9)]
    rx = 8.0 * (iota((8, 128), 0) - 2).astype(F32)
    square_x = rx * rx
    for oy in range(-2, 3):
        base = [around[(m * 5 + oy + 2) * 8 : (m * 5 + oy + 2) * 8 + 8, :] for m in range(4)]
        for oz in range(-2, 3):
            moved = base
            if oz:
                ok = (lane % 16 + oz >= 0) & (lane % 16 + oz < 16)
                moved = [jnp.where(ok, pltpu.roll(each, (-oz) % 128, 1), 0.0) for each in base]
            uses = ((uses_fine[(oy + 2) * 8 : (oy + 2) * 8 + 8, :] >> ((oz + 2) * 6)) & 63).astype(F32)
            add_terms(
                totals, uses, (rx, 8.0 * oy, 8.0 * oz),
                square_x + (64.0 * oy * oy + 64.0 * oz * oz), moved[0], moved[1:],
            )
    for e in range(9):
        result[e] = GRAVITY * (result[e] + jnp.sum(totals[e], axis=0, keepdims=True))
    return result, time_step


def outer_kernel(
    place, state, inner, x_one, x_two, far_y_one, far_y_two, uses_fine, uses_coarse, got, new, gravity,
    y_one, y_two, x_low, x_high, y_low, y_high, rims, by_x, by_y, around, field, made, pulls, arrived, written,
):
    reads = [
        pltpu.make_async_copy(far_y_one, y_one, arrived.at[0]),
        pltpu.make_async_copy(far_y_two, y_two, arrived.at[1]),
    ]
    for copy in reads:
        copy.start()
    sides(x_two, x_one, x_low, x_high, place[0])

    def x_edge(beyond, x):
        for f in range(5):
            cells = state[f * ROWS + x * NY : f * ROWS + x * NY + NY, :]
            for layer in range(3):
                beyond[(f * 3 + layer) * NY : (f * 3 + layer) * NY + NY, :] = cells

    pl.when(place[0] == 0)(lambda: x_edge(x_low, 0))
    pl.when(place[0] == place[2] - 1)(lambda: x_edge(x_high, NX - 1))

    def speed_of(k):
        def speed_at(i, q):
            inverse = reciprocal(q[0])
            return jnp.abs(q[1 + k]) * inverse + sound_of(q, inverse)

        return speed_at

    def along_x(step, _):
        start = pl.multiple_of(step * 8, 8)

        def load(f, i):
            if i < 0:
                return x_low[pl.ds(pl.multiple_of((f * 3 + i + 3) * NY + start, 8), 8), :]
            if i >= NX:
                return x_high[pl.ds(pl.multiple_of((f * 3 + i - NX) * NY + start, 8), 8), :]
            return state[pl.ds(pl.multiple_of(f * ROWS + i * NY + start, 8), 8), :]

        def store(i, values):
            for f in range(5):
                by_x[pl.ds(pl.multiple_of((f * 6 + (i if i < 3 else i - 10)) * NY + start, 8), 8), :] = values[f]

        sweep(load, speed_of(0), store, 0, 3, 0)
        sweep(load, speed_of(0), store, NX - 3, NX, 0)
        return 0

    lax.fori_loop(0, NY // 8, along_x, 0)

    for f in range(5):
        for x in range(NX):
            for side, y in ((0, 0), (8, NY - 8)):
                row = (f * NX + x) * RIM + side
                rims[row : row + 8, :] = state[f * ROWS + x * NY + y : f * ROWS + x * NY + y + 8, :]
                by_y[row : row + 8, :] = jnp.zeros((8, 128), F32)
    for copy in reads:
        copy.wait()
    sides(y_one, y_two, y_low, y_high, place[1])

    def y_edge(beyond, row):
        for f in range(5):
            cells = rims[pl.ds(f * NX * RIM + row, NX, stride=RIM), :]
            for layer in range(3):
                beyond[pl.ds(f * NX * 3 + layer, NX, stride=3), :] = cells

    pl.when(place[1] == 0)(lambda: y_edge(y_low, 0))
    pl.when(place[1] == place[3] - 1)(lambda: y_edge(y_high, 15))

    def along_y(step, _):
        start = pl.multiple_of(step * 8, 8)

        def rows(f, i):
            return pl.ds((f * NX + start) * RIM + (i if i < 8 else i - 16), 8, stride=RIM)

        def load(f, i):
            if i < 0:
                return y_low[pl.ds((f * NX + start) * 3 + i + 3, 8, stride=3), :]
            if i >= NY:
                return y_high[pl.ds((f * NX + start) * 3 + i - NY, 8, stride=3), :]
            return rims[rows(f, i), :]

        def store(i, values):
            for f in range(5):
                by_y[rows(f, i), :] = values[f]

        sweep(load, speed_of(1), store, 0, 3, 1)
        sweep(load, speed_of(1), store, NY - 3, NY, 1)
        return 0

    lax.fori_loop(0, NX // 8, along_y, 0)

    result, time_step = far_fields(place, uses_fine, uses_coarse, got, around)
    half_step = 0.5 * time_step
    keep = iota((8, 128), 1) // 16 == iota((8, 128), 0)
    spread = (iota((128, 128), 0) % 16 == iota((128, 128), 1) // 8).astype(F32)
    lines = jnp.concatenate([jnp.where(keep, each, 0.0) for each in result], axis=0)
    lines = jnp.dot(lines, spread, precision=HIGH, preferred_element_type=F32)
    lines = [lines[e * 8 : e * 8 + 8] for e in range(9)]
    offset_z = (iota((8, 128), 1) % 8).astype(F32) - 3.5
    for i in range(3):
        field[i * 8 : i * 8 + 8, :] = lines[i] + lines[3 + sym(i, 2)] * offset_z
        field[(3 + i) * 8 : (3 + i) * 8 + 8, :] = lines[3 + sym(i, 0)]
        field[(6 + i) * 8 : (6 + i) * 8 + 8, :] = lines[3 + sym(i, 1)]
    offset_y = iota((8, 128), 0).astype(F32) - 3.5

    def writes(part):
        rows = pl.ds(part * 4, 4)
        return [
            pltpu.make_async_copy(made.at[:, rows, :, :], new.at[:, rows, :, :], written.at[0, part]),
            pltpu.make_async_copy(pulls.at[:, rows, :, :], gravity.at[:, rows, :, :], written.at[1, part]),
        ]

    lines = {}
    for x in range(NX):
        for ty in range(4):
            tx, y = x // 8, ty * 8
            if x % 8 == 0:
                at = [field[e * 8 + tx * 4 + ty : e * 8 + tx * 4 + ty + 1, :] for e in range(9)]
                lines[ty] = ([at[e] + at[6 + e] * offset_y for e in range(3)], at[3:6])
            base, slope = lines[ty]
            q = [state[f * ROWS + x * NY + y : f * ROWS + x * NY + y + 8, :] for f in range(5)]
            pull = [base[e] + slope[e] * (x % 8 - 3.5) for e in range(3)]
            moved = []
            for f in range(5):
                total = inner[f * ROWS + x * NY + y : f * ROWS + x * NY + y + 8, :]
                if x < 3 or x >= NX - 3:
                    row = (f * 6 + (x if x < 3 else x - 10)) * NY + y
                    total = total + by_x[row : row + 8, :]
                if ty in (0, 3):
                    row = (f * NX + x) * RIM + (0 if ty == 0 else 8)
                    total = total + by_y[row : row + 8, :]
                moved.append(q[f] - half_step * total)
            weight = time_step * q[0]
            gain = q[1] * pull[0] + q[2] * pull[1] + q[3] * pull[2]
            made[0, x, y : y + 8, :] = moved[0]
            for e in range(3):
                pulls[e, x, y : y + 8, :] = pull[e]
                made[1 + e, x, y : y + 8, :] = moved[1 + e] + weight * pull[e]
            made[4, x, y : y + 8, :] = moved[4] + time_step * gain
        if x % 4 == 3:
            for copy in writes(x // 4):
                copy.start()
    for part in range(4):
        for copy in writes(part):
            copy.wait()


VMEM = pl.BlockSpec(memory_space=pltpu.VMEM)
SMEM = pl.BlockSpec(memory_space=pltpu.SMEM)
FAR = pl.BlockSpec(memory_space=pltpu.HBM)
LIMIT = pltpu.CompilerParams(vmem_limit_bytes=12 * 1024 * 1024)
SMALL = pl.CostEstimate(flops=1000, bytes_accessed=1000, transcendentals=0)


def far(values):
    return pltpu.with_memory_space_constraint(values, pltpu.HBM)


def call(kernel, outs, scratch, *args, sources=None, far_outs=(), whole_numbers=()):
    shapes = [(o, 128) if isinstance(o, int) else o for o in outs]
    return pl.pallas_call(
        kernel,
        out_shape=[
            pltpu.HBM(s, F32) if n in far_outs else jax.ShapeDtypeStruct(s, jnp.int32 if n in whole_numbers else F32)
            for n, s in enumerate(shapes)
        ],
        in_specs=[SMEM] + (sources or [VMEM] * (len(args) - 1)),
        out_specs=[FAR if n in far_outs else VMEM for n in range(len(outs))],
        scratch_shapes=[pltpu.VMEM((s, 128), F32) if isinstance(s, int) else s for s in scratch],
        compiler_params=LIMIT,
        cost_estimate=SMALL,
    )(*args)


def local(state, fine_pairs, fine_count, coarse_pairs):
    mortons, octs = lax.axis_size("morton"), lax.axis_size("oct")
    place = jnp.stack([lax.axis_index("morton"), lax.axis_index("oct"), mortons, octs]).astype(jnp.int32)
    many = NX * PITCH

    def swap(values, pair):
        pairs = [(m, o) for m in range(mortons) for o in range(octs)]
        index = lambda place: place[0] * octs + place[1]
        return lax.ppermute(values, AXES, [(index(p), index(pair(*p))) for p in pairs])

    def other(i):
        return (i - 1 ^ 1) + 1

    block = pltpu.VMEM((5, ROWS, 128), F32)
    sent, x_one, x_two, y_one, y_two = call(
        moments_kernel, [128 * SENT, 480, 480, 240, 240],
        [block, 128 * SENT, 240, 240, pltpu.SemaphoreType.DMA((4,)), pltpu.SemaphoreType.DMA((2, 5)),
         pltpu.SemaphoreType.DMA((3,))],
        place, far(state.reshape(5, ROWS, 128)), sources=[FAR], far_outs=range(5),
    )
    got = lax.all_to_all(sent.reshape(mortons * octs, 1, SENT * 128), AXES[::-1], 0, 0, tiled=True)
    x_one = swap(x_one, lambda m, o: (other(m), o) if 0 < m < mortons - 1 else (m, o ^ 1))
    x_two = swap(x_two, lambda m, o: (m ^ 1, o))
    y_one = swap(y_one, lambda m, o: (m, o ^ 1))
    y_two = swap(y_two, lambda m, o: (m, other(o)) if 0 < o < octs - 1 else (m, octs - 1 - o))
    rows = state.reshape(5 * ROWS, 128)
    rows, sent = lax.optimization_barrier((rows, sent))
    inner, uses_fine, uses_coarse = call(
        inner_kernel, [5 * ROWS, 40, 64],
        [5 * TALL, 5 * TALL, 640, 640, 5 * many, many, many, 5 * many, pltpu.VMEM((128, 32), jnp.int32),
         pltpu.VMEM((8, 16), jnp.int32), pltpu.VMEM((16, 32), jnp.int32), pltpu.SemaphoreType.DMA((3,))],
        place, rows, far(fine_pairs.reshape(128, 32)), far(fine_count.reshape(8, 16)), far(coarse_pairs.reshape(16, 32)),
        sources=[VMEM, FAR, FAR, FAR], whole_numbers=(1, 2),
    )
    rim = 5 * NX * RIM
    return call(
        outer_kernel, [(5, NX, NY, NZ), (3, NX, NY, NZ)],
        [240, 240, 480, 480, 240, 240, rim, 960, rim, 160, 72, pltpu.VMEM((5, NX, NY, NZ), F32),
         pltpu.VMEM((3, NX, NY, NZ), F32), pltpu.SemaphoreType.DMA((2,)), pltpu.SemaphoreType.DMA((2, 4))],
        place, rows, inner, x_one, x_two, far(y_one), far(y_two), uses_fine, uses_coarse,
        got.reshape(mortons * octs * SENT, 128),
        sources=[VMEM] * 4 + [FAR] * 2 + [VMEM] * 3, far_outs=range(2),
    )


def solution(mesh):
    in_specs = (
        P(None, "morton", "oct", None),
        P("morton", "oct", None, None),
        P("morton", "oct", None),
        P("morton", "oct", None, None),
    )
    out_specs = (P(None, "morton", "oct", None), P(None, "morton", "oct", None))
    return jax.shard_map(local, mesh=mesh, in_specs=in_specs, out_specs=out_specs, check_vma=False)
```

```python
import functools

import functools

import jax
import jax.numpy as jnp
from jax import lax
from jax.experimental import pallas as pl
from jax.experimental.pallas import tpu as pltpu
from jax.sharding import PartitionSpec as P

ADIABATIC = 5.0 / 3.0
COURANT = 0.2
GRAVITY = 1.0
AXES = ("morton", "oct")
F32 = jnp.float32
HIGH = lax.Precision.HIGHEST

NX, NY, NZ = 16, 32, 128
ROWS = NX * NY
PITCH = 33
TALL = 144
LONG = 488
RIM = 17
SENT = 3
SYM = ((0, 0), (0, 1), (0, 2), (1, 1), (1, 2), (2, 2))


def iota(shape, dim):
    return lax.broadcasted_iota(jnp.int32, shape, dim)


def sym(i, j):
    return SYM.index((min(i, j), max(i, j)))


def reciprocal(x):
    return pl.reciprocal(x, approx=True)


def sound_of(q, inverse):
    kinetic = (q[1] * q[1] + q[2] * q[2] + q[3] * q[3]) * inverse
    pressure = (2.0 / 3.0) * q[4] - (1.0 / 3.0) * kinetic
    square = ADIABATIC * pressure * inverse
    return square * lax.rsqrt(square)


def fold_rows(values, group):
    keep = iota(values.shape, 1) // group == iota(values.shape, 0)
    return jnp.sum(jnp.where(keep, values, 0.0), axis=0, keepdims=True)


def moments_kernel(
    place, state, sent, x_one, x_two, y_one, y_two, own, rows, near_sent, near_one, near_two, arrived, taken, written
):
    part = ROWS // 4
    copies = [
        pltpu.make_async_copy(
            state.at[:, pl.ds(c * part, part), :], rows.at[:, pl.ds(c * part, part), :], arrived.at[c]
        )
        for c in range(4)
    ]
    even, oct_even = place[0] % 2 == 0, place[1] % 2 == 0
    x_starts = (jnp.where(even, 0, NX - 3), jnp.where(even, NX - 3, 0))
    y_starts = (jnp.where(oct_even, NY - 3, 0), jnp.where(oct_even, 0, NY - 3))
    edges = [
        pltpu.make_async_copy(
            rows.at[f, pl.ds(pl.multiple_of(start * NY, 32), 96), :], out.at[pl.ds(f * 96, 96), :], taken.at[n, f]
        )
        for n, (out, start) in enumerate(((x_one, x_starts[0]), (x_two, x_starts[1])))
        for f in range(5)
    ]
    for copy in copies:
        copy.start()
    offset_y = iota((8, 128), 0).astype(F32) - 3.5
    fastest = jnp.zeros((8, 128), F32)
    sums, sums_x, sums_y = [], [], []
    for tx in range(2):
        totals, totals_x = [jnp.zeros((8, 128), F32)] * 4, [jnp.zeros((8, 128), F32)] * 4
        for half in range(2):
            copies[tx * 2 + half].wait()
            for x in range(half * 4, half * 4 + 4):
                for ty in range(4):
                    row = (tx * 8 + x) * NY + ty * 8
                    q = [rows[f, row : row + 8, :] for f in range(5)]
                    inverse = reciprocal(q[0])
                    speed_of_sound = sound_of(q, inverse)
                    largest = jnp.maximum(jnp.maximum(jnp.abs(q[1]), jnp.abs(q[2])), jnp.abs(q[3]))
                    fastest = jnp.maximum(fastest, largest * inverse + speed_of_sound)
                    totals[ty] = totals[ty] + q[0]
                    totals_x[ty] = totals_x[ty] + q[0] * (x - 3.5)
        for ty in range(4):
            sums.append(jnp.sum(totals[ty], axis=0, keepdims=True))
            sums_x.append(jnp.sum(totals_x[ty], axis=0, keepdims=True))
            sums_y.append(jnp.sum(totals[ty] * offset_y, axis=0, keepdims=True))
    for copy in edges:
        copy.start()
    for out, start in ((near_one, y_starts[0]), (near_two, y_starts[1])):
        for f in range(5):
            for x in range(NX):
                row = (f * NX + x) * 3
                out[row : row + 3, :] = rows[f, pl.ds(x * NY + start, 3), :]
    writes = [
        pltpu.make_async_copy(near, out, written.at[n])
        for n, (near, out) in enumerate(((near_one, y_one), (near_two, y_two), (near_sent, sent)))
    ]
    writes[0].start()
    writes[1].start()
    lines = jnp.concatenate(sums + sums_x + sums_y, axis=0)
    z = iota((128, 128), 0)
    pick = (z // 8 == iota((128, 128), 1) % 16).astype(F32)
    by_z = pick * ((z % 8).astype(F32) - 3.5)
    folded = jnp.dot(lines, pick, precision=HIGH, preferred_element_type=F32)
    folded_z = jnp.dot(lines[0:8], by_z, precision=HIGH, preferred_element_type=F32)
    mass = fold_rows(folded[0:8], 16)
    dipole = [fold_rows(folded[8:16], 16), fold_rows(folded[16:24], 16), fold_rows(folded_z, 16)]

    lane = iota((1, 128), 1)
    odd = [lane // 64, lane // 16 % 2, lane % 2]
    shifted = [d + 4.0 * (2 * o - 1).astype(F32) * mass for d, o in zip(dipole, odd, strict=True)]
    t = iota((128, 128), 0)
    parent = t // 32 % 2 * 8 + t % 16 // 2
    pick = (parent == iota((128, 128), 1) % 16).astype(F32)
    families = jnp.concatenate([mass] + shifted + [jnp.zeros((4, 128), F32)], axis=0)
    families = jnp.dot(families, pick, precision=HIGH, preferred_element_type=F32)
    last = jnp.where(lane < 64, fold_rows(families, 16), jnp.max(fastest))
    own[...] = jnp.concatenate([mass] + dipole + [jnp.zeros((4, 128), F32)], axis=0)
    extra = [
        pltpu.make_async_copy(own, out.at[pl.ds(480, 8), :], taken.at[n, 5]) for n, out in enumerate((x_one, x_two))
    ]
    for copy in extra:
        copy.start()
    patterns = []
    for side in range(2):
        packed = [
            jnp.where(lane < 32, pltpu.roll(v, (-32 * side) % 128, 1), pltpu.roll(v, (-32 - 32 * side) % 128, 1))
            for v in [mass] + dipole
        ]
        pairs = [jnp.where(lane < 64, packed[m], pltpu.roll(packed[m + 1], 64, 1)) for m in (0, 2)]
        patterns.append(jnp.concatenate([last] + pairs, axis=0))
    patterns = [jnp.concatenate([p] * 8, axis=0) for p in patterns]
    for octant in range(4):
        chosen = jnp.where(octant > place[1], patterns[1], patterns[0])
        for part in range(4):
            row = octant * 96 + part * 24
            near_sent[row : row + 24, :] = chosen
    writes[2].start()
    for copy in edges + extra + writes:
        copy.wait()


def rise(before, here, after):
    value = 0.5 * here + (1.0 / 12.0) * (before - after)
    return jnp.minimum(jnp.maximum(value, jnp.minimum(here, 0.0)), jnp.maximum(here, 0.0))


def upper_and_lower(centre, up, down):
    most_up, most_down = jnp.abs(down + down), jnp.abs(up + up)
    upper = centre + jnp.minimum(jnp.maximum(up, -most_up), most_up)
    lower = centre + jnp.minimum(jnp.maximum(down, -most_down), most_down)
    return upper, lower


def flux_of(q, k):
    inverse = reciprocal(q[0])
    velocity = q[1 + k] * inverse
    kinetic = (q[1] * q[1] + q[2] * q[2] + q[3] * q[3]) * inverse
    pressure = (2.0 / 3.0) * q[4] - (1.0 / 3.0) * kinetic
    out = [q[1 + k]] + [q[1 + c] * velocity for c in range(3)] + [(q[4] + pressure) * velocity]
    out[1 + k] = out[1 + k] + pressure
    return out


def twice_flux(left, right, speed, k):
    from_left, from_right = flux_of(left, k), flux_of(right, k)
    return [
        (a + b) - speed * (r - l) for a, b, l, r in zip(from_left, from_right, left, right, strict=True)
    ]


def sweep(load, speed_at, store, begin, end, k, beside=()):
    beside = list(beside)
    share = -(-len(beside) // (end - begin))
    start = [[load(f, begin + i) for f in range(5)] for i in (-3, -2, -1)]
    steps = [[b - a for a, b in zip(start[i], start[i + 1], strict=True)] for i in range(2)]
    cell = start[1], start[2]
    ups = upper_old = speed_old = flux_old = None
    for i in range(begin - 2, end + 1):
        ahead = [load(f, i + 2) for f in range(5)]
        steps.append([a - b for a, b in zip(ahead, cell[1], strict=True)])
        now = [rise(*each) for each in zip(*steps, strict=True)]
        if ups is not None:
            downs = [u - d for u, d in zip(ups, steps[0], strict=True)]
            pairs = [upper_and_lower(*each) for each in zip(cell[0], now, downs, strict=True)]
            upper, lower = [p[0] for p in pairs], [p[1] for p in pairs]
            speed = speed_at(i, cell[0])
            if upper_old is not None:
                flux = twice_flux(upper_old, lower, jnp.maximum(speed_old, speed), k)
                if flux_old is not None:
                    store(i - 1, [a - b for a, b in zip(flux, flux_old, strict=True)])
                flux_old = flux
            upper_old, speed_old = upper, speed
        for call in beside[:share]:
            call()
        beside = beside[share:]
        ups, cell, steps = now, (cell[1], ahead), steps[1:]
    for call in beside:
        call()


def sides(one, two, low, high, rank):
    even = rank % 2 == 0
    for row in range(0, low.shape[0], 8):
        a, b = one[row : row + 8, :], two[row : row + 8, :]
        low[row : row + 8, :] = jnp.where(even, b, a)
        high[row : row + 8, :] = jnp.where(even, a, b)


def inner_kernel(
    place, state, far_pairs, far_count, far_coarse, out, fine_uses, coarse_uses,
    turned_even, turned_odd, changes_even, changes_odd, padded, inverse_of, sound, by_y,
    fine_pairs, fine_count, coarse_pairs, arrived,
):
    turned, changes = (turned_even, turned_odd), (changes_even, changes_odd)

    def turn(block, f):
        into, base = turned[block % 2], f * TALL
        flat = state[f * ROWS + block * 128 : f * ROWS + block * 128 + 128, :].T
        into[base + 8 : base + 136, :] = flat
        into[base : base + 8, :] = jnp.broadcast_to(flat[0:1], (8, 128))
        into[base + 136 : base + 144, :] = jnp.broadcast_to(flat[127:128], (8, 128))

    def turn_back(block, f):
        flat = changes[block % 2][f * 128 : f * 128 + 128, :]
        out[f * ROWS + block * 128 : f * ROWS + block * 128 + 128, :] = flat.T

    def along_z(block, beside):
        source, into = turned[block % 2], changes[block % 2]

        def load(f, i):
            return source[pl.ds(f * TALL + 8 + i, 8, stride=16), :]

        def speed_at(i, q):
            inverse = reciprocal(q[0])
            return jnp.abs(q[3]) * inverse + sound_of(q, inverse)

        def store(i, values):
            for f in range(5):
                into[pl.ds(f * 128 + i, 8, stride=16), :] = values[f]

        sweep(load, speed_at, store, 0, 16, 2, beside)

    reads = [
        pltpu.make_async_copy(source, into, arrived.at[n])
        for n, (source, into) in enumerate(
            ((far_pairs, fine_pairs), (far_count, fine_count), (far_coarse, coarse_pairs))
        )
    ]
    for copy in reads:
        copy.start()
    for f in range(5):
        turn(0, f)
    for block in range(4):
        beside = []
        for f in range(5):
            if block < 3:
                beside.append(functools.partial(turn, block + 1, f))
            if block > 0:
                beside.append(functools.partial(turn_back, block - 1, f))
        along_z(block, beside)
    for f in range(5):
        turn_back(3, f)
    for copy in reads:
        copy.wait()
    codes = jnp.concatenate([fine_pairs[...].astype(F32)] * 4, axis=1).T[0:32]
    spread = (iota((16, 128), 1) % 16 == iota((16, 128), 0)).astype(F32)
    used = fold_rows(
        jnp.dot(fine_count[...].astype(F32), spread, precision=HIGH, preferred_element_type=F32), 16
    )
    codes = jnp.where(iota((32, 128), 0).astype(F32) < used, codes, 1000.0)
    along = jnp.floor((codes + 0.5) * 0.04)
    plane = codes - 25.0 * along
    group = jnp.floor((plane + 0.5) * 0.2)
    one = jnp.left_shift(1, (6.0 * (plane - 5.0 * group)).astype(jnp.int32))
    ones = [jnp.where(group == g, one, 0) for g in range(5)]
    for g in range(5):
        lines = []
        for ox in range(5):
            hits = jnp.where(along == ox, ones[g], 0)
            hits = (hits[0:8] + hits[8:16]) + (hits[16:24] + hits[24:32])
            lines.append(jnp.sum(hits, axis=0, keepdims=True))
        fine_uses[g * 8 : g * 8 + 8, :] = jnp.concatenate(lines + [jnp.zeros((3, 128), jnp.int32)], axis=0)

    slot = iota((8, 128), 1)
    device = slot % place[2] * place[3] + slot // place[2]
    for half in range(2):
        named = coarse_pairs[half * 8 : half * 8 + 8, :]
        coded = named // 16 + named % 4 * (6 * 256) + named // 4 % 4 * 65536
        counts = [jnp.zeros((8, 128), jnp.int32) for _ in range(4)]
        for j in range(32):
            code = jnp.broadcast_to(coded[:, j : j + 1], (8, 128))
            one = jnp.where((code & 255) == device, jnp.left_shift(1, (code >> 8) & 255), 0)
            group = code >> 16
            counts = [each + jnp.where(group == g, one, 0) for g, each in enumerate(counts)]
        for g in range(4):
            coarse_uses[(g * 2 + half) * 8 : (g * 2 + half) * 8 + 8, :] = counts[g]
    for x in range(NX):
        for y in range(0, NY, 8):
            row = x * NY + y
            q = [state[f * ROWS + row : f * ROWS + row + 8, :] for f in range(5)]
            inverse = reciprocal(q[0])
            at = x * PITCH + y
            for f in range(5):
                padded[f * NX * PITCH + at : f * NX * PITCH + at + 8, :] = q[f]
            inverse_of[at : at + 8, :] = inverse
            sound[at : at + 8, :] = sound_of(q, inverse)

    def along_x(step, _):
        start = pl.multiple_of(step * 8, 8)

        def rows(f, i):
            return pl.ds(pl.multiple_of(f * ROWS + i * NY + start, 8), 8)

        def speed_at(i, q):
            at = pl.ds(i * PITCH + start, 8)
            return jnp.abs(q[1]) * inverse_of[at, :] + sound[at, :]

        def store(i, values):
            for f in range(5):
                out[rows(f, i), :] = out[rows(f, i), :] + values[f]

        sweep(lambda f, i: state[rows(f, i), :], speed_at, store, 3, NX - 3, 0)
        return 0

    lax.fori_loop(0, NY // 8, along_x, 0)

    def along_y(step, _):
        start = pl.multiple_of(step * 8, 8)

        def rows(f, i):
            return pl.ds((f * NX + start) * PITCH + i, 8, stride=PITCH)

        def speed_at(i, q):
            return jnp.abs(q[2]) * inverse_of[rows(0, i), :] + sound[rows(0, i), :]

        def store(i, values):
            for f in range(5):
                by_y[rows(f, i), :] = values[f]

        for i in (0, 1, 2, NY - 3, NY - 2, NY - 1):
            store(i, [jnp.zeros((8, 128), F32)] * 5)
        sweep(lambda f, i: padded[rows(f, i), :], speed_at, store, 3, NY - 3, 1)
        return 0

    lax.fori_loop(0, NX // 8, along_y, 0)

    def total(x, _):
        for f in range(5):
            for y in range(0, NY, 8):
                row = pl.ds(pl.multiple_of(f * ROWS + x * NY + y, 8), 8)
                out[row, :] = out[row, :] + by_y[pl.ds((f * NX + x) * PITCH + y, 8), :]
        return 0

    lax.fori_loop(0, NX, total, 0, unroll=2)


def tensors(r, square):
    root = lax.rsqrt(jnp.maximum(square, 1.0))
    cube = root * root * root
    three = 3.0 * cube * (root * root)
    scaled = [three * each for each in r]
    pull = [each * cube for each in r]
    tide = [scaled[i] * r[j] - cube if i == j else scaled[i] * r[j] for i, j in SYM]
    return pull, tide


def add_terms(totals, uses, r, square, mass, dipole):
    pull, tide = tensors(r, square)
    mass = uses * mass
    dipole = [uses * d for d in dipole]
    for i in range(3):
        term = mass * pull[i]
        for j in range(3):
            term = term - tide[sym(i, j)] * dipole[j]
        totals[i] = totals[i] + term
    for e in range(6):
        totals[3 + e] = totals[3 + e] + mass * tide[e]


def far_fields(place, uses_fine, uses_coarse, got, own, beside, around):
    morton, octant = place[0], place[1]
    mortons, octs = place[2], place[3]
    lane = iota((8, 128), 1)
    lane_row = iota((1, 128), 1)

    rows = jnp.concatenate([got[pl.ds(g * 8 * SENT, 8, stride=SENT), :] for g in range(16)], axis=0)
    time_step = COURANT / jnp.max(rows[:, 64:128])
    moments = rows.T
    target_z = iota((8, 128), 0)
    rx = 16.0 * (lane % mortons - morton).astype(F32)
    coarse = []
    for half in range(2):
        totals = [jnp.zeros((8, 128), F32) for _ in range(9)]
        for lp in range(16):
            ry = 16.0 * (lane // mortons * 2 + lp // 8 - (2 * octant + half)).astype(F32)
            rz = 16.0 * (lp % 8 - target_z).astype(F32)
            families = [jnp.broadcast_to(moments[m * 16 + lp : m * 16 + lp + 1], (8, 128)) for m in range(4)]
            row = (lp // 4 * 2 + half) * 8
            uses = ((uses_coarse[row : row + 8, :] >> (lp % 4 * 6)) & 63).astype(F32)
            add_terms(totals, uses, (rx, ry, rz), rx * rx + ry * ry + rz * rz, families[0], families[1:])
        coarse.append([jnp.sum(each, axis=1, keepdims=True) for each in totals])
    result = []
    for e in range(9):
        column = jnp.where(lane // 32 % 2 == 0, coarse[0][e], coarse[1][e])
        column = jnp.where(lane % 16 // 2 == iota((8, 128), 0), column, 0.0)
        result.append(jnp.sum(column, axis=0, keepdims=True))
    side = [4.0 * (2 * s - 1).astype(F32) for s in (lane_row // 64, lane_row // 16 % 2, lane_row % 2)]
    for i in range(3):
        for j in range(3):
            result[i] = result[i] + result[3 + sym(i, j)] * side[j]

    def inside(dx, dy):
        at_x, at_y = morton + dx, octant + dy
        return (at_x >= 0) & (at_x < mortons) & (at_y >= 0) & (at_y < octs)

    blocks = []
    for dy in (-1, 0, 1):
        block = []
        if dy:
            halves = []
            for dx in (-1, 0, 1):
                device = jnp.clip(octant + dy, 0, octs - 1) * mortons + jnp.clip(morton + dx, 0, mortons - 1)
                for n in (1, 2):
                    halves.append(jnp.where(inside(dx, dy), got[pl.ds(device * SENT + n, 1), :], 0.0))
            halves = jnp.concatenate(halves + [jnp.zeros((2, 128), F32)], axis=0)
            back = 32 if dy < 0 else 0
            unpacked = [
                jnp.where(lane < 64, pltpu.roll(each, back, 1), pltpu.roll(each, 32 + back, 1)) if back
                else jnp.where(lane < 64, each, pltpu.roll(each, 32, 1))
                for each in (halves, pltpu.roll(halves, 64, 1))
            ]
            for n in range(6):
                block += [unpacked[0][n : n + 1], unpacked[1][n : n + 1]]
        else:
            for dx, source in ((-1, beside[0:4, :]), (0, own[0:4, :]), (1, beside[8:12, :])):
                block.append(jnp.where(inside(dx, 0), source, 0.0))
        blocks.append(jnp.concatenate(block + [jnp.zeros((4, 128), F32)], axis=0))
    wide = iota((16, 128), 1)
    around[...] = jnp.zeros(around.shape, F32)
    for oy in range(-2, 3):
        if oy == 0:
            moved = blocks[1]
        else:
            moved = pltpu.roll(blocks[1], (-16 * oy) % 128, 1)
            if oy > 0:
                moved = jnp.where(wide // 16 % 4 + oy > 3, pltpu.roll(blocks[2], (64 - 16 * oy) % 128, 1), moved)
            else:
                moved = jnp.where(wide // 16 % 4 + oy < 0, pltpu.roll(blocks[0], (-64 - 16 * oy) % 128, 1), moved)
        swapped = pltpu.roll(moved, 64, 1)
        for m in range(4):
            low, own, high = [(moved[d * 4 + m : d * 4 + m + 1], swapped[d * 4 + m : d * 4 + m + 1]) for d in range(3)]
            first = lane_row < 64
            lines = [
                low[0], jnp.where(first, low[1], own[1]), own[0], jnp.where(first, own[1], high[1]), high[0],
            ]
            row = (m * 5 + oy + 2) * 8
            around[row : row + 5, :] = jnp.concatenate(lines, axis=0)
    totals = [jnp.zeros((8, 128), F32) for _ in range(9)]
    rx = 8.0 * (iota((8, 128), 0) - 2).astype(F32)
    square_x = rx * rx
    for oy in range(-2, 3):
        base = [around[(m * 5 + oy + 2) * 8 : (m * 5 + oy + 2) * 8 + 8, :] for m in range(4)]
        for oz in range(-2, 3):
            moved = base
            if oz:
                ok = (lane % 16 + oz >= 0) & (lane % 16 + oz < 16)
                moved = [jnp.where(ok, pltpu.roll(each, (-oz) % 128, 1), 0.0) for each in base]
            uses = ((uses_fine[(oy + 2) * 8 : (oy + 2) * 8 + 8, :] >> ((oz + 2) * 6)) & 63).astype(F32)
            add_terms(
                totals, uses, (rx, 8.0 * oy, 8.0 * oz),
                square_x + (64.0 * oy * oy + 64.0 * oz * oz), moved[0], moved[1:],
            )
    for e in range(9):
        result[e] = GRAVITY * (result[e] + jnp.sum(totals[e], axis=0, keepdims=True))
    return result, time_step


def edge_kernel(
    place, state, inner, x_one, x_two, far_y_one, far_y_two, out, beside,
    y_one, y_two, x_low, x_high, y_low, y_high, rims, by_x, by_y, arrived,
):
    reads = [
        pltpu.make_async_copy(far_y_one, y_one, arrived.at[0]),
        pltpu.make_async_copy(far_y_two, y_two, arrived.at[1]),
    ]
    for copy in reads:
        copy.start()
    sides(x_two, x_one, x_low, x_high, place[0])
    even = place[0] % 2 == 0
    moments = x_one[480:488, :], x_two[480:488, :]
    beside[0:8, :] = jnp.where(even, moments[0], moments[1])
    beside[8:16, :] = jnp.where(even, moments[1], moments[0])

    def x_edge(beyond, x):
        for f in range(5):
            cells = state[f * ROWS + x * NY : f * ROWS + x * NY + NY, :]
            for layer in range(3):
                beyond[(f * 3 + layer) * NY : (f * 3 + layer) * NY + NY, :] = cells

    pl.when(place[0] == 0)(lambda: x_edge(x_low, 0))
    pl.when(place[0] == place[2] - 1)(lambda: x_edge(x_high, NX - 1))

    def speed_of(k):
        def speed_at(i, q):
            inverse = reciprocal(q[0])
            return jnp.abs(q[1 + k]) * inverse + sound_of(q, inverse)

        return speed_at

    def along_x(step, _):
        start = pl.multiple_of(step * 8, 8)

        def load(f, i):
            if i < 0:
                return x_low[pl.ds(pl.multiple_of((f * 3 + i + 3) * NY + start, 8), 8), :]
            if i >= NX:
                return x_high[pl.ds(pl.multiple_of((f * 3 + i - NX) * NY + start, 8), 8), :]
            return state[pl.ds(pl.multiple_of(f * ROWS + i * NY + start, 8), 8), :]

        def store(i, values):
            for f in range(5):
                by_x[pl.ds(pl.multiple_of((f * 6 + (i if i < 3 else i - 10)) * NY + start, 8), 8), :] = values[f]

        sweep(load, speed_of(0), store, 0, 3, 0)
        sweep(load, speed_of(0), store, NX - 3, NX, 0)
        return 0

    lax.fori_loop(0, NY // 8, along_x, 0)

    for f in range(5):
        for x in range(NX):
            for side, y in ((0, 0), (8, NY - 8)):
                row = (f * NX + x) * RIM + side
                rims[row : row + 8, :] = state[f * ROWS + x * NY + y : f * ROWS + x * NY + y + 8, :]
                by_y[row : row + 8, :] = jnp.zeros((8, 128), F32)
    for copy in reads:
        copy.wait()
    sides(y_one, y_two, y_low, y_high, place[1])

    def y_edge(beyond, row):
        for f in range(5):
            cells = rims[pl.ds(f * NX * RIM + row, NX, stride=RIM), :]
            for layer in range(3):
                beyond[pl.ds(f * NX * 3 + layer, NX, stride=3), :] = cells

    pl.when(place[1] == 0)(lambda: y_edge(y_low, 0))
    pl.when(place[1] == place[3] - 1)(lambda: y_edge(y_high, 15))

    def along_y(step, _):
        start = pl.multiple_of(step * 8, 8)

        def rows(f, i):
            return pl.ds((f * NX + start) * RIM + (i if i < 8 else i - 16), 8, stride=RIM)

        def load(f, i):
            if i < 0:
                return y_low[pl.ds((f * NX + start) * 3 + i + 3, 8, stride=3), :]
            if i >= NY:
                return y_high[pl.ds((f * NX + start) * 3 + i - NY, 8, stride=3), :]
            return rims[rows(f, i), :]

        def store(i, values):
            for f in range(5):
                by_y[rows(f, i), :] = values[f]

        sweep(load, speed_of(1), store, 0, 3, 1)
        sweep(load, speed_of(1), store, NY - 3, NY, 1)
        return 0

    lax.fori_loop(0, NX // 8, along_y, 0)

    for f in range(5):
        for x in range(NX):
            for y in range(0, NY, 8):
                row = f * ROWS + x * NY + y
                total = inner[row : row + 8, :]
                if x < 3 or x >= NX - 3:
                    at = (f * 6 + (x if x < 3 else x - 10)) * NY + y
                    total = total + by_x[at : at + 8, :]
                if y in (0, NY - 8):
                    at = (f * NX + x) * RIM + (0 if y == 0 else 8)
                    total = total + by_y[at : at + 8, :]
                out[row : row + 8, :] = total


def update_kernel(
    place, state, twice, uses_fine, uses_coarse, got, own, beside, new, gravity, around, field, made, pulls, written
):
    result, time_step = far_fields(place, uses_fine, uses_coarse, got, own, beside, around)
    half_step = 0.5 * time_step
    source = iota((8, 128), 0) * 16 + iota((8, 128), 1) // 8
    lines = [
        jnp.take_along_axis(jnp.broadcast_to(each, (8, 128)), source, axis=1, mode="promise_in_bounds") for each in result
    ]
    offset_z = (iota((8, 128), 1) % 8).astype(F32) - 3.5
    for i in range(3):
        field[i * 8 : i * 8 + 8, :] = lines[i] + lines[3 + sym(i, 2)] * offset_z
        field[(3 + i) * 8 : (3 + i) * 8 + 8, :] = lines[3 + sym(i, 0)]
        field[(6 + i) * 8 : (6 + i) * 8 + 8, :] = lines[3 + sym(i, 1)]
    offset_y = iota((8, 128), 0).astype(F32) - 3.5

    def writes(part):
        rows = pl.ds(part * 4, 4)
        return [
            pltpu.make_async_copy(made.at[:, rows, :, :], new.at[:, rows, :, :], written.at[0, part]),
            pltpu.make_async_copy(pulls.at[:, rows, :, :], gravity.at[:, rows, :, :], written.at[1, part]),
        ]

    lines = {}
    for x in range(NX):
        for ty in range(4):
            tx, y = x // 8, ty * 8
            if x % 8 == 0:
                at = [field[e * 8 + tx * 4 + ty : e * 8 + tx * 4 + ty + 1, :] for e in range(9)]
                lines[ty] = ([at[e] + at[6 + e] * offset_y for e in range(3)], at[3:6])
            base, slope = lines[ty]
            q = [state[f * ROWS + x * NY + y : f * ROWS + x * NY + y + 8, :] for f in range(5)]
            pull = [base[e] + slope[e] * (x % 8 - 3.5) for e in range(3)]
            moved = []
            for f in range(5):
                total = twice[f * ROWS + x * NY + y : f * ROWS + x * NY + y + 8, :]
                moved.append(q[f] - half_step * total)
            weight = time_step * q[0]
            gain = q[1] * pull[0] + q[2] * pull[1] + q[3] * pull[2]
            made[0, x, y : y + 8, :] = moved[0]
            for e in range(3):
                pulls[e, x, y : y + 8, :] = pull[e]
                made[1 + e, x, y : y + 8, :] = moved[1 + e] + weight * pull[e]
            made[4, x, y : y + 8, :] = moved[4] + time_step * gain
        if x % 4 == 3:
            for copy in writes(x // 4):
                copy.start()
    for part in range(4):
        for copy in writes(part):
            copy.wait()


VMEM = pl.BlockSpec(memory_space=pltpu.VMEM)
SMEM = pl.BlockSpec(memory_space=pltpu.SMEM)
FAR = pl.BlockSpec(memory_space=pltpu.HBM)
LIMIT = pltpu.CompilerParams(vmem_limit_bytes=12 * 1024 * 1024)
SMALL = pl.CostEstimate(flops=1000, bytes_accessed=1000, transcendentals=0)


def far(values):
    return pltpu.with_memory_space_constraint(values, pltpu.HBM)


def call(kernel, outs, scratch, *args, sources=None, far_outs=(), whole_numbers=()):
    shapes = [(o, 128) if isinstance(o, int) else o for o in outs]
    return pl.pallas_call(
        kernel,
        out_shape=[
            pltpu.HBM(s, F32) if n in far_outs else jax.ShapeDtypeStruct(s, jnp.int32 if n in whole_numbers else F32)
            for n, s in enumerate(shapes)
        ],
        in_specs=[SMEM] + (sources or [VMEM] * (len(args) - 1)),
        out_specs=[FAR if n in far_outs else VMEM for n in range(len(outs))],
        scratch_shapes=[pltpu.VMEM((s, 128), F32) if isinstance(s, int) else s for s in scratch],
        compiler_params=LIMIT,
        cost_estimate=SMALL,
    )(*args)


def local(state, fine_pairs, fine_count, coarse_pairs):
    mortons, octs = lax.axis_size("morton"), lax.axis_size("oct")
    place = jnp.stack([lax.axis_index("morton"), lax.axis_index("oct"), mortons, octs]).astype(jnp.int32)
    many = NX * PITCH

    def swap(values, pair):
        pairs = [(m, o) for m in range(mortons) for o in range(octs)]
        index = lambda place: place[0] * octs + place[1]
        return lax.ppermute(values, AXES, [(index(p), index(pair(*p))) for p in pairs])

    def other(i):
        return (i - 1 ^ 1) + 1

    block = pltpu.VMEM((5, ROWS, 128), F32)
    sent, x_one, x_two, y_one, y_two, own = call(
        moments_kernel, [128 * SENT, LONG, LONG, 240, 240, 8],
        [block, 128 * SENT, 240, 240, pltpu.SemaphoreType.DMA((4,)), pltpu.SemaphoreType.DMA((2, 6)),
         pltpu.SemaphoreType.DMA((3,))],
        place, far(state.reshape(5, ROWS, 128)), sources=[FAR], far_outs=range(5),
    )
    got = lax.all_to_all(sent.reshape(mortons * octs, 1, SENT * 128), AXES[::-1], 0, 0, tiled=True)
    x_one = swap(x_one, lambda m, o: (other(m), o) if 0 < m < mortons - 1 else (m, o ^ 1))
    x_two = swap(x_two, lambda m, o: (m ^ 1, o))
    y_one = swap(y_one, lambda m, o: (m, o ^ 1))
    y_two = swap(y_two, lambda m, o: (m, other(o)) if 0 < o < octs - 1 else (m, octs - 1 - o))
    rows = state.reshape(5 * ROWS, 128)
    rows, sent = lax.optimization_barrier((rows, sent))
    inner, uses_fine, uses_coarse = call(
        inner_kernel, [5 * ROWS, 40, 64],
        [5 * TALL, 5 * TALL, 640, 640, 5 * many, many, many, 5 * many, pltpu.VMEM((128, 32), jnp.int32),
         pltpu.VMEM((8, 16), jnp.int32), pltpu.VMEM((16, 32), jnp.int32), pltpu.SemaphoreType.DMA((3,))],
        place, rows, far(fine_pairs.reshape(128, 32)), far(fine_count.reshape(8, 16)), far(coarse_pairs.reshape(16, 32)),
        sources=[VMEM, FAR, FAR, FAR], whole_numbers=(1, 2),
    )
    rim = 5 * NX * RIM
    twice, beside = call(
        edge_kernel, [5 * ROWS, 16], [240, 240, 480, 480, 240, 240, rim, 960, rim, pltpu.SemaphoreType.DMA((2,))],
        place, rows, inner, x_one, x_two, far(y_one), far(y_two), sources=[VMEM] * 4 + [FAR] * 2,
    )
    return call(
        update_kernel, [(5, NX, NY, NZ), (3, NX, NY, NZ)],
        [160, 72, pltpu.VMEM((5, NX, NY, NZ), F32), pltpu.VMEM((3, NX, NY, NZ), F32), pltpu.SemaphoreType.DMA((2, 4))],
        place, rows, twice, uses_fine, uses_coarse, got.reshape(mortons * octs * SENT, 128), own, beside,
        far_outs=range(2),
    )


def solution(mesh):
    in_specs = (
        P(None, "morton", "oct", None),
        P("morton", "oct", None, None),
        P("morton", "oct", None),
        P("morton", "oct", None, None),
    )
    out_specs = (P(None, "morton", "oct", None), P(None, "morton", "oct", None))
    return jax.shard_map(local, mesh=mesh, in_specs=in_specs, out_specs=out_specs, check_vma=False)
```

```python
import functools

import functools

import jax
import jax.numpy as jnp
from jax import lax
from jax.experimental import pallas as pl
from jax.experimental.pallas import tpu as pltpu
from jax.sharding import PartitionSpec as P

ADIABATIC = 5.0 / 3.0
COURANT = 0.2
GRAVITY = 1.0
AXES = ("morton", "oct")
F32 = jnp.float32
HIGH = lax.Precision.HIGHEST

NX, NY, NZ = 16, 32, 128
ROWS = NX * NY
PITCH = 33
TALL = 144
LONG = 488
RIM = 17
SENT = 3
SYM = ((0, 0), (0, 1), (0, 2), (1, 1), (1, 2), (2, 2))


def iota(shape, dim):
    return lax.broadcasted_iota(jnp.int32, shape, dim)


def sym(i, j):
    return SYM.index((min(i, j), max(i, j)))


def reciprocal(x):
    return pl.reciprocal(x, approx=True)


def sound_of(q, inverse):
    kinetic = (q[1] * q[1] + q[2] * q[2] + q[3] * q[3]) * inverse
    pressure = (2.0 / 3.0) * q[4] - (1.0 / 3.0) * kinetic
    square = ADIABATIC * pressure * inverse
    return square * lax.rsqrt(square)


def fold_rows(values, group):
    keep = iota(values.shape, 1) // group == iota(values.shape, 0)
    return jnp.sum(jnp.where(keep, values, 0.0), axis=0, keepdims=True)


def moments_kernel(
    place, state, sent, x_one, x_two, y_one, y_two, own, rows, arrived
):
    part = ROWS // 4
    copies = [
        pltpu.make_async_copy(
            state.at[:, pl.ds(c * part, part), :], rows.at[:, pl.ds(c * part, part), :], arrived.at[c]
        )
        for c in range(4)
    ]
    even, oct_even = place[0] % 2 == 0, place[1] % 2 == 0
    x_starts = (jnp.where(even, 0, NX - 3), jnp.where(even, NX - 3, 0))
    y_starts = (jnp.where(oct_even, NY - 3, 0), jnp.where(oct_even, 0, NY - 3))
    for copy in copies:
        copy.start()
    offset_y = iota((8, 128), 0).astype(F32) - 3.5
    fastest = jnp.zeros((8, 128), F32)
    sums, sums_x, sums_y = [], [], []
    for tx in range(2):
        totals, totals_x = [jnp.zeros((8, 128), F32)] * 4, [jnp.zeros((8, 128), F32)] * 4
        for half in range(2):
            copies[tx * 2 + half].wait()
            for x in range(half * 4, half * 4 + 4):
                for ty in range(4):
                    row = (tx * 8 + x) * NY + ty * 8
                    q = [rows[f, row : row + 8, :] for f in range(5)]
                    inverse = reciprocal(q[0])
                    speed_of_sound = sound_of(q, inverse)
                    largest = jnp.maximum(jnp.maximum(jnp.abs(q[1]), jnp.abs(q[2])), jnp.abs(q[3]))
                    fastest = jnp.maximum(fastest, largest * inverse + speed_of_sound)
                    totals[ty] = totals[ty] + q[0]
                    totals_x[ty] = totals_x[ty] + q[0] * (x - 3.5)
        for ty in range(4):
            sums.append(jnp.sum(totals[ty], axis=0, keepdims=True))
            sums_x.append(jnp.sum(totals_x[ty], axis=0, keepdims=True))
            sums_y.append(jnp.sum(totals[ty] * offset_y, axis=0, keepdims=True))
    for out, start in ((x_one, x_starts[0]), (x_two, x_starts[1])):
        for f in range(5):
            out[f * 96 : f * 96 + 96, :] = rows[f, pl.ds(pl.multiple_of(start * NY, 32), 96), :]
    for out, start in ((y_one, y_starts[0]), (y_two, y_starts[1])):
        for f in range(5):
            for x in range(NX):
                row = (f * NX + x) * 3
                out[row : row + 3, :] = rows[f, pl.ds(x * NY + start, 3), :]
    parents = []
    for py in range(2):
        children = [(tx, ty) for tx in range(2) for ty in (2 * py, 2 * py + 1)]
        terms = [[], [], []]
        for tx, ty in children:
            n = tx * 4 + ty
            terms[0].append(sums[n])
            terms[1].append(sums_x[n] + (8.0 * tx - 4.0) * sums[n])
            terms[2].append(sums_y[n] + (8.0 * (ty % 2) - 4.0) * sums[n])
        parents.append([(t[0] + t[1]) + (t[2] + t[3]) for t in terms])
    parents = [parents[py][m] for m in range(3) for py in range(2)]
    lines = jnp.concatenate(sums + sums_x + sums_y + parents + [jnp.zeros((2, 128), F32)], axis=0)
    z, lanes = iota((128, 128), 0), iota((128, 128), 1)
    pick = (z // 8 == lanes % 16).astype(F32)
    pick_parent = (z // 16 == lanes % 8).astype(F32)
    picks = [
        pick, pick * ((z % 8).astype(F32) - 3.5), pick_parent, pick_parent * ((z % 16).astype(F32) - 7.5)
    ]
    folded = jnp.dot(lines, jnp.concatenate(picks, axis=1), precision=HIGH, preferred_element_type=F32)
    mass = fold_rows(folded[0:8, 0:128], 16)
    dipole = [
        fold_rows(folded[8:16, 0:128], 16), fold_rows(folded[16:24, 0:128], 16), fold_rows(folded[0:8, 128:256], 16)
    ]
    lane = iota((1, 128), 1)
    families = jnp.concatenate([folded[24:30, 256:384], folded[24:26, 384:512]], axis=0)
    last = jnp.where(lane < 64, fold_rows(families, 8), jnp.max(fastest))
    own[...] = jnp.concatenate([mass] + dipole + [jnp.zeros((4, 128), F32)], axis=0)
    x_one[480:488, :] = own[...]
    x_two[480:488, :] = own[...]
    patterns = []
    for side in range(2):
        packed = [
            jnp.where(lane < 32, pltpu.roll(v, (-32 * side) % 128, 1), pltpu.roll(v, (-32 - 32 * side) % 128, 1))
            for v in [mass] + dipole
        ]
        pairs = [jnp.where(lane < 64, packed[m], pltpu.roll(packed[m + 1], 64, 1)) for m in (0, 2)]
        patterns.append(jnp.concatenate([last] + pairs, axis=0))
    patterns = [jnp.concatenate([p] * 8, axis=0) for p in patterns]
    for octant in range(4):
        chosen = jnp.where(octant > place[1], patterns[1], patterns[0])
        for part in range(4):
            row = octant * 96 + part * 24
            sent[row : row + 24, :] = chosen


def rise(before, here, after):
    value = 0.5 * here + (1.0 / 12.0) * (before - after)
    return jnp.minimum(jnp.maximum(value, jnp.minimum(here, 0.0)), jnp.maximum(here, 0.0))


def upper_and_lower(centre, up, down):
    most_up, most_down = jnp.abs(down + down), jnp.abs(up + up)
    upper = centre + jnp.minimum(jnp.maximum(up, -most_up), most_up)
    lower = centre + jnp.minimum(jnp.maximum(down, -most_down), most_down)
    return upper, lower


def flux_of(q, k):
    inverse = reciprocal(q[0])
    velocity = q[1 + k] * inverse
    kinetic = (q[1] * q[1] + q[2] * q[2] + q[3] * q[3]) * inverse
    pressure = (2.0 / 3.0) * q[4] - (1.0 / 3.0) * kinetic
    out = [q[1 + k]] + [q[1 + c] * velocity for c in range(3)] + [(q[4] + pressure) * velocity]
    out[1 + k] = out[1 + k] + pressure
    return out


def twice_flux(left, right, speed, k):
    from_left, from_right = flux_of(left, k), flux_of(right, k)
    return [
        (a + b) - speed * (r - l) for a, b, l, r in zip(from_left, from_right, left, right, strict=True)
    ]


def sweep(load, speed_at, store, begin, end, k, beside=()):
    beside = list(beside)
    share = -(-len(beside) // (end - begin))
    start = [[load(f, begin + i) for f in range(5)] for i in (-3, -2, -1)]
    steps = [[b - a for a, b in zip(start[i], start[i + 1], strict=True)] for i in range(2)]
    cell = start[1], start[2]
    ups = upper_old = speed_old = flux_old = None
    for i in range(begin - 2, end + 1):
        ahead = [load(f, i + 2) for f in range(5)]
        steps.append([a - b for a, b in zip(ahead, cell[1], strict=True)])
        now = [rise(*each) for each in zip(*steps, strict=True)]
        if ups is not None:
            downs = [u - d for u, d in zip(ups, steps[0], strict=True)]
            pairs = [upper_and_lower(*each) for each in zip(cell[0], now, downs, strict=True)]
            upper, lower = [p[0] for p in pairs], [p[1] for p in pairs]
            speed = speed_at(i, cell[0])
            if upper_old is not None:
                flux = twice_flux(upper_old, lower, jnp.maximum(speed_old, speed), k)
                if flux_old is not None:
                    store(i - 1, [a - b for a, b in zip(flux, flux_old, strict=True)])
                flux_old = flux
            upper_old, speed_old = upper, speed
        for call in beside[:share]:
            call()
        beside = beside[share:]
        ups, cell, steps = now, (cell[1], ahead), steps[1:]
    for call in beside:
        call()


def sides(one, two, low, high, rank):
    even = rank % 2 == 0
    for row in range(0, low.shape[0], 8):
        a, b = one[row : row + 8, :], two[row : row + 8, :]
        low[row : row + 8, :] = jnp.where(even, b, a)
        high[row : row + 8, :] = jnp.where(even, a, b)


def inner_kernel(
    place, state, far_pairs, far_count, far_coarse, out, fine_uses, coarse_uses,
    turned_even, turned_odd, changes_even, changes_odd, padded, inverse_of, sound, by_y,
    fine_pairs, fine_count, coarse_pairs, arrived,
):
    turned, changes = (turned_even, turned_odd), (changes_even, changes_odd)

    def turn(block, f):
        into, base = turned[block % 2], f * TALL
        flat = state[f * ROWS + block * 128 : f * ROWS + block * 128 + 128, :].T
        into[base + 8 : base + 136, :] = flat
        into[base : base + 8, :] = jnp.broadcast_to(flat[0:1], (8, 128))
        into[base + 136 : base + 144, :] = jnp.broadcast_to(flat[127:128], (8, 128))

    def turn_back(block, f):
        flat = changes[block % 2][f * 128 : f * 128 + 128, :]
        out[f * ROWS + block * 128 : f * ROWS + block * 128 + 128, :] = flat.T

    def along_z(block, beside):
        source, into = turned[block % 2], changes[block % 2]

        def load(f, i):
            return source[pl.ds(f * TALL + 8 + i, 8, stride=16), :]

        def speed_at(i, q):
            inverse = reciprocal(q[0])
            return jnp.abs(q[3]) * inverse + sound_of(q, inverse)

        def store(i, values):
            for f in range(5):
                into[pl.ds(f * 128 + i, 8, stride=16), :] = values[f]

        sweep(load, speed_at, store, 0, 16, 2, beside)

    reads = [
        pltpu.make_async_copy(source, into, arrived.at[n])
        for n, (source, into) in enumerate(
            ((far_pairs, fine_pairs), (far_count, fine_count), (far_coarse, coarse_pairs))
        )
    ]
    for copy in reads:
        copy.start()
    for f in range(5):
        turn(0, f)
    for block in range(4):
        beside = []
        for f in range(5):
            if block < 3:
                beside.append(functools.partial(turn, block + 1, f))
            if block > 0:
                beside.append(functools.partial(turn_back, block - 1, f))
        along_z(block, beside)
    for f in range(5):
        turn_back(3, f)
    for copy in reads:
        copy.wait()
    codes = jnp.concatenate([fine_pairs[...].astype(F32)] * 4, axis=1).T[0:32]
    spread = (iota((16, 128), 1) % 16 == iota((16, 128), 0)).astype(F32)
    used = fold_rows(
        jnp.dot(fine_count[...].astype(F32), spread, precision=HIGH, preferred_element_type=F32), 16
    )
    codes = jnp.where(iota((32, 128), 0).astype(F32) < used, codes, 1000.0)
    along = jnp.floor((codes + 0.5) * 0.04)
    plane = codes - 25.0 * along
    group = jnp.floor((plane + 0.5) * 0.2)
    one = jnp.left_shift(1, (6.0 * (plane - 5.0 * group)).astype(jnp.int32))
    ones = [jnp.where(group == g, one, 0) for g in range(5)]
    fine_uses[24:32, :] = jnp.zeros((8, 128), jnp.int32)
    for g in range(5):
        lines = []
        for ox in range(5):
            hits = jnp.where(along == ox, ones[g], 0)
            hits = (hits[0:8] + hits[8:16]) + (hits[16:24] + hits[24:32])
            lines.append(jnp.sum(hits, axis=0, keepdims=True))
        fine_uses[g * 5 : g * 5 + 5, :] = jnp.concatenate(lines, axis=0)

    slot = iota((8, 128), 1)
    device = slot % place[2] * place[3] + slot // place[2]
    for half in range(2):
        named = coarse_pairs[half * 8 : half * 8 + 8, :]
        coded = named // 16 + named % 4 * (6 * 256) + named // 4 % 4 * 65536
        counts = [jnp.zeros((8, 128), jnp.int32) for _ in range(4)]
        for j in range(32):
            code = jnp.broadcast_to(coded[:, j : j + 1], (8, 128))
            one = jnp.where((code & 255) == device, jnp.left_shift(1, (code >> 8) & 255), 0)
            group = code >> 16
            counts = [each + jnp.where(group == g, one, 0) for g, each in enumerate(counts)]
        for g in range(4):
            coarse_uses[(g * 2 + half) * 8 : (g * 2 + half) * 8 + 8, :] = counts[g]
    for x in range(NX):
        for y in range(0, NY, 8):
            row = x * NY + y
            q = [state[f * ROWS + row : f * ROWS + row + 8, :] for f in range(5)]
            inverse = reciprocal(q[0])
            at = x * PITCH + y
            for f in range(5):
                padded[f * NX * PITCH + at : f * NX * PITCH + at + 8, :] = q[f]
            inverse_of[at : at + 8, :] = inverse
            sound[at : at + 8, :] = sound_of(q, inverse)

    def along_x(step, _):
        start = pl.multiple_of(step * 8, 8)

        def rows(f, i):
            return pl.ds(pl.multiple_of(f * ROWS + i * NY + start, 8), 8)

        def speed_at(i, q):
            at = pl.ds(i * PITCH + start, 8)
            return jnp.abs(q[1]) * inverse_of[at, :] + sound[at, :]

        def store(i, values):
            for f in range(5):
                out[rows(f, i), :] = out[rows(f, i), :] + values[f]

        sweep(lambda f, i: state[rows(f, i), :], speed_at, store, 3, NX - 3, 0)
        return 0

    lax.fori_loop(0, NY // 8, along_x, 0)

    def along_y(step, _):
        start = pl.multiple_of(step * 8, 8)

        def rows(f, i):
            return pl.ds((f * NX + start) * PITCH + i, 8, stride=PITCH)

        def speed_at(i, q):
            return jnp.abs(q[2]) * inverse_of[rows(0, i), :] + sound[rows(0, i), :]

        def store(i, values):
            for f in range(5):
                by_y[rows(f, i), :] = values[f]

        for i in (0, 1, 2, NY - 3, NY - 2, NY - 1):
            store(i, [jnp.zeros((8, 128), F32)] * 5)
        sweep(lambda f, i: padded[rows(f, i), :], speed_at, store, 3, NY - 3, 1)
        return 0

    lax.fori_loop(0, NX // 8, along_y, 0)

    def total(x, _):
        for f in range(5):
            for y in range(0, NY, 8):
                row = pl.ds(pl.multiple_of(f * ROWS + x * NY + y, 8), 8)
                out[row, :] = out[row, :] + by_y[pl.ds((f * NX + x) * PITCH + y, 8), :]
        return 0

    lax.fori_loop(0, NX, total, 0, unroll=2)


def tensors(r, square):
    root = lax.rsqrt(jnp.maximum(square, 1.0))
    cube = root * root * root
    three = 3.0 * cube * (root * root)
    scaled = [three * each for each in r]
    pull = [each * cube for each in r]
    tide = [scaled[i] * r[j] - cube if i == j else scaled[i] * r[j] for i, j in SYM]
    return pull, tide


def add_terms(totals, uses, r, square, mass, dipole):
    pull, tide = tensors(r, square)
    mass = uses * mass
    dipole = [uses * d for d in dipole]
    for i in range(3):
        term = mass * pull[i]
        for j in range(3):
            term = term - tide[sym(i, j)] * dipole[j]
        totals[i] = totals[i] + term
    for e in range(6):
        totals[3 + e] = totals[3 + e] + mass * tide[e]


def far_fields(place, uses_fine, uses_coarse, got, own, beside, around):
    morton, octant = place[0], place[1]
    mortons, octs = place[2], place[3]
    lane = iota((8, 128), 1)
    lane_row = iota((1, 128), 1)

    rows = jnp.concatenate([got[pl.ds(g * 8 * SENT, 8, stride=SENT), :] for g in range(16)], axis=0)
    time_step = COURANT / jnp.max(rows[:, 64:128])
    moments = rows.T
    target_z = iota((8, 128), 0)
    rx = 16.0 * (lane % mortons - morton).astype(F32)
    coarse = []
    for half in range(2):
        totals = [jnp.zeros((8, 128), F32) for _ in range(9)]
        for lp in range(16):
            ry = 16.0 * (lane // mortons * 2 + lp // 8 - (2 * octant + half)).astype(F32)
            rz = 16.0 * (lp % 8 - target_z).astype(F32)
            families = [jnp.broadcast_to(moments[m * 16 + lp : m * 16 + lp + 1], (8, 128)) for m in range(4)]
            row = (lp // 4 * 2 + half) * 8
            uses = ((uses_coarse[row : row + 8, :] >> (lp % 4 * 6)) & 63).astype(F32)
            add_terms(totals, uses, (rx, ry, rz), rx * rx + ry * ry + rz * rz, families[0], families[1:])
        coarse.append([jnp.sum(each, axis=1, keepdims=True) for each in totals])
    result = []
    for e in range(9):
        column = jnp.where(lane // 32 % 2 == 0, coarse[0][e], coarse[1][e])
        column = jnp.where(lane % 16 // 2 == iota((8, 128), 0), column, 0.0)
        result.append(jnp.sum(column, axis=0, keepdims=True))
    side = [4.0 * (2 * s - 1).astype(F32) for s in (lane_row // 64, lane_row // 16 % 2, lane_row % 2)]
    for i in range(3):
        for j in range(3):
            result[i] = result[i] + result[3 + sym(i, j)] * side[j]

    def inside(dx, dy):
        at_x, at_y = morton + dx, octant + dy
        return (at_x >= 0) & (at_x < mortons) & (at_y >= 0) & (at_y < octs)

    blocks = []
    for dy in (-1, 0, 1):
        block = []
        if dy:
            halves = []
            for dx in (-1, 0, 1):
                device = jnp.clip(octant + dy, 0, octs - 1) * mortons + jnp.clip(morton + dx, 0, mortons - 1)
                for n in (1, 2):
                    halves.append(jnp.where(inside(dx, dy), got[pl.ds(device * SENT + n, 1), :], 0.0))
            halves = jnp.concatenate(halves + [jnp.zeros((2, 128), F32)], axis=0)
            back = 32 if dy < 0 else 0
            unpacked = [
                jnp.where(lane < 64, pltpu.roll(each, back, 1), pltpu.roll(each, 32 + back, 1)) if back
                else jnp.where(lane < 64, each, pltpu.roll(each, 32, 1))
                for each in (halves, pltpu.roll(halves, 64, 1))
            ]
            for n in range(6):
                block += [unpacked[0][n : n + 1], unpacked[1][n : n + 1]]
        else:
            for dx, source in ((-1, beside[0:4, :]), (0, own[0:4, :]), (1, beside[8:12, :])):
                block.append(jnp.where(inside(dx, 0), source, 0.0))
        blocks.append(jnp.concatenate(block + [jnp.zeros((4, 128), F32)], axis=0))
    wide = iota((16, 128), 1)
    around[...] = jnp.zeros(around.shape, F32)
    for oy in range(-2, 3):
        if oy == 0:
            moved = blocks[1]
        else:
            moved = pltpu.roll(blocks[1], (-16 * oy) % 128, 1)
            if oy > 0:
                moved = jnp.where(wide // 16 % 4 + oy > 3, pltpu.roll(blocks[2], (64 - 16 * oy) % 128, 1), moved)
            else:
                moved = jnp.where(wide // 16 % 4 + oy < 0, pltpu.roll(blocks[0], (-64 - 16 * oy) % 128, 1), moved)
        swapped = pltpu.roll(moved, 64, 1)
        for m in range(4):
            low, own, high = [(moved[d * 4 + m : d * 4 + m + 1], swapped[d * 4 + m : d * 4 + m + 1]) for d in range(3)]
            first = lane_row < 64
            lines = [
                low[0], jnp.where(first, low[1], own[1]), own[0], jnp.where(first, own[1], high[1]), high[0],
            ]
            row = (m * 5 + oy + 2) * 8
            around[row : row + 5, :] = jnp.concatenate(lines, axis=0)
    totals = [jnp.zeros((8, 128), F32) for _ in range(9)]
    rx = 8.0 * (iota((8, 128), 0) - 2).astype(F32)
    square_x = rx * rx
    for oy in range(-2, 3):
        base = [around[(m * 5 + oy + 2) * 8 : (m * 5 + oy + 2) * 8 + 8, :] for m in range(4)]
        for oz in range(-2, 3):
            moved = base
            if oz:
                ok = (lane % 16 + oz >= 0) & (lane % 16 + oz < 16)
                moved = [jnp.where(ok, pltpu.roll(each, (-oz) % 128, 1), 0.0) for each in base]
            uses = ((uses_fine[(oy + 2) * 5 : (oy + 2) * 5 + 8, :] >> ((oz + 2) * 6)) & 63).astype(F32)
            add_terms(
                totals, uses, (rx, 8.0 * oy, 8.0 * oz),
                square_x + (64.0 * oy * oy + 64.0 * oz * oz), moved[0], moved[1:],
            )
    for e in range(9):
        result[e] = GRAVITY * (result[e] + jnp.sum(totals[e], axis=0, keepdims=True))
    return result, time_step


def edge_kernel(
    place, state, inner, x_one, x_two, y_one, y_two, out, beside,
    x_low, x_high, y_low, y_high, rims, by_x, by_y,
):
    sides(x_two, x_one, x_low, x_high, place[0])
    even = place[0] % 2 == 0
    moments = x_one[480:488, :], x_two[480:488, :]
    beside[0:8, :] = jnp.where(even, moments[0], moments[1])
    beside[8:16, :] = jnp.where(even, moments[1], moments[0])

    def x_edge(beyond, x):
        for f in range(5):
            cells = state[f * ROWS + x * NY : f * ROWS + x * NY + NY, :]
            for layer in range(3):
                beyond[(f * 3 + layer) * NY : (f * 3 + layer) * NY + NY, :] = cells

    pl.when(place[0] == 0)(lambda: x_edge(x_low, 0))
    pl.when(place[0] == place[2] - 1)(lambda: x_edge(x_high, NX - 1))

    def speed_of(k):
        def speed_at(i, q):
            inverse = reciprocal(q[0])
            return jnp.abs(q[1 + k]) * inverse + sound_of(q, inverse)

        return speed_at

    def along_x(step, _):
        start = pl.multiple_of(step * 8, 8)

        def load(f, i):
            if i < 0:
                return x_low[pl.ds(pl.multiple_of((f * 3 + i + 3) * NY + start, 8), 8), :]
            if i >= NX:
                return x_high[pl.ds(pl.multiple_of((f * 3 + i - NX) * NY + start, 8), 8), :]
            return state[pl.ds(pl.multiple_of(f * ROWS + i * NY + start, 8), 8), :]

        def store(i, values):
            for f in range(5):
                by_x[pl.ds(pl.multiple_of((f * 6 + (i if i < 3 else i - 10)) * NY + start, 8), 8), :] = values[f]

        sweep(load, speed_of(0), store, 0, 3, 0)
        sweep(load, speed_of(0), store, NX - 3, NX, 0)
        return 0

    lax.fori_loop(0, NY // 8, along_x, 0)

    for f in range(5):
        for x in range(NX):
            for side, y in ((0, 0), (8, NY - 8)):
                row = (f * NX + x) * RIM + side
                rims[row : row + 8, :] = state[f * ROWS + x * NY + y : f * ROWS + x * NY + y + 8, :]
                by_y[row : row + 8, :] = jnp.zeros((8, 128), F32)
    sides(y_one, y_two, y_low, y_high, place[1])

    def y_edge(beyond, row):
        for f in range(5):
            cells = rims[pl.ds(f * NX * RIM + row, NX, stride=RIM), :]
            for layer in range(3):
                beyond[pl.ds(f * NX * 3 + layer, NX, stride=3), :] = cells

    pl.when(place[1] == 0)(lambda: y_edge(y_low, 0))
    pl.when(place[1] == place[3] - 1)(lambda: y_edge(y_high, 15))

    def along_y(step, _):
        start = pl.multiple_of(step * 8, 8)

        def rows(f, i):
            return pl.ds((f * NX + start) * RIM + (i if i < 8 else i - 16), 8, stride=RIM)

        def load(f, i):
            if i < 0:
                return y_low[pl.ds((f * NX + start) * 3 + i + 3, 8, stride=3), :]
            if i >= NY:
                return y_high[pl.ds((f * NX + start) * 3 + i - NY, 8, stride=3), :]
            return rims[rows(f, i), :]

        def store(i, values):
            for f in range(5):
                by_y[rows(f, i), :] = values[f]

        sweep(load, speed_of(1), store, 0, 3, 1)
        sweep(load, speed_of(1), store, NY - 3, NY, 1)
        return 0

    lax.fori_loop(0, NX // 8, along_y, 0)

    for f in range(5):
        for x in range(NX):
            for y in range(0, NY, 8):
                row = f * ROWS + x * NY + y
                total = inner[row : row + 8, :]
                if x < 3 or x >= NX - 3:
                    at = (f * 6 + (x if x < 3 else x - 10)) * NY + y
                    total = total + by_x[at : at + 8, :]
                if y in (0, NY - 8):
                    at = (f * NX + x) * RIM + (0 if y == 0 else 8)
                    total = total + by_y[at : at + 8, :]
                out[row : row + 8, :] = total


def update_kernel(
    place, state, twice, uses_fine, uses_coarse, got, own, beside, new, gravity, around, field, made, pulls, written
):
    result, time_step = far_fields(place, uses_fine, uses_coarse, got, own, beside, around)
    half_step = 0.5 * time_step
    source = iota((8, 128), 0) * 16 + iota((8, 128), 1) // 8
    lines = [
        jnp.take_along_axis(jnp.broadcast_to(each, (8, 128)), source, axis=1, mode="promise_in_bounds") for each in result
    ]
    offset_z = (iota((8, 128), 1) % 8).astype(F32) - 3.5
    for i in range(3):
        field[i * 8 : i * 8 + 8, :] = lines[i] + lines[3 + sym(i, 2)] * offset_z
        field[(3 + i) * 8 : (3 + i) * 8 + 8, :] = lines[3 + sym(i, 0)]
        field[(6 + i) * 8 : (6 + i) * 8 + 8, :] = lines[3 + sym(i, 1)]
    offset_y = iota((8, 128), 0).astype(F32) - 3.5

    def writes(part):
        rows = pl.ds(part * 4, 4)
        return [
            pltpu.make_async_copy(made.at[:, rows, :, :], new.at[:, rows, :, :], written.at[0, part]),
            pltpu.make_async_copy(pulls.at[:, rows, :, :], gravity.at[:, rows, :, :], written.at[1, part]),
        ]

    lines = {}
    for x in range(NX):
        for ty in range(4):
            tx, y = x // 8, ty * 8
            if x % 8 == 0:
                at = [field[e * 8 + tx * 4 + ty : e * 8 + tx * 4 + ty + 1, :] for e in range(9)]
                lines[ty] = ([at[e] + at[6 + e] * offset_y for e in range(3)], at[3:6])
            base, slope = lines[ty]
            q = [state[f * ROWS + x * NY + y : f * ROWS + x * NY + y + 8, :] for f in range(5)]
            pull = [base[e] + slope[e] * (x % 8 - 3.5) for e in range(3)]
            moved = []
            for f in range(5):
                total = twice[f * ROWS + x * NY + y : f * ROWS + x * NY + y + 8, :]
                moved.append(q[f] - half_step * total)
            weight = time_step * q[0]
            gain = q[1] * pull[0] + q[2] * pull[1] + q[3] * pull[2]
            made[0, x, y : y + 8, :] = moved[0]
            for e in range(3):
                pulls[e, x, y : y + 8, :] = pull[e]
                made[1 + e, x, y : y + 8, :] = moved[1 + e] + weight * pull[e]
            made[4, x, y : y + 8, :] = moved[4] + time_step * gain
        if x % 4 == 3:
            for copy in writes(x // 4):
                copy.start()
    for part in range(4):
        for copy in writes(part):
            copy.wait()


VMEM = pl.BlockSpec(memory_space=pltpu.VMEM)
SMEM = pl.BlockSpec(memory_space=pltpu.SMEM)
FAR = pl.BlockSpec(memory_space=pltpu.HBM)
LIMIT = pltpu.CompilerParams(vmem_limit_bytes=12 * 1024 * 1024)
SMALL = pl.CostEstimate(flops=1000, bytes_accessed=1000, transcendentals=0)


def far(values):
    return pltpu.with_memory_space_constraint(values, pltpu.HBM)


def call(kernel, outs, scratch, *args, sources=None, far_outs=(), whole_numbers=()):
    shapes = [(o, 128) if isinstance(o, int) else o for o in outs]
    return pl.pallas_call(
        kernel,
        out_shape=[
            pltpu.HBM(s, F32) if n in far_outs else jax.ShapeDtypeStruct(s, jnp.int32 if n in whole_numbers else F32)
            for n, s in enumerate(shapes)
        ],
        in_specs=[SMEM] + (sources or [VMEM] * (len(args) - 1)),
        out_specs=[FAR if n in far_outs else VMEM for n in range(len(outs))],
        scratch_shapes=[pltpu.VMEM((s, 128), F32) if isinstance(s, int) else s for s in scratch],
        compiler_params=LIMIT,
        cost_estimate=SMALL,
    )(*args)


def local(state, fine_pairs, fine_count, coarse_pairs):
    mortons, octs = lax.axis_size("morton"), lax.axis_size("oct")
    place = jnp.stack([lax.axis_index("morton"), lax.axis_index("oct"), mortons, octs]).astype(jnp.int32)
    many = NX * PITCH

    def swap(values, pair):
        pairs = [(m, o) for m in range(mortons) for o in range(octs)]
        index = lambda place: place[0] * octs + place[1]
        return lax.ppermute(values, AXES, [(index(p), index(pair(*p))) for p in pairs])

    def other(i):
        return (i - 1 ^ 1) + 1

    block = pltpu.VMEM((5, ROWS, 128), F32)
    sent, x_one, x_two, y_one, y_two, own = call(
        moments_kernel, [128 * SENT, LONG, LONG, 240, 240, 8],
        [block, pltpu.SemaphoreType.DMA((4,))], place, far(state.reshape(5, ROWS, 128)), sources=[FAR],
    )
    got = lax.all_to_all(sent.reshape(mortons * octs, 1, SENT * 128), AXES[::-1], 0, 0, tiled=True)
    x_one = swap(x_one, lambda m, o: (other(m), o) if 0 < m < mortons - 1 else (m, o ^ 1))
    x_two = swap(x_two, lambda m, o: (m ^ 1, o))
    y_one = swap(y_one, lambda m, o: (m, o ^ 1))
    y_two = swap(y_two, lambda m, o: (m, other(o)) if 0 < o < octs - 1 else (m, octs - 1 - o))
    rows = state.reshape(5 * ROWS, 128)
    rows, sent = lax.optimization_barrier((rows, sent))
    inner, uses_fine, uses_coarse = call(
        inner_kernel, [5 * ROWS, 32, 64],
        [5 * TALL, 5 * TALL, 640, 640, 5 * many, many, many, 5 * many, pltpu.VMEM((128, 32), jnp.int32),
         pltpu.VMEM((8, 16), jnp.int32), pltpu.VMEM((16, 32), jnp.int32), pltpu.SemaphoreType.DMA((3,))],
        place, rows, far(fine_pairs.reshape(128, 32)), far(fine_count.reshape(8, 16)), far(coarse_pairs.reshape(16, 32)),
        sources=[VMEM, FAR, FAR, FAR], whole_numbers=(1, 2),
    )
    rim = 5 * NX * RIM
    twice, beside = call(
        edge_kernel, [5 * ROWS, 16], [480, 480, 240, 240, rim, 960, rim],
        place, rows, inner, x_one, x_two, y_one, y_two,
    )
    return call(
        update_kernel, [(5, NX, NY, NZ), (3, NX, NY, NZ)],
        [160, 72, pltpu.VMEM((5, NX, NY, NZ), F32), pltpu.VMEM((3, NX, NY, NZ), F32), pltpu.SemaphoreType.DMA((2, 4))],
        place, rows, twice, uses_fine, uses_coarse, got.reshape(mortons * octs * SENT, 128), own, beside,
        far_outs=range(2),
    )


def solution(mesh):
    in_specs = (
        P(None, "morton", "oct", None),
        P("morton", "oct", None, None),
        P("morton", "oct", None),
        P("morton", "oct", None, None),
    )
    out_specs = (P(None, "morton", "oct", None), P(None, "morton", "oct", None))
    return jax.shard_map(local, mesh=mesh, in_specs=in_specs, out_specs=out_specs, check_vma=False)
```

```python
import functools

import functools

import jax
import jax.numpy as jnp
from jax import lax
from jax.experimental import pallas as pl
from jax.experimental.pallas import tpu as pltpu
from jax.sharding import PartitionSpec as P

ADIABATIC = 5.0 / 3.0
COURANT = 0.2
GRAVITY = 1.0
AXES = ("morton", "oct")
F32 = jnp.float32
HIGH = lax.Precision.HIGHEST

NX, NY, NZ = 16, 32, 128
ROWS = NX * NY
PITCH = 33
TALL = 144
LONG = 488
RIM = 17
SENT = 3
SYM = ((0, 0), (0, 1), (0, 2), (1, 1), (1, 2), (2, 2))


def iota(shape, dim):
    return lax.broadcasted_iota(jnp.int32, shape, dim)


def sym(i, j):
    return SYM.index((min(i, j), max(i, j)))


def reciprocal(x):
    return pl.reciprocal(x, approx=True)


def sound_of(q, inverse):
    kinetic = (q[1] * q[1] + q[2] * q[2] + q[3] * q[3]) * inverse
    pressure = (2.0 / 3.0) * q[4] - (1.0 / 3.0) * kinetic
    square = ADIABATIC * pressure * inverse
    return square * lax.rsqrt(square)


def here():
    return [of(axis) for of in (lax.axis_index, lax.axis_size) for axis in AXES]


def fold_rows(values, group):
    keep = iota(values.shape, 1) // group == iota(values.shape, 0)
    return jnp.sum(jnp.where(keep, values, 0.0), axis=0, keepdims=True)


def moments_kernel(
    state, sent, x_one, x_two, y_one, y_two, own, rows, arrived
):
    place = here()
    part = ROWS // 4
    copies = [
        pltpu.make_async_copy(
            state.at[:, pl.ds(c * part, part), :], rows.at[:, pl.ds(c * part, part), :], arrived.at[c]
        )
        for c in range(4)
    ]
    even, oct_even = place[0] % 2 == 0, place[1] % 2 == 0
    x_starts = (jnp.where(even, 0, NX - 3), jnp.where(even, NX - 3, 0))
    y_starts = (jnp.where(oct_even, NY - 3, 0), jnp.where(oct_even, 0, NY - 3))
    for copy in copies:
        copy.start()
    offset_y = iota((8, 128), 0).astype(F32) - 3.5
    fastest = jnp.zeros((8, 128), F32)
    sums, sums_x, sums_y = [], [], []
    for tx in range(2):
        totals, totals_x = [jnp.zeros((8, 128), F32)] * 4, [jnp.zeros((8, 128), F32)] * 4
        for half in range(2):
            copies[tx * 2 + half].wait()
            for x in range(half * 4, half * 4 + 4):
                for ty in range(4):
                    row = (tx * 8 + x) * NY + ty * 8
                    q = [rows[f, row : row + 8, :] for f in range(5)]
                    inverse = reciprocal(q[0])
                    speed_of_sound = sound_of(q, inverse)
                    largest = jnp.maximum(jnp.maximum(jnp.abs(q[1]), jnp.abs(q[2])), jnp.abs(q[3]))
                    fastest = jnp.maximum(fastest, largest * inverse + speed_of_sound)
                    totals[ty] = totals[ty] + q[0]
                    totals_x[ty] = totals_x[ty] + q[0] * (x - 3.5)
        for ty in range(4):
            sums.append(jnp.sum(totals[ty], axis=0, keepdims=True))
            sums_x.append(jnp.sum(totals_x[ty], axis=0, keepdims=True))
            sums_y.append(jnp.sum(totals[ty] * offset_y, axis=0, keepdims=True))
    for out, start in ((x_one, x_starts[0]), (x_two, x_starts[1])):
        for f in range(5):
            out[f * 96 : f * 96 + 96, :] = rows[f, pl.ds(pl.multiple_of(start * NY, 32), 96), :]
    for out, start in ((y_one, y_starts[0]), (y_two, y_starts[1])):
        for f in range(5):
            for x in range(NX):
                row = (f * NX + x) * 3
                out[row : row + 3, :] = rows[f, pl.ds(x * NY + start, 3), :]
    parents = []
    for py in range(2):
        children = [(tx, ty) for tx in range(2) for ty in (2 * py, 2 * py + 1)]
        terms = [[], [], []]
        for tx, ty in children:
            n = tx * 4 + ty
            terms[0].append(sums[n])
            terms[1].append(sums_x[n] + (8.0 * tx - 4.0) * sums[n])
            terms[2].append(sums_y[n] + (8.0 * (ty % 2) - 4.0) * sums[n])
        parents.append([(t[0] + t[1]) + (t[2] + t[3]) for t in terms])
    parents = [parents[py][m] for m in range(3) for py in range(2)]
    lines = jnp.concatenate(sums + sums_x + sums_y + parents + [jnp.zeros((2, 128), F32)], axis=0)
    z, lanes = iota((128, 128), 0), iota((128, 128), 1)
    pick = (z // 8 == lanes % 16).astype(F32)
    pick_parent = (z // 16 == lanes % 8).astype(F32)
    picks = [
        pick, pick * ((z % 8).astype(F32) - 3.5), pick_parent, pick_parent * ((z % 16).astype(F32) - 7.5)
    ]
    folded = jnp.dot(lines, jnp.concatenate(picks, axis=1), precision=HIGH, preferred_element_type=F32)
    mass = fold_rows(folded[0:8, 0:128], 16)
    dipole = [
        fold_rows(folded[8:16, 0:128], 16), fold_rows(folded[16:24, 0:128], 16), fold_rows(folded[0:8, 128:256], 16)
    ]
    lane = iota((1, 128), 1)
    families = jnp.concatenate([folded[24:30, 256:384], folded[24:26, 384:512]], axis=0)
    last = jnp.where(lane < 64, fold_rows(families, 8), jnp.max(fastest))
    own[...] = jnp.concatenate([mass] + dipole + [jnp.zeros((4, 128), F32)], axis=0)
    x_one[480:488, :] = own[...]
    x_two[480:488, :] = own[...]
    patterns = []
    for side in range(2):
        packed = [
            jnp.where(lane < 32, pltpu.roll(v, (-32 * side) % 128, 1), pltpu.roll(v, (-32 - 32 * side) % 128, 1))
            for v in [mass] + dipole
        ]
        pairs = [jnp.where(lane < 64, packed[m], pltpu.roll(packed[m + 1], 64, 1)) for m in (0, 2)]
        patterns.append(jnp.concatenate([last] + pairs, axis=0))
    patterns = [jnp.concatenate([p] * 8, axis=0) for p in patterns]
    for octant in range(4):
        chosen = jnp.where(octant > place[1], patterns[1], patterns[0])
        for part in range(4):
            row = octant * 96 + part * 24
            sent[row : row + 24, :] = chosen


def rise(before, here, after):
    value = 0.5 * here + (1.0 / 12.0) * (before - after)
    return jnp.minimum(jnp.maximum(value, jnp.minimum(here, 0.0)), jnp.maximum(here, 0.0))


def upper_and_lower(centre, up, down):
    most_up, most_down = jnp.abs(down + down), jnp.abs(up + up)
    upper = centre + jnp.minimum(jnp.maximum(up, -most_up), most_up)
    lower = centre + jnp.minimum(jnp.maximum(down, -most_down), most_down)
    return upper, lower


def flux_of(q, k):
    inverse = reciprocal(q[0])
    velocity = q[1 + k] * inverse
    kinetic = (q[1] * q[1] + q[2] * q[2] + q[3] * q[3]) * inverse
    pressure = (2.0 / 3.0) * q[4] - (1.0 / 3.0) * kinetic
    out = [q[1 + k]] + [q[1 + c] * velocity for c in range(3)] + [(q[4] + pressure) * velocity]
    out[1 + k] = out[1 + k] + pressure
    return out


def twice_flux(left, right, speed, k):
    from_left, from_right = flux_of(left, k), flux_of(right, k)
    return [
        (a + b) - speed * (r - l) for a, b, l, r in zip(from_left, from_right, left, right, strict=True)
    ]


def sweep(load, speed_at, store, begin, end, k, beside=()):
    beside = list(beside)
    share = -(-len(beside) // (end - begin))
    start = [[load(f, begin + i) for f in range(5)] for i in (-3, -2, -1)]
    steps = [[b - a for a, b in zip(start[i], start[i + 1], strict=True)] for i in range(2)]
    cell = start[1], start[2]
    ups = upper_old = speed_old = flux_old = None
    for i in range(begin - 2, end + 1):
        ahead = [load(f, i + 2) for f in range(5)]
        steps.append([a - b for a, b in zip(ahead, cell[1], strict=True)])
        now = [rise(*each) for each in zip(*steps, strict=True)]
        if ups is not None:
            downs = [u - d for u, d in zip(ups, steps[0], strict=True)]
            pairs = [upper_and_lower(*each) for each in zip(cell[0], now, downs, strict=True)]
            upper, lower = [p[0] for p in pairs], [p[1] for p in pairs]
            speed = speed_at(i, cell[0])
            if upper_old is not None:
                flux = twice_flux(upper_old, lower, jnp.maximum(speed_old, speed), k)
                if flux_old is not None:
                    store(i - 1, [a - b for a, b in zip(flux, flux_old, strict=True)])
                flux_old = flux
            upper_old, speed_old = upper, speed
        for call in beside[:share]:
            call()
        beside = beside[share:]
        ups, cell, steps = now, (cell[1], ahead), steps[1:]
    for call in beside:
        call()


def sides(one, two, low, high, rank):
    even = rank % 2 == 0
    for row in range(0, low.shape[0], 8):
        a, b = one[row : row + 8, :], two[row : row + 8, :]
        low[row : row + 8, :] = jnp.where(even, b, a)
        high[row : row + 8, :] = jnp.where(even, a, b)


def inner_kernel(
    state, far_pairs, far_count, far_coarse, out, fine_uses, coarse_uses,
    turned_even, turned_odd, changes_even, changes_odd, padded, inverse_of, sound, by_y,
    fine_pairs, fine_count, coarse_pairs, arrived,
):
    place = here()
    turned, changes = (turned_even, turned_odd), (changes_even, changes_odd)

    def turn(block, f):
        into, base = turned[block % 2], f * TALL
        flat = state[f * ROWS + block * 128 : f * ROWS + block * 128 + 128, :].T
        into[base + 8 : base + 136, :] = flat
        into[base : base + 8, :] = jnp.broadcast_to(flat[0:1], (8, 128))
        into[base + 136 : base + 144, :] = jnp.broadcast_to(flat[127:128], (8, 128))

    def turn_back(block, f):
        flat = changes[block % 2][f * 128 : f * 128 + 128, :]
        out[f * ROWS + block * 128 : f * ROWS + block * 128 + 128, :] = flat.T

    def along_z(block, beside):
        source, into = turned[block % 2], changes[block % 2]

        def load(f, i):
            return source[pl.ds(f * TALL + 8 + i, 8, stride=16), :]

        def speed_at(i, q):
            inverse = reciprocal(q[0])
            return jnp.abs(q[3]) * inverse + sound_of(q, inverse)

        def store(i, values):
            for f in range(5):
                into[pl.ds(f * 128 + i, 8, stride=16), :] = values[f]

        sweep(load, speed_at, store, 0, 16, 2, beside)

    reads = [
        pltpu.make_async_copy(source, into, arrived.at[n])
        for n, (source, into) in enumerate(
            ((far_pairs, fine_pairs), (far_count, fine_count), (far_coarse, coarse_pairs))
        )
    ]
    for copy in reads:
        copy.start()
    for f in range(5):
        turn(0, f)
    for block in range(4):
        beside = []
        for f in range(5):
            if block < 3:
                beside.append(functools.partial(turn, block + 1, f))
            if block > 0:
                beside.append(functools.partial(turn_back, block - 1, f))
        along_z(block, beside)
    for f in range(5):
        turn_back(3, f)
    for copy in reads:
        copy.wait()
    codes = jnp.concatenate([fine_pairs[...].astype(F32)] * 4, axis=1).T[0:32]
    spread = (iota((16, 128), 1) % 16 == iota((16, 128), 0)).astype(F32)
    used = fold_rows(
        jnp.dot(fine_count[...].astype(F32), spread, precision=HIGH, preferred_element_type=F32), 16
    )
    codes = jnp.where(iota((32, 128), 0).astype(F32) < used, codes, 1000.0)
    along = jnp.floor((codes + 0.5) * 0.04)
    plane = codes - 25.0 * along
    group = jnp.floor((plane + 0.5) * 0.2)
    one = jnp.left_shift(1, (6.0 * (plane - 5.0 * group)).astype(jnp.int32))
    ones = [jnp.where(group == g, one, 0) for g in range(5)]
    fine_uses[24:32, :] = jnp.zeros((8, 128), jnp.int32)
    for g in range(5):
        lines = []
        for ox in range(5):
            hits = jnp.where(along == ox, ones[g], 0)
            hits = (hits[0:8] + hits[8:16]) + (hits[16:24] + hits[24:32])
            lines.append(jnp.sum(hits, axis=0, keepdims=True))
        fine_uses[g * 5 : g * 5 + 5, :] = jnp.concatenate(lines, axis=0)

    slot = iota((8, 128), 1)
    device = slot % place[2] * place[3] + slot // place[2]
    for half in range(2):
        named = coarse_pairs[half * 8 : half * 8 + 8, :]
        coded = named // 16 + named % 4 * (6 * 256) + named // 4 % 4 * 65536
        counts = [jnp.zeros((8, 128), jnp.int32) for _ in range(4)]
        for j in range(32):
            code = jnp.broadcast_to(coded[:, j : j + 1], (8, 128))
            one = jnp.where((code & 255) == device, jnp.left_shift(1, (code >> 8) & 255), 0)
            group = code >> 16
            counts = [each + jnp.where(group == g, one, 0) for g, each in enumerate(counts)]
        for g in range(4):
            coarse_uses[(g * 2 + half) * 8 : (g * 2 + half) * 8 + 8, :] = counts[g]
    for x in range(NX):
        for y in range(0, NY, 8):
            row = x * NY + y
            q = [state[f * ROWS + row : f * ROWS + row + 8, :] for f in range(5)]
            inverse = reciprocal(q[0])
            at = x * PITCH + y
            for f in range(5):
                padded[f * NX * PITCH + at : f * NX * PITCH + at + 8, :] = q[f]
            inverse_of[at : at + 8, :] = inverse
            sound[at : at + 8, :] = sound_of(q, inverse)

    def along_x(step, _):
        start = pl.multiple_of(step * 8, 8)

        def rows(f, i):
            return pl.ds(pl.multiple_of(f * ROWS + i * NY + start, 8), 8)

        def speed_at(i, q):
            at = pl.ds(i * PITCH + start, 8)
            return jnp.abs(q[1]) * inverse_of[at, :] + sound[at, :]

        def store(i, values):
            for f in range(5):
                out[rows(f, i), :] = out[rows(f, i), :] + values[f]

        sweep(lambda f, i: state[rows(f, i), :], speed_at, store, 3, NX - 3, 0)
        return 0

    lax.fori_loop(0, NY // 8, along_x, 0)

    def along_y(step, _):
        start = pl.multiple_of(step * 8, 8)

        def rows(f, i):
            return pl.ds((f * NX + start) * PITCH + i, 8, stride=PITCH)

        def speed_at(i, q):
            return jnp.abs(q[2]) * inverse_of[rows(0, i), :] + sound[rows(0, i), :]

        def store(i, values):
            for f in range(5):
                by_y[rows(f, i), :] = values[f]

        for i in (0, 1, 2, NY - 3, NY - 2, NY - 1):
            store(i, [jnp.zeros((8, 128), F32)] * 5)
        sweep(lambda f, i: padded[rows(f, i), :], speed_at, store, 3, NY - 3, 1)
        return 0

    lax.fori_loop(0, NX // 8, along_y, 0)

    def total(x, _):
        for f in range(5):
            for y in range(0, NY, 8):
                row = pl.ds(pl.multiple_of(f * ROWS + x * NY + y, 8), 8)
                out[row, :] = out[row, :] + by_y[pl.ds((f * NX + x) * PITCH + y, 8), :]
        return 0

    lax.fori_loop(0, NX, total, 0, unroll=2)


def tensors(r, square):
    root = lax.rsqrt(jnp.maximum(square, 1.0))
    cube = root * root * root
    three = 3.0 * cube * (root * root)
    scaled = [three * each for each in r]
    pull = [each * cube for each in r]
    tide = [scaled[i] * r[j] - cube if i == j else scaled[i] * r[j] for i, j in SYM]
    return pull, tide


def add_terms(totals, uses, r, square, mass, dipole):
    pull, tide = tensors(r, square)
    mass = uses * mass
    dipole = [uses * d for d in dipole]
    for i in range(3):
        term = mass * pull[i]
        for j in range(3):
            term = term - tide[sym(i, j)] * dipole[j]
        totals[i] = totals[i] + term
    for e in range(6):
        totals[3 + e] = totals[3 + e] + mass * tide[e]


def far_fields(place, uses_fine, uses_coarse, got, own, beside, around):
    morton, octant = place[0], place[1]
    mortons, octs = place[2], place[3]
    lane = iota((8, 128), 1)
    lane_row = iota((1, 128), 1)

    rows = jnp.concatenate([got[pl.ds(g * 8 * SENT, 8, stride=SENT), :] for g in range(16)], axis=0)
    time_step = COURANT / jnp.max(rows[:, 64:128])
    moments = rows.T
    target_z = iota((8, 128), 0)
    rx = 16.0 * (lane % mortons - morton).astype(F32)
    coarse = []
    for half in range(2):
        totals = [jnp.zeros((8, 128), F32) for _ in range(9)]
        for lp in range(16):
            ry = 16.0 * (lane // mortons * 2 + lp // 8 - (2 * octant + half)).astype(F32)
            rz = 16.0 * (lp % 8 - target_z).astype(F32)
            families = [jnp.broadcast_to(moments[m * 16 + lp : m * 16 + lp + 1], (8, 128)) for m in range(4)]
            row = (lp // 4 * 2 + half) * 8
            uses = ((uses_coarse[row : row + 8, :] >> (lp % 4 * 6)) & 63).astype(F32)
            add_terms(totals, uses, (rx, ry, rz), rx * rx + ry * ry + rz * rz, families[0], families[1:])
        coarse.append([jnp.sum(each, axis=1, keepdims=True) for each in totals])
    result = []
    for e in range(9):
        column = jnp.where(lane // 32 % 2 == 0, coarse[0][e], coarse[1][e])
        column = jnp.where(lane % 16 // 2 == iota((8, 128), 0), column, 0.0)
        result.append(jnp.sum(column, axis=0, keepdims=True))
    side = [4.0 * (2 * s - 1).astype(F32) for s in (lane_row // 64, lane_row // 16 % 2, lane_row % 2)]
    for i in range(3):
        for j in range(3):
            result[i] = result[i] + result[3 + sym(i, j)] * side[j]

    def inside(dx, dy):
        at_x, at_y = morton + dx, octant + dy
        return (at_x >= 0) & (at_x < mortons) & (at_y >= 0) & (at_y < octs)

    blocks = []
    for dy in (-1, 0, 1):
        block = []
        if dy:
            halves = []
            for dx in (-1, 0, 1):
                device = jnp.clip(octant + dy, 0, octs - 1) * mortons + jnp.clip(morton + dx, 0, mortons - 1)
                for n in (1, 2):
                    halves.append(jnp.where(inside(dx, dy), got[pl.ds(device * SENT + n, 1), :], 0.0))
            halves = jnp.concatenate(halves + [jnp.zeros((2, 128), F32)], axis=0)
            back = 32 if dy < 0 else 0
            unpacked = [
                jnp.where(lane < 64, pltpu.roll(each, back, 1), pltpu.roll(each, 32 + back, 1)) if back
                else jnp.where(lane < 64, each, pltpu.roll(each, 32, 1))
                for each in (halves, pltpu.roll(halves, 64, 1))
            ]
            for n in range(6):
                block += [unpacked[0][n : n + 1], unpacked[1][n : n + 1]]
        else:
            for dx, source in ((-1, beside[0:4, :]), (0, own[0:4, :]), (1, beside[8:12, :])):
                block.append(jnp.where(inside(dx, 0), source, 0.0))
        blocks.append(jnp.concatenate(block + [jnp.zeros((4, 128), F32)], axis=0))
    wide = iota((16, 128), 1)
    around[...] = jnp.zeros(around.shape, F32)
    for oy in range(-2, 3):
        if oy == 0:
            moved = blocks[1]
        else:
            moved = pltpu.roll(blocks[1], (-16 * oy) % 128, 1)
            if oy > 0:
                moved = jnp.where(wide // 16 % 4 + oy > 3, pltpu.roll(blocks[2], (64 - 16 * oy) % 128, 1), moved)
            else:
                moved = jnp.where(wide // 16 % 4 + oy < 0, pltpu.roll(blocks[0], (-64 - 16 * oy) % 128, 1), moved)
        swapped = pltpu.roll(moved, 64, 1)
        for m in range(4):
            low, own, high = [(moved[d * 4 + m : d * 4 + m + 1], swapped[d * 4 + m : d * 4 + m + 1]) for d in range(3)]
            first = lane_row < 64
            lines = [
                low[0], jnp.where(first, low[1], own[1]), own[0], jnp.where(first, own[1], high[1]), high[0],
            ]
            row = (m * 5 + oy + 2) * 8
            around[row : row + 5, :] = jnp.concatenate(lines, axis=0)
    totals = [jnp.zeros((8, 128), F32) for _ in range(9)]
    rx = 8.0 * (iota((8, 128), 0) - 2).astype(F32)
    square_x = rx * rx
    for oy in range(-2, 3):
        base = [around[(m * 5 + oy + 2) * 8 : (m * 5 + oy + 2) * 8 + 8, :] for m in range(4)]
        for oz in range(-2, 3):
            moved = base
            if oz:
                ok = (lane % 16 + oz >= 0) & (lane % 16 + oz < 16)
                moved = [jnp.where(ok, pltpu.roll(each, (-oz) % 128, 1), 0.0) for each in base]
            uses = ((uses_fine[(oy + 2) * 5 : (oy + 2) * 5 + 8, :] >> ((oz + 2) * 6)) & 63).astype(F32)
            add_terms(
                totals, uses, (rx, 8.0 * oy, 8.0 * oz),
                square_x + (64.0 * oy * oy + 64.0 * oz * oz), moved[0], moved[1:],
            )
    for e in range(9):
        result[e] = GRAVITY * (result[e] + jnp.sum(totals[e], axis=0, keepdims=True))
    return result, time_step


def edge_kernel(
    state, inner, x_one, x_two, y_one, y_two, out, beside,
    x_low, x_high, y_low, y_high, rims, by_x, by_y,
):
    place = here()
    sides(x_two, x_one, x_low, x_high, place[0])
    even = place[0] % 2 == 0
    moments = x_one[480:488, :], x_two[480:488, :]
    beside[0:8, :] = jnp.where(even, moments[0], moments[1])
    beside[8:16, :] = jnp.where(even, moments[1], moments[0])

    def x_edge(beyond, x):
        for f in range(5):
            cells = state[f * ROWS + x * NY : f * ROWS + x * NY + NY, :]
            for layer in range(3):
                beyond[(f * 3 + layer) * NY : (f * 3 + layer) * NY + NY, :] = cells

    pl.when(place[0] == 0)(lambda: x_edge(x_low, 0))
    pl.when(place[0] == place[2] - 1)(lambda: x_edge(x_high, NX - 1))

    def speed_of(k):
        def speed_at(i, q):
            inverse = reciprocal(q[0])
            return jnp.abs(q[1 + k]) * inverse + sound_of(q, inverse)

        return speed_at

    def along_x(step, _):
        start = pl.multiple_of(step * 8, 8)

        def load(f, i):
            if i < 0:
                return x_low[pl.ds(pl.multiple_of((f * 3 + i + 3) * NY + start, 8), 8), :]
            if i >= NX:
                return x_high[pl.ds(pl.multiple_of((f * 3 + i - NX) * NY + start, 8), 8), :]
            return state[pl.ds(pl.multiple_of(f * ROWS + i * NY + start, 8), 8), :]

        def store(i, values):
            for f in range(5):
                by_x[pl.ds(pl.multiple_of((f * 6 + (i if i < 3 else i - 10)) * NY + start, 8), 8), :] = values[f]

        sweep(load, speed_of(0), store, 0, 3, 0)
        sweep(load, speed_of(0), store, NX - 3, NX, 0)
        return 0

    lax.fori_loop(0, NY // 8, along_x, 0)

    for f in range(5):
        for x in range(NX):
            for side, y in ((0, 0), (8, NY - 8)):
                row = (f * NX + x) * RIM + side
                rims[row : row + 8, :] = state[f * ROWS + x * NY + y : f * ROWS + x * NY + y + 8, :]
                by_y[row : row + 8, :] = jnp.zeros((8, 128), F32)
    sides(y_one, y_two, y_low, y_high, place[1])

    def y_edge(beyond, row):
        for f in range(5):
            cells = rims[pl.ds(f * NX * RIM + row, NX, stride=RIM), :]
            for layer in range(3):
                beyond[pl.ds(f * NX * 3 + layer, NX, stride=3), :] = cells

    pl.when(place[1] == 0)(lambda: y_edge(y_low, 0))
    pl.when(place[1] == place[3] - 1)(lambda: y_edge(y_high, 15))

    def along_y(step, _):
        start = pl.multiple_of(step * 8, 8)

        def rows(f, i):
            return pl.ds((f * NX + start) * RIM + (i if i < 8 else i - 16), 8, stride=RIM)

        def load(f, i):
            if i < 0:
                return y_low[pl.ds((f * NX + start) * 3 + i + 3, 8, stride=3), :]
            if i >= NY:
                return y_high[pl.ds((f * NX + start) * 3 + i - NY, 8, stride=3), :]
            return rims[rows(f, i), :]

        def store(i, values):
            for f in range(5):
                by_y[rows(f, i), :] = values[f]

        sweep(load, speed_of(1), store, 0, 3, 1)
        sweep(load, speed_of(1), store, NY - 3, NY, 1)
        return 0

    lax.fori_loop(0, NX // 8, along_y, 0)

    for f in range(5):
        for x in range(NX):
            for y in range(0, NY, 8):
                row = f * ROWS + x * NY + y
                total = inner[row : row + 8, :]
                if x < 3 or x >= NX - 3:
                    at = (f * 6 + (x if x < 3 else x - 10)) * NY + y
                    total = total + by_x[at : at + 8, :]
                if y in (0, NY - 8):
                    at = (f * NX + x) * RIM + (0 if y == 0 else 8)
                    total = total + by_y[at : at + 8, :]
                out[row : row + 8, :] = total


def update_kernel(
    state, twice, uses_fine, uses_coarse, got, own, beside, new, gravity, around, field, made, pulls, written
):
    place = here()
    result, time_step = far_fields(place, uses_fine, uses_coarse, got, own, beside, around)
    half_step = 0.5 * time_step
    source = iota((8, 128), 0) * 16 + iota((8, 128), 1) // 8
    lines = [
        jnp.take_along_axis(jnp.broadcast_to(each, (8, 128)), source, axis=1, mode="promise_in_bounds") for each in result
    ]
    offset_z = (iota((8, 128), 1) % 8).astype(F32) - 3.5
    for i in range(3):
        field[i * 8 : i * 8 + 8, :] = lines[i] + lines[3 + sym(i, 2)] * offset_z
        field[(3 + i) * 8 : (3 + i) * 8 + 8, :] = lines[3 + sym(i, 0)]
        field[(6 + i) * 8 : (6 + i) * 8 + 8, :] = lines[3 + sym(i, 1)]
    offset_y = iota((8, 128), 0).astype(F32) - 3.5

    def writes(part):
        rows = pl.ds(part * 4, 4)
        return [
            pltpu.make_async_copy(made.at[:, rows, :, :], new.at[:, rows, :, :], written.at[0, part]),
            pltpu.make_async_copy(pulls.at[:, rows, :, :], gravity.at[:, rows, :, :], written.at[1, part]),
        ]

    lines = {}
    for x in range(NX):
        for ty in range(4):
            tx, y = x // 8, ty * 8
            if x % 8 == 0:
                at = [field[e * 8 + tx * 4 + ty : e * 8 + tx * 4 + ty + 1, :] for e in range(9)]
                lines[ty] = ([at[e] + at[6 + e] * offset_y for e in range(3)], at[3:6])
            base, slope = lines[ty]
            q = [state[f * ROWS + x * NY + y : f * ROWS + x * NY + y + 8, :] for f in range(5)]
            pull = [base[e] + slope[e] * (x % 8 - 3.5) for e in range(3)]
            moved = []
            for f in range(5):
                total = twice[f * ROWS + x * NY + y : f * ROWS + x * NY + y + 8, :]
                moved.append(q[f] - half_step * total)
            weight = time_step * q[0]
            gain = q[1] * pull[0] + q[2] * pull[1] + q[3] * pull[2]
            made[0, x, y : y + 8, :] = moved[0]
            for e in range(3):
                pulls[e, x, y : y + 8, :] = pull[e]
                made[1 + e, x, y : y + 8, :] = moved[1 + e] + weight * pull[e]
            made[4, x, y : y + 8, :] = moved[4] + time_step * gain
        if x % 4 == 3:
            for copy in writes(x // 4):
                copy.start()
    for part in range(4):
        for copy in writes(part):
            copy.wait()


VMEM = pl.BlockSpec(memory_space=pltpu.VMEM)
FAR = pl.BlockSpec(memory_space=pltpu.HBM)
LIMIT = pltpu.CompilerParams(vmem_limit_bytes=12 * 1024 * 1024)
SMALL = pl.CostEstimate(flops=1000, bytes_accessed=1000, transcendentals=0)


def far(values):
    return pltpu.with_memory_space_constraint(values, pltpu.HBM)


def call(kernel, outs, scratch, *args, sources=None, far_outs=(), whole_numbers=()):
    shapes = [(o, 128) if isinstance(o, int) else o for o in outs]
    return pl.pallas_call(
        kernel,
        out_shape=[
            pltpu.HBM(s, F32) if n in far_outs else jax.ShapeDtypeStruct(s, jnp.int32 if n in whole_numbers else F32)
            for n, s in enumerate(shapes)
        ],
        in_specs=sources or [VMEM] * len(args),
        out_specs=[FAR if n in far_outs else VMEM for n in range(len(outs))],
        scratch_shapes=[pltpu.VMEM((s, 128), F32) if isinstance(s, int) else s for s in scratch],
        compiler_params=LIMIT,
        cost_estimate=SMALL,
    )(*args)


def local(state, fine_pairs, fine_count, coarse_pairs):
    mortons, octs = lax.axis_size("morton"), lax.axis_size("oct")
    many = NX * PITCH

    def swap(values, pair):
        pairs = [(m, o) for m in range(mortons) for o in range(octs)]
        index = lambda at: at[0] * octs + at[1]
        return lax.ppermute(values, AXES, [(index(p), index(pair(*p))) for p in pairs])

    def other(i):
        return (i - 1 ^ 1) + 1

    block = pltpu.VMEM((5, ROWS, 128), F32)
    sent, x_one, x_two, y_one, y_two, own = call(
        moments_kernel, [128 * SENT, LONG, LONG, 240, 240, 8],
        [block, pltpu.SemaphoreType.DMA((4,))], far(state.reshape(5, ROWS, 128)), sources=[FAR],
    )
    got = lax.all_to_all(sent.reshape(mortons * octs, 1, SENT * 128), AXES[::-1], 0, 0, tiled=True)
    x_one = swap(x_one, lambda m, o: (other(m), o) if 0 < m < mortons - 1 else (m, o ^ 1))
    x_two = swap(x_two, lambda m, o: (m ^ 1, o))
    y_one = swap(y_one, lambda m, o: (m, o ^ 1))
    y_two = swap(y_two, lambda m, o: (m, other(o)) if 0 < o < octs - 1 else (m, octs - 1 - o))
    rows = state.reshape(5 * ROWS, 128)
    rows, sent = lax.optimization_barrier((rows, sent))
    inner, uses_fine, uses_coarse = call(
        inner_kernel, [5 * ROWS, 32, 64],
        [5 * TALL, 5 * TALL, 640, 640, 5 * many, many, many, 5 * many, pltpu.VMEM((128, 32), jnp.int32),
         pltpu.VMEM((8, 16), jnp.int32), pltpu.VMEM((16, 32), jnp.int32), pltpu.SemaphoreType.DMA((3,))],
        rows, far(fine_pairs.reshape(128, 32)), far(fine_count.reshape(8, 16)), far(coarse_pairs.reshape(16, 32)),
        sources=[VMEM, FAR, FAR, FAR], whole_numbers=(1, 2),
    )
    rim = 5 * NX * RIM
    twice, beside = call(
        edge_kernel, [5 * ROWS, 16], [480, 480, 240, 240, rim, 960, rim],
        rows, inner, x_one, x_two, y_one, y_two,
    )
    return call(
        update_kernel, [(5, NX, NY, NZ), (3, NX, NY, NZ)],
        [160, 72, pltpu.VMEM((5, NX, NY, NZ), F32), pltpu.VMEM((3, NX, NY, NZ), F32), pltpu.SemaphoreType.DMA((2, 4))],
        rows, twice, uses_fine, uses_coarse, got.reshape(mortons * octs * SENT, 128), own, beside,
        far_outs=range(2),
    )


def solution(mesh):
    in_specs = (
        P(None, "morton", "oct", None),
        P("morton", "oct", None, None),
        P("morton", "oct", None),
        P("morton", "oct", None, None),
    )
    out_specs = (P(None, "morton", "oct", None), P(None, "morton", "oct", None))
    return jax.shard_map(local, mesh=mesh, in_specs=in_specs, out_specs=out_specs, check_vma=False)
```

```python
import functools

import functools

import jax
import jax.numpy as jnp
from jax import lax
from jax.experimental import pallas as pl
from jax.experimental.pallas import tpu as pltpu
from jax.sharding import PartitionSpec as P

ADIABATIC = 5.0 / 3.0
COURANT = 0.2
GRAVITY = 1.0
AXES = ("morton", "oct")
F32 = jnp.float32
HIGH = lax.Precision.HIGHEST

NX, NY, NZ = 16, 32, 128
ROWS = NX * NY
PITCH = 33
TALL = 144
LONG = 488
RIM = 17
SENT = 3
SYM = ((0, 0), (0, 1), (0, 2), (1, 1), (1, 2), (2, 2))


def iota(shape, dim):
    return lax.broadcasted_iota(jnp.int32, shape, dim)


def sym(i, j):
    return SYM.index((min(i, j), max(i, j)))


def reciprocal(x):
    return pl.reciprocal(x, approx=True)


def sound_of(q, inverse):
    kinetic = (q[1] * q[1] + q[2] * q[2] + q[3] * q[3]) * inverse
    pressure = (2.0 / 3.0) * q[4] - (1.0 / 3.0) * kinetic
    square = ADIABATIC * pressure * inverse
    return square * lax.rsqrt(square)


def here():
    return [of(axis) for of in (lax.axis_index, lax.axis_size) for axis in AXES]


def fold_rows(values, group):
    keep = iota(values.shape, 1) // group == iota(values.shape, 0)
    return jnp.sum(jnp.where(keep, values, 0.0), axis=0, keepdims=True)


def moments_kernel(
    state, sent, x_one, x_two, y_one, y_two, own, rows, arrived
):
    place = here()
    part = ROWS // 8
    copies = [
        pltpu.make_async_copy(
            state.at[:, pl.ds(c * part, part), :], rows.at[:, pl.ds(c * part, part), :], arrived.at[c]
        )
        for c in range(8)
    ]
    even, oct_even = place[0] % 2 == 0, place[1] % 2 == 0
    x_starts = (jnp.where(even, 0, NX - 3), jnp.where(even, NX - 3, 0))
    y_starts = (jnp.where(oct_even, NY - 3, 0), jnp.where(oct_even, 0, NY - 3))
    for copy in copies:
        copy.start()
    offset_y = iota((8, 128), 0).astype(F32) - 3.5
    fastest = jnp.zeros((8, 128), F32)
    sums, sums_x, sums_y = [], [], []
    for tx in range(2):
        totals, totals_x = [jnp.zeros((8, 128), F32)] * 4, [jnp.zeros((8, 128), F32)] * 4
        for half in range(4):
            copies[tx * 4 + half].wait()
            for x in range(half * 2, half * 2 + 2):
                for ty in range(4):
                    row = (tx * 8 + x) * NY + ty * 8
                    q = [rows[f, row : row + 8, :] for f in range(5)]
                    inverse = reciprocal(q[0])
                    speed_of_sound = sound_of(q, inverse)
                    largest = jnp.maximum(jnp.maximum(jnp.abs(q[1]), jnp.abs(q[2])), jnp.abs(q[3]))
                    fastest = jnp.maximum(fastest, largest * inverse + speed_of_sound)
                    totals[ty] = totals[ty] + q[0]
                    totals_x[ty] = totals_x[ty] + q[0] * (x - 3.5)
        for ty in range(4):
            sums.append(jnp.sum(totals[ty], axis=0, keepdims=True))
            sums_x.append(jnp.sum(totals_x[ty], axis=0, keepdims=True))
            sums_y.append(jnp.sum(totals[ty] * offset_y, axis=0, keepdims=True))
    for out, start in ((x_one, x_starts[0]), (x_two, x_starts[1])):
        for f in range(5):
            out[f * 96 : f * 96 + 96, :] = rows[f, pl.ds(pl.multiple_of(start * NY, 32), 96), :]
    for out, start in ((y_one, y_starts[0]), (y_two, y_starts[1])):
        for f in range(5):
            for x in range(NX):
                row = (f * NX + x) * 3
                out[row : row + 3, :] = rows[f, pl.ds(x * NY + start, 3), :]
    parents = []
    for py in range(2):
        children = [(tx, ty) for tx in range(2) for ty in (2 * py, 2 * py + 1)]
        terms = [[], [], []]
        for tx, ty in children:
            n = tx * 4 + ty
            terms[0].append(sums[n])
            terms[1].append(sums_x[n] + (8.0 * tx - 4.0) * sums[n])
            terms[2].append(sums_y[n] + (8.0 * (ty % 2) - 4.0) * sums[n])
        parents.append([(t[0] + t[1]) + (t[2] + t[3]) for t in terms])
    parents = [parents[py][m] for m in range(3) for py in range(2)]
    lines = jnp.concatenate(sums + sums_x + sums_y + parents + [jnp.zeros((2, 128), F32)], axis=0)
    z, lanes = iota((128, 128), 0), iota((128, 128), 1)
    pick = (z // 8 == lanes % 16).astype(F32)
    pick_parent = (z // 16 == lanes % 8).astype(F32)
    picks = [
        pick, pick * ((z % 8).astype(F32) - 3.5), pick_parent, pick_parent * ((z % 16).astype(F32) - 7.5)
    ]
    folded = jnp.dot(lines, jnp.concatenate(picks, axis=1), precision=HIGH, preferred_element_type=F32)
    mass = fold_rows(folded[0:8, 0:128], 16)
    dipole = [
        fold_rows(folded[8:16, 0:128], 16), fold_rows(folded[16:24, 0:128], 16), fold_rows(folded[0:8, 128:256], 16)
    ]
    lane = iota((1, 128), 1)
    families = jnp.concatenate([folded[24:30, 256:384], folded[24:26, 384:512]], axis=0)
    last = jnp.where(lane < 64, fold_rows(families, 8), jnp.max(fastest))
    own[...] = jnp.concatenate([mass] + dipole + [jnp.zeros((4, 128), F32)], axis=0)
    x_one[480:488, :] = own[...]
    x_two[480:488, :] = own[...]
    patterns = []
    for side in range(2):
        packed = [
            jnp.where(lane < 32, pltpu.roll(v, (-32 * side) % 128, 1), pltpu.roll(v, (-32 - 32 * side) % 128, 1))
            for v in [mass] + dipole
        ]
        pairs = [jnp.where(lane < 64, packed[m], pltpu.roll(packed[m + 1], 64, 1)) for m in (0, 2)]
        patterns.append(jnp.concatenate([last] + pairs, axis=0))
    patterns = [jnp.concatenate([p] * 8, axis=0) for p in patterns]
    for octant in range(4):
        chosen = jnp.where(octant > place[1], patterns[1], patterns[0])
        for part in range(4):
            row = octant * 96 + part * 24
            sent[row : row + 24, :] = chosen


def rise(before, here, after):
    value = 0.5 * here + (1.0 / 12.0) * (before - after)
    return jnp.minimum(jnp.maximum(value, jnp.minimum(here, 0.0)), jnp.maximum(here, 0.0))


def upper_and_lower(centre, up, down):
    most_up, most_down = jnp.abs(down + down), jnp.abs(up + up)
    upper = centre + jnp.minimum(jnp.maximum(up, -most_up), most_up)
    lower = centre + jnp.minimum(jnp.maximum(down, -most_down), most_down)
    return upper, lower


def flux_of(q, k):
    inverse = reciprocal(q[0])
    velocity = q[1 + k] * inverse
    kinetic = (q[1] * q[1] + q[2] * q[2] + q[3] * q[3]) * inverse
    pressure = (2.0 / 3.0) * q[4] - (1.0 / 3.0) * kinetic
    out = [q[1 + k]] + [q[1 + c] * velocity for c in range(3)] + [(q[4] + pressure) * velocity]
    out[1 + k] = out[1 + k] + pressure
    return out


def twice_flux(left, right, speed, k):
    from_left, from_right = flux_of(left, k), flux_of(right, k)
    return [
        (a + b) - speed * (r - l) for a, b, l, r in zip(from_left, from_right, left, right, strict=True)
    ]


def sweep(load, speed_at, store, begin, end, k, beside=()):
    beside = list(beside)
    share = -(-len(beside) // (end - begin))
    start = [[load(f, begin + i) for f in range(5)] for i in (-3, -2, -1)]
    steps = [[b - a for a, b in zip(start[i], start[i + 1], strict=True)] for i in range(2)]
    cell = start[1], start[2]
    ups = upper_old = speed_old = flux_old = None
    for i in range(begin - 2, end + 1):
        ahead = [load(f, i + 2) for f in range(5)]
        steps.append([a - b for a, b in zip(ahead, cell[1], strict=True)])
        now = [rise(*each) for each in zip(*steps, strict=True)]
        if ups is not None:
            downs = [u - d for u, d in zip(ups, steps[0], strict=True)]
            pairs = [upper_and_lower(*each) for each in zip(cell[0], now, downs, strict=True)]
            upper, lower = [p[0] for p in pairs], [p[1] for p in pairs]
            speed = speed_at(i, cell[0])
            if upper_old is not None:
                flux = twice_flux(upper_old, lower, jnp.maximum(speed_old, speed), k)
                if flux_old is not None:
                    store(i - 1, [a - b for a, b in zip(flux, flux_old, strict=True)])
                flux_old = flux
            upper_old, speed_old = upper, speed
        for call in beside[:share]:
            call()
        beside = beside[share:]
        ups, cell, steps = now, (cell[1], ahead), steps[1:]
    for call in beside:
        call()


def sides(one, two, low, high, rank):
    even = rank % 2 == 0
    for row in range(0, low.shape[0], 8):
        a, b = one[row : row + 8, :], two[row : row + 8, :]
        low[row : row + 8, :] = jnp.where(even, b, a)
        high[row : row + 8, :] = jnp.where(even, a, b)


def inner_kernel(
    state, far_pairs, far_count, far_coarse, out, fine_uses, coarse_uses,
    turned_even, turned_odd, changes_even, changes_odd, padded, inverse_of, sound, by_y,
    fine_pairs, fine_count, coarse_pairs, arrived,
):
    place = here()
    turned, changes = (turned_even, turned_odd), (changes_even, changes_odd)

    def turn(block, f):
        into, base = turned[block % 2], f * TALL
        flat = state[f * ROWS + block * 128 : f * ROWS + block * 128 + 128, :].T
        into[base + 8 : base + 136, :] = flat
        into[base : base + 8, :] = jnp.broadcast_to(flat[0:1], (8, 128))
        into[base + 136 : base + 144, :] = jnp.broadcast_to(flat[127:128], (8, 128))

    def turn_back(block, f):
        flat = changes[block % 2][f * 128 : f * 128 + 128, :]
        out[f * ROWS + block * 128 : f * ROWS + block * 128 + 128, :] = flat.T

    def along_z(block, beside):
        source, into = turned[block % 2], changes[block % 2]

        def load(f, i):
            return source[pl.ds(f * TALL + 8 + i, 8, stride=16), :]

        def speed_at(i, q):
            inverse = reciprocal(q[0])
            return jnp.abs(q[3]) * inverse + sound_of(q, inverse)

        def store(i, values):
            for f in range(5):
                into[pl.ds(f * 128 + i, 8, stride=16), :] = values[f]

        sweep(load, speed_at, store, 0, 16, 2, beside)

    reads = [
        pltpu.make_async_copy(source, into, arrived.at[n])
        for n, (source, into) in enumerate(
            ((far_pairs, fine_pairs), (far_count, fine_count), (far_coarse, coarse_pairs))
        )
    ]
    for copy in reads:
        copy.start()
    for f in range(5):
        turn(0, f)
    for block in range(4):
        beside = []
        for f in range(5):
            if block < 3:
                beside.append(functools.partial(turn, block + 1, f))
            if block > 0:
                beside.append(functools.partial(turn_back, block - 1, f))
        along_z(block, beside)
    for f in range(5):
        turn_back(3, f)
    for copy in reads:
        copy.wait()
    codes = jnp.concatenate([fine_pairs[...].astype(F32)] * 4, axis=1).T[0:32]
    spread = (iota((16, 128), 1) % 16 == iota((16, 128), 0)).astype(F32)
    used = fold_rows(
        jnp.dot(fine_count[...].astype(F32), spread, precision=HIGH, preferred_element_type=F32), 16
    )
    codes = jnp.where(iota((32, 128), 0).astype(F32) < used, codes, 1000.0)
    along = jnp.floor((codes + 0.5) * 0.04)
    plane = codes - 25.0 * along
    group = jnp.floor((plane + 0.5) * 0.2)
    one = jnp.left_shift(1, (6.0 * (plane - 5.0 * group)).astype(jnp.int32))
    ones = [jnp.where(group == g, one, 0) for g in range(5)]
    fine_uses[24:32, :] = jnp.zeros((8, 128), jnp.int32)
    for g in range(5):
        lines = []
        for ox in range(5):
            hits = jnp.where(along == ox, ones[g], 0)
            hits = (hits[0:8] + hits[8:16]) + (hits[16:24] + hits[24:32])
            lines.append(jnp.sum(hits, axis=0, keepdims=True))
        fine_uses[g * 5 : g * 5 + 5, :] = jnp.concatenate(lines, axis=0)

    slot = iota((8, 128), 1)
    device = slot % place[2] * place[3] + slot // place[2]
    for half in range(2):
        named = coarse_pairs[half * 8 : half * 8 + 8, :]
        coded = named // 16 + named % 4 * (6 * 256) + named // 4 % 4 * 65536
        counts = [jnp.zeros((8, 128), jnp.int32) for _ in range(4)]
        for j in range(32):
            code = jnp.broadcast_to(coded[:, j : j + 1], (8, 128))
            one = jnp.where((code & 255) == device, jnp.left_shift(1, (code >> 8) & 255), 0)
            group = code >> 16
            counts = [each + jnp.where(group == g, one, 0) for g, each in enumerate(counts)]
        for g in range(4):
            coarse_uses[(g * 2 + half) * 8 : (g * 2 + half) * 8 + 8, :] = counts[g]
    for x in range(NX):
        for y in range(0, NY, 8):
            row = x * NY + y
            q = [state[f * ROWS + row : f * ROWS + row + 8, :] for f in range(5)]
            inverse = reciprocal(q[0])
            at = x * PITCH + y
            for f in range(5):
                padded[f * NX * PITCH + at : f * NX * PITCH + at + 8, :] = q[f]
            inverse_of[at : at + 8, :] = inverse
            sound[at : at + 8, :] = sound_of(q, inverse)

    def along_x(step, _):
        start = pl.multiple_of(step * 8, 8)

        def rows(f, i):
            return pl.ds(pl.multiple_of(f * ROWS + i * NY + start, 8), 8)

        def speed_at(i, q):
            at = pl.ds(i * PITCH + start, 8)
            return jnp.abs(q[1]) * inverse_of[at, :] + sound[at, :]

        def store(i, values):
            for f in range(5):
                out[rows(f, i), :] = out[rows(f, i), :] + values[f]

        sweep(lambda f, i: state[rows(f, i), :], speed_at, store, 3, NX - 3, 0)
        return 0

    lax.fori_loop(0, NY // 8, along_x, 0)

    def along_y(step, _):
        start = pl.multiple_of(step * 8, 8)

        def rows(f, i):
            return pl.ds((f * NX + start) * PITCH + i, 8, stride=PITCH)

        def speed_at(i, q):
            return jnp.abs(q[2]) * inverse_of[rows(0, i), :] + sound[rows(0, i), :]

        def store(i, values):
            for f in range(5):
                by_y[rows(f, i), :] = values[f]

        for i in (0, 1, 2, NY - 3, NY - 2, NY - 1):
            store(i, [jnp.zeros((8, 128), F32)] * 5)
        sweep(lambda f, i: padded[rows(f, i), :], speed_at, store, 3, NY - 3, 1)
        return 0

    lax.fori_loop(0, NX // 8, along_y, 0)

    def total(x, _):
        for f in range(5):
            for y in range(0, NY, 8):
                row = pl.ds(pl.multiple_of(f * ROWS + x * NY + y, 8), 8)
                out[row, :] = out[row, :] + by_y[pl.ds((f * NX + x) * PITCH + y, 8), :]
        return 0

    lax.fori_loop(0, NX, total, 0, unroll=2)


def tensors(r, square):
    root = lax.rsqrt(jnp.maximum(square, 1.0))
    cube = root * root * root
    three = 3.0 * cube * (root * root)
    scaled = [three * each for each in r]
    pull = [each * cube for each in r]
    tide = [scaled[i] * r[j] - cube if i == j else scaled[i] * r[j] for i, j in SYM]
    return pull, tide


def add_terms(totals, uses, r, square, mass, dipole):
    pull, tide = tensors(r, square)
    mass = uses * mass
    dipole = [uses * d for d in dipole]
    for i in range(3):
        term = mass * pull[i]
        for j in range(3):
            term = term - tide[sym(i, j)] * dipole[j]
        totals[i] = totals[i] + term
    for e in range(6):
        totals[3 + e] = totals[3 + e] + mass * tide[e]


def far_fields(place, uses_fine, uses_coarse, got, own, beside, around):
    morton, octant = place[0], place[1]
    mortons, octs = place[2], place[3]
    lane = iota((8, 128), 1)
    lane_row = iota((1, 128), 1)

    rows = jnp.concatenate([got[pl.ds(g * 8 * SENT, 8, stride=SENT), :] for g in range(16)], axis=0)
    time_step = COURANT / jnp.max(rows[:, 64:128])
    moments = rows.T
    target_z = iota((8, 128), 0)
    rx = 16.0 * (lane % mortons - morton).astype(F32)
    coarse = []
    for half in range(2):
        totals = [jnp.zeros((8, 128), F32) for _ in range(9)]
        for lp in range(16):
            ry = 16.0 * (lane // mortons * 2 + lp // 8 - (2 * octant + half)).astype(F32)
            rz = 16.0 * (lp % 8 - target_z).astype(F32)
            families = [jnp.broadcast_to(moments[m * 16 + lp : m * 16 + lp + 1], (8, 128)) for m in range(4)]
            row = (lp // 4 * 2 + half) * 8
            uses = ((uses_coarse[row : row + 8, :] >> (lp % 4 * 6)) & 63).astype(F32)
            add_terms(totals, uses, (rx, ry, rz), rx * rx + ry * ry + rz * rz, families[0], families[1:])
        coarse.append([jnp.sum(each, axis=1, keepdims=True) for each in totals])
    result = []
    for e in range(9):
        column = jnp.where(lane // 32 % 2 == 0, coarse[0][e], coarse[1][e])
        column = jnp.where(lane % 16 // 2 == iota((8, 128), 0), column, 0.0)
        result.append(jnp.sum(column, axis=0, keepdims=True))
    side = [4.0 * (2 * s - 1).astype(F32) for s in (lane_row // 64, lane_row // 16 % 2, lane_row % 2)]
    for i in range(3):
        for j in range(3):
            result[i] = result[i] + result[3 + sym(i, j)] * side[j]

    def inside(dx, dy):
        at_x, at_y = morton + dx, octant + dy
        return (at_x >= 0) & (at_x < mortons) & (at_y >= 0) & (at_y < octs)

    blocks = []
    for dy in (-1, 0, 1):
        block = []
        if dy:
            halves = []
            for dx in (-1, 0, 1):
                device = jnp.clip(octant + dy, 0, octs - 1) * mortons + jnp.clip(morton + dx, 0, mortons - 1)
                for n in (1, 2):
                    halves.append(jnp.where(inside(dx, dy), got[pl.ds(device * SENT + n, 1), :], 0.0))
            halves = jnp.concatenate(halves + [jnp.zeros((2, 128), F32)], axis=0)
            back = 32 if dy < 0 else 0
            unpacked = [
                jnp.where(lane < 64, pltpu.roll(each, back, 1), pltpu.roll(each, 32 + back, 1)) if back
                else jnp.where(lane < 64, each, pltpu.roll(each, 32, 1))
                for each in (halves, pltpu.roll(halves, 64, 1))
            ]
            for n in range(6):
                block += [unpacked[0][n : n + 1], unpacked[1][n : n + 1]]
        else:
            for dx, source in ((-1, beside[0:4, :]), (0, own[0:4, :]), (1, beside[8:12, :])):
                block.append(jnp.where(inside(dx, 0), source, 0.0))
        blocks.append(jnp.concatenate(block + [jnp.zeros((4, 128), F32)], axis=0))
    wide = iota((16, 128), 1)
    around[...] = jnp.zeros(around.shape, F32)
    for oy in range(-2, 3):
        if oy == 0:
            moved = blocks[1]
        else:
            moved = pltpu.roll(blocks[1], (-16 * oy) % 128, 1)
            if oy > 0:
                moved = jnp.where(wide // 16 % 4 + oy > 3, pltpu.roll(blocks[2], (64 - 16 * oy) % 128, 1), moved)
            else:
                moved = jnp.where(wide // 16 % 4 + oy < 0, pltpu.roll(blocks[0], (-64 - 16 * oy) % 128, 1), moved)
        swapped = pltpu.roll(moved, 64, 1)
        for m in range(4):
            low, own, high = [(moved[d * 4 + m : d * 4 + m + 1], swapped[d * 4 + m : d * 4 + m + 1]) for d in range(3)]
            first = lane_row < 64
            lines = [
                low[0], jnp.where(first, low[1], own[1]), own[0], jnp.where(first, own[1], high[1]), high[0],
            ]
            row = (m * 5 + oy + 2) * 8
            around[row : row + 5, :] = jnp.concatenate(lines, axis=0)
    totals = [jnp.zeros((8, 128), F32) for _ in range(9)]
    rx = 8.0 * (iota((8, 128), 0) - 2).astype(F32)
    square_x = rx * rx
    for oy in range(-2, 3):
        base = [around[(m * 5 + oy + 2) * 8 : (m * 5 + oy + 2) * 8 + 8, :] for m in range(4)]
        for oz in range(-2, 3):
            moved = base
            if oz:
                ok = (lane % 16 + oz >= 0) & (lane % 16 + oz < 16)
                moved = [jnp.where(ok, pltpu.roll(each, (-oz) % 128, 1), 0.0) for each in base]
            uses = ((uses_fine[(oy + 2) * 5 : (oy + 2) * 5 + 8, :] >> ((oz + 2) * 6)) & 63).astype(F32)
            add_terms(
                totals, uses, (rx, 8.0 * oy, 8.0 * oz),
                square_x + (64.0 * oy * oy + 64.0 * oz * oz), moved[0], moved[1:],
            )
    for e in range(9):
        result[e] = GRAVITY * (result[e] + jnp.sum(totals[e], axis=0, keepdims=True))
    return result, time_step


def edge_kernel(
    state, inner, x_one, x_two, y_one, y_two, out, beside,
    x_low, x_high, y_low, y_high, rims, by_x, by_y,
):
    place = here()
    sides(x_two, x_one, x_low, x_high, place[0])
    even = place[0] % 2 == 0
    moments = x_one[480:488, :], x_two[480:488, :]
    beside[0:8, :] = jnp.where(even, moments[0], moments[1])
    beside[8:16, :] = jnp.where(even, moments[1], moments[0])

    def x_edge(beyond, x):
        for f in range(5):
            cells = state[f * ROWS + x * NY : f * ROWS + x * NY + NY, :]
            for layer in range(3):
                beyond[(f * 3 + layer) * NY : (f * 3 + layer) * NY + NY, :] = cells

    pl.when(place[0] == 0)(lambda: x_edge(x_low, 0))
    pl.when(place[0] == place[2] - 1)(lambda: x_edge(x_high, NX - 1))

    def speed_of(k):
        def speed_at(i, q):
            inverse = reciprocal(q[0])
            return jnp.abs(q[1 + k]) * inverse + sound_of(q, inverse)

        return speed_at

    def along_x(step, _):
        start = pl.multiple_of(step * 8, 8)

        def load(f, i):
            if i < 0:
                return x_low[pl.ds(pl.multiple_of((f * 3 + i + 3) * NY + start, 8), 8), :]
            if i >= NX:
                return x_high[pl.ds(pl.multiple_of((f * 3 + i - NX) * NY + start, 8), 8), :]
            return state[pl.ds(pl.multiple_of(f * ROWS + i * NY + start, 8), 8), :]

        def store(i, values):
            for f in range(5):
                by_x[pl.ds(pl.multiple_of((f * 6 + (i if i < 3 else i - 10)) * NY + start, 8), 8), :] = values[f]

        sweep(load, speed_of(0), store, 0, 3, 0)
        sweep(load, speed_of(0), store, NX - 3, NX, 0)
        return 0

    lax.fori_loop(0, NY // 8, along_x, 0)

    for f in range(5):
        for x in range(NX):
            for side, y in ((0, 0), (8, NY - 8)):
                row = (f * NX + x) * RIM + side
                rims[row : row + 8, :] = state[f * ROWS + x * NY + y : f * ROWS + x * NY + y + 8, :]
                by_y[row : row + 8, :] = jnp.zeros((8, 128), F32)
    sides(y_one, y_two, y_low, y_high, place[1])

    def y_edge(beyond, row):
        for f in range(5):
            cells = rims[pl.ds(f * NX * RIM + row, NX, stride=RIM), :]
            for layer in range(3):
                beyond[pl.ds(f * NX * 3 + layer, NX, stride=3), :] = cells

    pl.when(place[1] == 0)(lambda: y_edge(y_low, 0))
    pl.when(place[1] == place[3] - 1)(lambda: y_edge(y_high, 15))

    def along_y(step, _):
        start = pl.multiple_of(step * 8, 8)

        def rows(f, i):
            return pl.ds((f * NX + start) * RIM + (i if i < 8 else i - 16), 8, stride=RIM)

        def load(f, i):
            if i < 0:
                return y_low[pl.ds((f * NX + start) * 3 + i + 3, 8, stride=3), :]
            if i >= NY:
                return y_high[pl.ds((f * NX + start) * 3 + i - NY, 8, stride=3), :]
            return rims[rows(f, i), :]

        def store(i, values):
            for f in range(5):
                by_y[rows(f, i), :] = values[f]

        sweep(load, speed_of(1), store, 0, 3, 1)
        sweep(load, speed_of(1), store, NY - 3, NY, 1)
        return 0

    lax.fori_loop(0, NX // 8, along_y, 0)

    for f in range(5):
        for x in range(NX):
            for y in range(0, NY, 8):
                row = f * ROWS + x * NY + y
                total = inner[row : row + 8, :]
                if x < 3 or x >= NX - 3:
                    at = (f * 6 + (x if x < 3 else x - 10)) * NY + y
                    total = total + by_x[at : at + 8, :]
                if y in (0, NY - 8):
                    at = (f * NX + x) * RIM + (0 if y == 0 else 8)
                    total = total + by_y[at : at + 8, :]
                out[row : row + 8, :] = total


def update_kernel(
    state, twice, uses_fine, uses_coarse, got, own, beside, new, gravity, around, field, made, pulls, written
):
    place = here()
    result, time_step = far_fields(place, uses_fine, uses_coarse, got, own, beside, around)
    half_step = 0.5 * time_step
    source = iota((8, 128), 0) * 16 + iota((8, 128), 1) // 8
    lines = [
        jnp.take_along_axis(jnp.broadcast_to(each, (8, 128)), source, axis=1, mode="promise_in_bounds") for each in result
    ]
    offset_z = (iota((8, 128), 1) % 8).astype(F32) - 3.5
    for i in range(3):
        field[i * 8 : i * 8 + 8, :] = lines[i] + lines[3 + sym(i, 2)] * offset_z
        field[(3 + i) * 8 : (3 + i) * 8 + 8, :] = lines[3 + sym(i, 0)]
        field[(6 + i) * 8 : (6 + i) * 8 + 8, :] = lines[3 + sym(i, 1)]
    offset_y = iota((8, 128), 0).astype(F32) - 3.5

    def writes(part):
        rows = pl.ds(part * 2, 2)
        return [
            pltpu.make_async_copy(made.at[:, rows, :, :], new.at[:, rows, :, :], written.at[0, part]),
            pltpu.make_async_copy(pulls.at[:, rows, :, :], gravity.at[:, rows, :, :], written.at[1, part]),
        ]

    lines = {}
    for x in range(NX):
        for ty in range(4):
            tx, y = x // 8, ty * 8
            if x % 8 == 0:
                at = [field[e * 8 + tx * 4 + ty : e * 8 + tx * 4 + ty + 1, :] for e in range(9)]
                lines[ty] = ([at[e] + at[6 + e] * offset_y for e in range(3)], at[3:6])
            base, slope = lines[ty]
            q = [state[f * ROWS + x * NY + y : f * ROWS + x * NY + y + 8, :] for f in range(5)]
            pull = [base[e] + slope[e] * (x % 8 - 3.5) for e in range(3)]
            moved = []
            for f in range(5):
                total = twice[f * ROWS + x * NY + y : f * ROWS + x * NY + y + 8, :]
                moved.append(q[f] - half_step * total)
            weight = time_step * q[0]
            gain = q[1] * pull[0] + q[2] * pull[1] + q[3] * pull[2]
            made[0, x, y : y + 8, :] = moved[0]
            for e in range(3):
                pulls[e, x, y : y + 8, :] = pull[e]
                made[1 + e, x, y : y + 8, :] = moved[1 + e] + weight * pull[e]
            made[4, x, y : y + 8, :] = moved[4] + time_step * gain
        if x % 2 == 1:
            for copy in writes(x // 2):
                copy.start()
    for part in range(8):
        for copy in writes(part):
            copy.wait()


VMEM = pl.BlockSpec(memory_space=pltpu.VMEM)
FAR = pl.BlockSpec(memory_space=pltpu.HBM)
LIMIT = pltpu.CompilerParams(vmem_limit_bytes=12 * 1024 * 1024)
SMALL = pl.CostEstimate(flops=1000, bytes_accessed=1000, transcendentals=0)


def far(values):
    return pltpu.with_memory_space_constraint(values, pltpu.HBM)


def call(kernel, outs, scratch, *args, sources=None, far_outs=(), whole_numbers=()):
    shapes = [(o, 128) if isinstance(o, int) else o for o in outs]
    return pl.pallas_call(
        kernel,
        out_shape=[
            pltpu.HBM(s, F32) if n in far_outs else jax.ShapeDtypeStruct(s, jnp.int32 if n in whole_numbers else F32)
            for n, s in enumerate(shapes)
        ],
        in_specs=sources or [VMEM] * len(args),
        out_specs=[FAR if n in far_outs else VMEM for n in range(len(outs))],
        scratch_shapes=[pltpu.VMEM((s, 128), F32) if isinstance(s, int) else s for s in scratch],
        compiler_params=LIMIT,
        cost_estimate=SMALL,
    )(*args)


def local(state, fine_pairs, fine_count, coarse_pairs):
    mortons, octs = lax.axis_size("morton"), lax.axis_size("oct")
    many = NX * PITCH

    def swap(values, pair):
        pairs = [(m, o) for m in range(mortons) for o in range(octs)]
        index = lambda at: at[0] * octs + at[1]
        return lax.ppermute(values, AXES, [(index(p), index(pair(*p))) for p in pairs])

    def other(i):
        return (i - 1 ^ 1) + 1

    block = pltpu.VMEM((5, ROWS, 128), F32)
    sent, x_one, x_two, y_one, y_two, own = call(
        moments_kernel, [128 * SENT, LONG, LONG, 240, 240, 8],
        [block, pltpu.SemaphoreType.DMA((8,))], far(state.reshape(5, ROWS, 128)), sources=[FAR],
    )
    got = lax.all_to_all(sent.reshape(mortons * octs, 1, SENT * 128), AXES[::-1], 0, 0, tiled=True)
    x_one = swap(x_one, lambda m, o: (other(m), o) if 0 < m < mortons - 1 else (m, o ^ 1))
    x_two = swap(x_two, lambda m, o: (m ^ 1, o))
    y_one = swap(y_one, lambda m, o: (m, o ^ 1))
    y_two = swap(y_two, lambda m, o: (m, other(o)) if 0 < o < octs - 1 else (m, octs - 1 - o))
    rows = state.reshape(5 * ROWS, 128)
    rows, sent = lax.optimization_barrier((rows, sent))
    inner, uses_fine, uses_coarse = call(
        inner_kernel, [5 * ROWS, 32, 64],
        [5 * TALL, 5 * TALL, 640, 640, 5 * many, many, many, 5 * many, pltpu.VMEM((128, 32), jnp.int32),
         pltpu.VMEM((8, 16), jnp.int32), pltpu.VMEM((16, 32), jnp.int32), pltpu.SemaphoreType.DMA((3,))],
        rows, far(fine_pairs.reshape(128, 32)), far(fine_count.reshape(8, 16)), far(coarse_pairs.reshape(16, 32)),
        sources=[VMEM, FAR, FAR, FAR], whole_numbers=(1, 2),
    )
    rim = 5 * NX * RIM
    twice, beside = call(
        edge_kernel, [5 * ROWS, 16], [480, 480, 240, 240, rim, 960, rim],
        rows, inner, x_one, x_two, y_one, y_two,
    )
    return call(
        update_kernel, [(5, NX, NY, NZ), (3, NX, NY, NZ)],
        [160, 72, pltpu.VMEM((5, NX, NY, NZ), F32), pltpu.VMEM((3, NX, NY, NZ), F32), pltpu.SemaphoreType.DMA((2, 8))],
        rows, twice, uses_fine, uses_coarse, got.reshape(mortons * octs * SENT, 128), own, beside,
        far_outs=range(2),
    )


def solution(mesh):
    in_specs = (
        P(None, "morton", "oct", None),
        P("morton", "oct", None, None),
        P("morton", "oct", None),
        P("morton", "oct", None, None),
    )
    out_specs = (P(None, "morton", "oct", None), P(None, "morton", "oct", None))
    return jax.shard_map(local, mesh=mesh, in_specs=in_specs, out_specs=out_specs, check_vma=False)
```
